128 devices in a mesh: fsdp: 128 (over z, x, y, core).
Axes of the slice: x: 4, y: 4, z: 4, core: 2. Of those that a mesh axis runs over, the one named last changes fastest.
Arguments:
- tokens: bfloat16 [65536, 768], P('fsdp'), may hold values from -6 to 6
- in_weight: bfloat16 [2574336], P('fsdp'), may hold values from -0.21875 to 0.21875
- out_weight: bfloat16 [1179648], P('fsdp'), may hold values from -0.15625 to 0.15625
- norm_gain: float32 [768], replicated, may hold values from 0.1 to 1.9
- conv_weight: float32 [4, 1792], replicated, may hold values from -3 to 3
- conv_bias: float32 [1792], replicated, may hold values from -3 to 3
- dt_bias: float32 [24], replicated, may hold values from -4.5 to -1
- a_log: float32 [24], replicated, may hold values from 0 to 2.8
- d_skip: float32 [24], replicated, may hold values from 0.5 to 2
- gated_gain: float32 [1536], replicated, may hold values from 0.1 to 1.9
- cotangent: bfloat16 [65536, 768], P('fsdp'), may hold values from -6 to 6
Outputs:
- output: bfloat16 [65536, 768], P('fsdp')
- grad_tokens: float32 [65536, 768], P('fsdp')
- grad_in_weight: float32 [2574336], P('fsdp')
- grad_out_weight: float32 [1179648], P('fsdp')
- grad_norm_gain: float32 [768], replicated
- grad_conv_weight: float32 [4, 1792], replicated
- grad_conv_bias: float32 [1792], replicated
- grad_dt_bias: float32 [24], replicated
- grad_a_log: float32 [24], replicated
- grad_d_skip: float32 [24], replicated
- grad_gated_gain: float32 [1536], replicated
The draws below stay inside these ranges and needn't reach their ends.
All inputs are finite; a program needn't handle non-finite values.
Results may differ from the reference program's by a relative error of at most 0.0092.
Values may be sent and summed in bfloat16 or wider, within the bound.
No kernel may reach another device: no remote copies, remote signals or barrier semaphores. Data moves between devices by JAX's collectives and lax.ppermute only.
A program may use at most 128 MiB of HBM per device.

```python
import math
import jax
import jax.numpy as jnp
from jax import lax

D = 768
NH = 24
DS = 128
HEAD = 64
CONV = 4
LEN = 256
DI = 1536
CONV_CH = 1792
NCOL = 3352
TOKENS = 65536


def block_scale(key, shape, shards, smallest, largest):
    factor_of = 1.0
    for dim, blocks in shards:
        draws = jax.random.uniform(jax.random.fold_in(jax.random.fold_in(key, 6), dim), (blocks,), jnp.float32, smallest / len(shards), largest / len(shards))
        factor_of = factor_of * jnp.repeat(jnp.exp(draws), shape[dim] // blocks).reshape((-1,) + (1,) * (len(shape) - 1 - dim))
    return factor_of


def normal_values(stream_key, extent, width, most, shards=(), dtype=jnp.bfloat16):
    level = block_scale(stream_key, extent, shards, -0.22, 0.18) if shards else 1.0
    values = jax.random.normal(stream_key, extent, jnp.float32) * width * level
    return jnp.minimum(jnp.maximum(values, -most), most).astype(dtype)


def setup_inputs(seed: int = 0) -> dict:
    key_of = jax.random.split(jax.random.key(seed), 12)
    return {
        "tokens": normal_values(key_of[0], (TOKENS, D), 1.0, 6.0, ((0, 128),)),
        "in_weight": normal_values(key_of[1], (D * NCOL,), D ** -0.5, 0.21875, ((0, 128),)),
        "out_weight": normal_values(key_of[2], (DI * D,), DI ** -0.5, 0.15625, ((0, 128),)),
        "norm_gain": jnp.clip(1.0 + 0.18 * jax.random.normal(key_of[3], (D,), jnp.float32), 0.1, 1.9),
        "conv_weight": normal_values(key_of[4], (CONV, CONV_CH), CONV ** -0.5, 3.0, (), jnp.float32),
        "conv_bias": normal_values(key_of[5], (CONV_CH,), 0.5, 3.0, (), jnp.float32),
        "dt_bias": jnp.clip(jax.random.uniform(key_of[6], (NH,), jnp.float32, -4.5, -1.0), -4.5, -1.0),
        "a_log": jnp.clip(jax.random.uniform(key_of[7], (NH,), jnp.float32, 0.0, 2.8), 0.0, 2.8),
        "d_skip": jnp.clip(jax.random.uniform(key_of[8], (NH,), jnp.float32, 0.5, 2.0), 0.5, 2.0),
        "gated_gain": jnp.clip(1.0 + 0.18 * jax.random.normal(key_of[9], (DI,), jnp.float32), 0.1, 1.9),
        "cotangent": normal_values(key_of[10], (TOKENS, D), 1.0, 6.0, ((0, 128),)),
    }


@jax.custom_vjp
def low(v):
    return lax.optimization_barrier(v.astype(jnp.bfloat16)).astype(jnp.float32)

@jax.custom_vjp
def lowered_backward(v):
    return v

def low_keep(v):
    return (low(v), None)

def low_pass(kept, grad):
    return (grad,)

def back_keep(v):
    return (v, None)

def back_low(kept, grad):
    return (low(grad),)
low.defvjp(low_keep, low_pass)
lowered_backward.defvjp(back_keep, back_low)
epsilon = 1e-05
highest_precision = lax.Precision.HIGHEST

def mixer_layer(input_rows, input_weight, output_weight, norm_gain, conv_weight, conv_bias, dt_bias, a_log, d_skip, gated_gain):
    seq_count = input_rows.shape[0]
    inv_rms = lax.rsqrt(lax.optimization_barrier(jnp.mean(input_rows * input_rows, axis=-1, keepdims=True)) + epsilon)
    hidden_state = low(input_rows * inv_rms * norm_gain)
    projected_rows = lowered_backward(jnp.einsum('wuq,qj->wuj', hidden_state, input_weight, precision=highest_precision))
    gate_in = projected_rows[..., :DI]
    conv_input = projected_rows[..., DI:DI + CONV_CH]
    dt_raw = projected_rows[..., DI + CONV_CH:]
    padded = jnp.pad(conv_input, ((0, 0), (CONV - 1, 0), (0, 0)))
    conv_sum = conv_bias + conv_weight[0] * padded[:, 0:LEN]
    for offset in range(1, CONV):
        conv_sum = conv_sum + conv_weight[offset] * padded[:, offset:offset + LEN]
    activated = jax.nn.silu(conv_sum)
    heads_x = low(activated[..., :DI]).reshape(seq_count, LEN, NH, HEAD)
    b_state = low(activated[..., DI:DI + DS])
    c_state = low(activated[..., DI + DS:])
    dt_step = jax.nn.softplus(dt_raw + dt_bias)
    decay_rate = -jnp.exp(a_log)
    cumulative = jnp.cumsum(dt_step * decay_rate, axis=1)
    scores = lowered_backward(jnp.einsum('std,sud->stu', c_state, b_state, precision=highest_precision))
    cum_heads = jnp.swapaxes(cumulative, 1, 2)
    step_heads = jnp.swapaxes(dt_step, 1, 2)
    causal = jnp.arange(LEN)[:, None] >= jnp.arange(LEN)[None, :]
    log_gap = cum_heads[:, :, :, None] - cum_heads[:, :, None, :]
    decay_factor = jnp.where(causal, jnp.exp(jnp.where(causal, log_gap, 0.0)), 0.0)
    mix_weight = low(scores[:, None] * decay_factor * step_heads[:, :, None, :])
    ssd_out = lowered_backward(jnp.einsum('shtu,suhp->sthp', mix_weight, heads_x, precision=highest_precision))
    y_heads = ssd_out + d_skip[:, None] * heads_x
    gated_value = y_heads.reshape(seq_count, LEN, DI) * jax.nn.silu(gate_in)
    gated_inv = lax.rsqrt(lax.optimization_barrier(jnp.mean(gated_value * gated_value, axis=-1, keepdims=True)) + epsilon)
    normed_input = low(gated_value * gated_inv * gated_gain)
    return input_rows + jnp.einsum('tgq,qh->tgh', normed_input, output_weight, precision=highest_precision)

def reference(tokens, in_weight, out_weight, norm_gain, conv_weight, conv_bias, dt_bias, a_log, d_skip, gated_gain, cotangent):
    total_seqs = tokens.shape[0] // LEN
    group_size = math.gcd(total_seqs, 16)
    blocks = total_seqs // group_size
    input_rows = tokens.astype(jnp.float32).reshape(blocks, group_size, LEN, D)
    cot_blocks = cotangent.astype(jnp.float32).reshape(blocks, group_size, LEN, D)
    params = (in_weight.astype(jnp.float32).reshape(D, NCOL), out_weight.astype(jnp.float32).reshape(DI, D), norm_gain, conv_weight, conv_bias, dt_bias, a_log, d_skip, gated_gain)

    def one_block(totals, pair):
        block_in, block_cot = pair
        result, pullback = jax.vjp(mixer_layer, block_in, *params)
        grads = pullback(block_cot)
        totals = jax.tree.map(lambda left, right: left + right, totals, tuple(grads[1:]))
        return (totals, (result.astype(jnp.bfloat16), grads[0]))
    start = jax.tree.map(lambda v: jnp.zeros(v.shape, jnp.float32), params)
    totals, (results, grad_in) = lax.scan(one_block, start, (input_rows, cot_blocks))
    return (results.reshape(tokens.shape[0], D), grad_in.reshape(tokens.shape[0], D), totals[0].reshape(-1), totals[1].reshape(-1), totals[2], totals[3], totals[4], totals[5], totals[6], totals[7], totals[8])
```

```python
import jax
import jax.numpy as jnp
from jax import lax
from jax.experimental import pallas as pl
from jax.experimental.pallas import tpu as pltpu
from jax.sharding import PartitionSpec as P

D = 768
NH = 24
DS = 128
HEAD = 64
CONV = 4
LEN = 256
DI = 1536
CONV_CH = 1792
NCOL = 3352
ROWS = 512
SEQS = 2
PADLEN = LEN + 8
HALF1 = 1024
WIDE1 = 2048
EPS = 1e-5
LOG2E = 1.4426950408889634
LIMIT = 58 * 1024 * 1024
F32 = jnp.float32
BF16 = jnp.bfloat16
HIGHEST = lax.Precision.HIGHEST


def index_of(z, x, y, c):
    return ((z % 4 * 4 + x % 4) * 4 + y % 4) * 2 + c


def everyone():
    for z in range(4):
        for x in range(4):
            for y in range(4):
                for c in range(2):
                    yield z, x, y, c


def ring_pairs(shift, last):
    pairs = []
    for z, x, y, c in everyone():
        along_z = (c == 0) == last
        to = (z + shift, x, y, c) if along_z else (z, x + shift, y, c)
        pairs.append((index_of(z, x, y, c), index_of(*to)))
    return pairs


CORE_PAIRS = [(index_of(*p), index_of(*p[:3], 1 - p[3])) for p in everyone()]
EIGHTS = [[(z * 4 + x) * 8 + k for k in range(8)] for z in range(4) for x in range(4)]


def ring_gather(value, last):
    return [value] + [
        lax.ppermute(value, "fsdp", ring_pairs(shift, last)) for shift in (1, 2, 3)
    ]


def ring_reduce(parts, last):
    got = [parts[0].astype(F32)] + [
        lax.ppermute(parts[r].astype(BF16), "fsdp", ring_pairs(r, last)).astype(F32)
        for r in (1, 2, 3)
    ]
    return (got[0] + got[2]) + (got[1] + got[3])


def swap_core(value):
    return lax.ppermute(value, "fsdp", CORE_PAIRS)


def dot_nn(a, b):
    return jnp.dot(a, b, preferred_element_type=F32)


def dot_nt(a, b):
    return lax.dot_general(a, b, (((1,), (1,)), ((), ())), preferred_element_type=F32)


def dot_tn(a, b):
    return lax.dot_general(a, b, (((0,), (0,)), ((), ())), preferred_element_type=F32)


def dot_exact(a, b):
    return jnp.dot(a, b, preferred_element_type=F32, precision=HIGHEST)


def sigmoid(v):
    return 0.5 * jnp.tanh(0.5 * v) + 0.5


def softplus(v):
    e = jnp.exp(-jnp.abs(v))
    small = e * (1.0 - e * (0.5 - e * (1.0 / 3.0)))
    return jnp.maximum(v, 0.0) + jnp.where(e < 1e-3, small, jnp.log(1.0 + e))


def iota(shape, dim):
    return lax.broadcasted_iota(jnp.int32, shape, dim)


def source_zx(half, z0, x0, r3, r2):
    zr = jnp.where(half == 0, r3, r2)
    xr = jnp.where(half == 0, r2, r3)
    return lax.rem(z0 - zr + 4, 4) * 4 + lax.rem(x0 - xr + 4, 4)


def slot_of(half, z0, x0, zx):
    dz = lax.rem(zx // 4 - z0 + 4, 4)
    dx = lax.rem(zx % 4 - x0 + 4, 4)
    return jnp.where(half == 0, dz * 4 + dx, dx * 4 + dz)


def head_masks():
    lane = iota((1, 128), 1)
    first = jnp.where(lane < 64, 1.0, 0.0).astype(BF16)
    second = jnp.where(lane < 64, 0.0, 1.0).astype(BF16)
    return first, second


def kernel_a(
    pos, tokens, gain, conv_w, conv_b, dt_bias, rate, d_skip,
    b0, b1, b2, b3, q0, q1, q2, q3,
    hidden, w1, conv_in, slope, xs, bc, dt_pre, acum, bcum, y,
    score, bcum_t, sems,
):
    z0, x0, core = pos[0], pos[1], pos[2]
    copies = []
    for side, refs in enumerate(((b0, b1, b2, b3), (q0, q1, q2, q3))):
        half = core if side == 0 else 1 - core
        col = pl.multiple_of(half * HALF1, HALF1)
        for r3 in range(4):
            for r2 in range(4):
                row = pl.multiple_of(source_zx(half, z0, x0, r3, r2) * 48, 16)
                copies.append(
                    pltpu.make_async_copy(
                        refs[r3].at[pl.ds(r2 * 48, 48)],
                        w1.at[pl.ds(row, 48), pl.ds(col, HALF1)],
                        sems.at[side, r3, r2],
                    )
                )
    for copy in copies:
        copy.start()

    @pl.loop(0, ROWS // 64)
    def _(i):
        rows = pl.ds(pl.multiple_of(i * 64, 64), 64)
        t = tokens[rows].astype(F32)
        inv = lax.rsqrt(jnp.mean(t * t, axis=1, keepdims=True) + EPS)
        hidden[rows] = (t * inv * gain[...]).astype(BF16)

    for s in range(SEQS):
        conv_in[s, 0:8] = jnp.zeros((8, CONV_CH), F32)
    for copy in copies:
        copy.wait()

    def conv_tile(cols, emit):
        p = dot_nn(hidden[...], w1[:, cols])
        for s in range(SEQS):
            conv_in[s, 8:PADLEN, cols] = p[s * LEN : (s + 1) * LEN]
        w = conv_w[:, cols]
        bias = conv_b[:, cols]
        for s in range(SEQS):

            @pl.loop(0, LEN // 32)
            def _(i):
                base = pl.multiple_of(i * 32, 32)
                near = conv_in[s, pl.ds(base, 40), cols]
                total = bias + w[0:1] * near[5:37]
                for k in range(1, CONV):
                    total = total + w[k : k + 1] * near[5 + k : 37 + k]
                sig = sigmoid(total)
                act = total * sig
                rows = pl.ds(pl.multiple_of(s * LEN + base, 32), 32)
                slope[rows, cols] = sig * (1.0 + total * (1.0 - sig))
                emit(rows, act.astype(BF16))

    @pl.loop(0, 6)
    def _(j):
        cols = pl.ds(pl.multiple_of(j * 256, 256), 256)

        def emit(rows, act):
            xs[rows, cols] = act

        conv_tile(cols, emit)

    def emit_bc(rows, act):
        bc[rows] = act

    conv_tile(pl.ds(1536, 256), emit_bc)

    pre = dot_nn(hidden[...], w1[:, CONV_CH : CONV_CH + 128]) + dt_bias[...]
    dt_pre[...] = pre
    step = softplus(pre)
    inc = step * rate[...] * LOG2E
    log_step = jnp.log(jnp.maximum(step, 1e-37)) * LOG2E
    below = iota((LEN, LEN), 0) >= iota((LEN, LEN), 1)
    lower = jnp.where(below, 1.0, 0.0)
    mask0, mask1 = head_masks()
    for s in range(SEQS):
        rows = slice(s * LEN, (s + 1) * LEN)
        a = dot_exact(lower, inc[rows])
        b = a - log_step[rows]
        acum[rows] = a
        bcum[rows] = b
        bcum_t[...] = b.T
        score[...] = jnp.where(below, dot_nt(bc[rows, DS:], bc[rows, :DS]), 0.0)

        @pl.loop(0, NH // 2)
        def _(p):
            lanes = pl.ds(pl.multiple_of(p * 128, 128), 128)
            x = xs[s * LEN : (s + 1) * LEN, lanes]
            turned = pltpu.roll(a, lax.rem(128 - 2 * p, 128), 1)
            top = jnp.zeros((128, 128), F32)
            low = jnp.zeros((128, 128), F32)
            for i, mask in enumerate((mask0, mask1)):
                col = turned[:, i : i + 1]
                row = bcum_t[pl.ds(2 * p + i, 1), :]
                xm = x * mask
                e0 = jnp.exp2(jnp.minimum(col[:128] - row[:, :128], 64.0))
                m0 = (e0 * score[:128, :128]).astype(BF16)
                top = top + dot_nn(m0, xm[:128])
                e1 = jnp.exp2(jnp.minimum(col[128:] - row, 64.0))
                m1 = (e1 * score[128:, :]).astype(BF16)
                low = low + dot_nn(m1, xm)
            skip = d_skip[:, lanes]
            y[s * LEN : s * LEN + 128, lanes] = top + skip * x[:128].astype(F32)
            y[s * LEN + 128 : (s + 1) * LEN, lanes] = low + skip * x[128:].astype(F32)


def kernel_b(
    pos, hidden, y, tokens, cot, gain,
    b0, b1, b2, b3, q0, q1, q2, q3,
    out, d_y, grads, d_hid, gain_grad,
    weights, gate_in, d_normed, normed, d_gate, gate_inv, acc, sems,
):
    z0, x0, core = pos[0], pos[1], pos[2]
    copies = []
    for side, refs in enumerate(((b0, b1, b2, b3), (q0, q1, q2, q3))):
        half = core if side == 0 else 1 - core
        for r3 in range(4):
            for r2 in range(4):
                zx = source_zx(half, z0, x0, r3, r2)
                for lr in range(2):
                    row = jnp.where(half == 0, lr * D + zx * 48, DI + zx * 96 + lr * 48)
                    copies.append(
                        pltpu.make_async_copy(
                            refs[r3].at[pl.ds(r2 * 96 + lr * 48, 48)],
                            weights.at[pl.ds(pl.multiple_of(row, 16), 48)],
                            sems.at[side, r3, r2, lr],
                        )
                    )
    for copy in copies:
        copy.start()
    for copy in copies:
        copy.wait()

    @pl.loop(0, 3)
    def _(j):
        cols = pl.ds(pl.multiple_of(j * 256, 256), 256)
        right = pl.ds(pl.multiple_of(j * 256 + D, 256), 256)
        gate_in[:, cols] = dot_nn(hidden[...], weights[0:D, cols])
        gate_in[:, right] = dot_nn(hidden[...], weights[D:DI, cols])

    @pl.loop(0, ROWS // 16)
    def _(i):
        rows = pl.ds(pl.multiple_of(i * 16, 16), 16)
        g = gate_in[rows]
        gated = y[rows] * (g * sigmoid(g))
        inv = lax.rsqrt(jnp.mean(gated * gated, axis=1, keepdims=True) + EPS)
        gate_inv[rows] = jnp.broadcast_to(inv, (16, 128))
        normed[rows] = (gated * inv * gain[...]).astype(BF16)

    @pl.loop(0, 3)
    def _(j):
        cols = pl.ds(pl.multiple_of(j * 256, 256), 256)
        mixed = dot_nn(normed[...], weights[DI:, cols])
        out[:, cols] = (tokens[:, cols].astype(F32) + mixed).astype(BF16)

    @pl.loop(0, 6)
    def _(j):
        cols = pl.ds(pl.multiple_of(j * 256, 256), 256)
        d_normed[:, cols] = dot_nt(cot[...], weights[pl.ds(pl.multiple_of(j * 256 + DI, 256), 256)])

    acc[...] = jnp.zeros_like(acc)

    @pl.loop(0, ROWS // 16)
    def _(i):
        rows = pl.ds(pl.multiple_of(i * 16, 16), 16)
        g = gate_in[rows]
        sig = sigmoid(g)
        act = g * sig
        yv = y[rows]
        inv = gate_inv[rows][:, 0:1]
        gnorm = yv * act * inv
        dn = d_normed[rows]
        prod = dn * gnorm
        acc[...] += prod
        dgn = dn * gain[...]
        mean = jnp.mean(dgn * gnorm, axis=1, keepdims=True)
        d_gated = inv * (dgn - gnorm * mean)
        d_y[rows] = d_gated * act
        d_gate[rows] = (d_gated * yv * (sig * (1.0 + g * (1.0 - sig)))).astype(BF16)

    gain_grad[...] = jnp.sum(acc[...], axis=0, keepdims=True)

    @pl.loop(0, 3)
    def _(j):
        cols = pl.ds(pl.multiple_of(j * 256, 256), 256)
        for lr in range(2):
            src = pl.ds(pl.multiple_of(j * 256 + lr * D, 256), 256)
            g = dot_tn(hidden[...], d_gate[:, src]).astype(BF16)
            for zx in range(16):
                grads[core, slot_of(0, z0, x0, zx), lr * 48 : lr * 48 + 48, cols] = g[
                    zx * 48 : zx * 48 + 48
                ]

    for t in range(4):
        g = dot_tn(normed[:, t * 384 : (t + 1) * 384], cot[...]).astype(BF16)
        for k in range(4):
            grads[1 - core, slot_of(1, z0, x0, t * 4 + k)] = g[k * 96 : (k + 1) * 96]

    @pl.loop(0, 3)
    def _(j):
        cols = pl.ds(pl.multiple_of(j * 256, 256), 256)
        right = pl.ds(pl.multiple_of(j * 256 + D, 256), 256)
        d_hid[:, cols] = dot_nt(d_gate[:, :D], weights[cols]) + dot_nt(
            d_gate[:, D:], weights[right]
        )


def kernel_c(
    pos, xs, bc, acum, bcum, dt_pre, d_y, y, conv_in, slope, conv_w, rate, d_skip, hidden,
    grads, d_proj, g_conv_w, g_conv_b, g_skip, g_dt, g_alog,
    d_conv, score_t, acum_t, d_score, rsum, csum,
):
    z0, x0, core = pos[0], pos[1], pos[2]
    above = iota((LEN, LEN), 0) <= iota((LEN, LEN), 1)
    upper = jnp.where(above, 1.0, 0.0)
    mask0, mask1 = head_masks()
    lane_head = iota((128, 128), 0) // 64
    head_col = iota((128, 128), 1)
    g_skip[...] = jnp.zeros_like(g_skip)
    g_dt[...] = jnp.zeros_like(g_dt)
    g_alog[...] = jnp.zeros_like(g_alog)
    d_proj[:, CONV_CH + 128 :] = jnp.zeros((ROWS, 128), BF16)

    for s in range(SEQS):
        rows = slice(s * LEN, (s + 1) * LEN)
        d_conv[s, LEN:] = jnp.zeros((8, CONV_CH), F32)
        acum_t[...] = acum[rows].T
        score_t[...] = jnp.where(above, dot_nt(bc[rows, :DS], bc[rows, DS:]), 0.0)
        d_score[...] = jnp.zeros_like(d_score)
        rsum[...] = jnp.zeros_like(rsum)
        csum[...] = jnp.zeros_like(csum)
        b = bcum[rows]

        @pl.loop(0, NH // 2)
        def _(p):
            lanes = pl.ds(pl.multiple_of(p * 128, 128), 128)
            x = xs[s * LEN : (s + 1) * LEN, lanes]
            dy = d_y[s * LEN : (s + 1) * LEN, lanes]
            ds = dy.astype(BF16)
            turned = pltpu.roll(b, lax.rem(128 - 2 * p, 128), 1)
            top = jnp.zeros((128, 128), F32)
            low = jnp.zeros((128, 128), F32)
            for i, mask in enumerate((mask0, mask1)):
                col = turned[:, i : i + 1]
                row = acum_t[pl.ds(2 * p + i, 1), :]
                dm = ds * mask
                xm = x * mask
                e0 = jnp.exp2(jnp.minimum(row - col[:128], 64.0))
                m0 = (e0 * score_t[:128, :]).astype(BF16)
                top = top + dot_nn(m0, dm)
                d_score[:128, :] += dot_nt(xm[:128], ds) * e0
                e1 = jnp.exp2(jnp.minimum(row[:, 128:] - col[128:], 64.0))
                m1 = (e1 * score_t[128:, 128:]).astype(BF16)
                low = low + dot_nn(m1, dm[128:])
                d_score[128:, 128:] += dot_nt(xm[128:], ds[128:]) * e1
            dxs = jnp.concatenate([top, low], axis=0)
            skip = d_skip[:, lanes]
            xf = x.astype(F32)
            own = ds.astype(F32) * (y[s * LEN : (s + 1) * LEN, lanes] - skip * xf)
            across = xf * dxs
            pick = jnp.where(lane_head + 2 * p == head_col, 1.0, 0.0)
            rsum[...] += dot_exact(own, pick)
            csum[...] += dot_exact(across, pick)
            g_skip[:, lanes] += jnp.sum(dy * xf, axis=0, keepdims=True)
            d_conv[s, 0:LEN, lanes] = (skip * dy + dxs) * slope[
                s * LEN : (s + 1) * LEN, lanes
            ]

        pre = dt_pre[rows]
        step = softplus(pre)
        sig = 1.0 / (1.0 + jnp.exp(-pre))
        ratio = jnp.where(pre < -20.0, 1.0, sig / jnp.maximum(step, 1e-30))
        d_cum = rsum[...] - csum[...]
        d_inc = dot_exact(upper, d_cum)
        g_alog[...] += jnp.sum(d_inc * step, axis=0, keepdims=True) * rate[...]
        d_pre = csum[...] * ratio + d_inc * rate[...] * sig
        g_dt[...] += jnp.sum(d_pre, axis=0, keepdims=True)
        d_proj[rows, CONV_CH : CONV_CH + 128] = d_pre.astype(BF16)
        dsc = jnp.where(above, d_score[...], 0.0).astype(BF16)
        d_b = dot_nn(dsc, bc[rows, DS:])
        d_c = dot_tn(dsc, bc[rows, :DS])
        d_conv[s, 0:LEN, DI : DI + DS] = d_b * slope[rows, DI : DI + DS]
        d_conv[s, 0:LEN, DI + DS :] = d_c * slope[rows, DI + DS :]

    @pl.loop(0, CONV_CH // 256)
    def _(j):
        cols = pl.ds(pl.multiple_of(j * 256, 256), 256)
        w = conv_w[:, cols]
        zero = jnp.zeros((8, 256), F32)
        sums = (zero,) * (CONV + 1)
        for s in range(SEQS):

            def chunk(i, sums):
                base = pl.multiple_of(i * 32, 32)
                later = d_conv[s, pl.ds(base, 40), cols]
                near = conv_in[s, pl.ds(base, 40), cols]
                here = later[0:32]
                back = w[CONV - 1 : CONV] * here
                for k in range(CONV - 1):
                    back = back + w[k : k + 1] * later[3 - k : 35 - k]
                d_proj[pl.ds(pl.multiple_of(s * LEN + base, 32), 32), cols] = back.astype(BF16)

                def fold(v):
                    return (v[0:8] + v[8:16]) + (v[16:24] + v[24:32])

                new = [sums[k] + fold(here * near[5 + k : 37 + k]) for k in range(CONV)]
                return tuple(new) + (sums[CONV] + fold(here),)

            sums = lax.fori_loop(0, LEN // 32, chunk, sums)
        for k in range(CONV):
            g_conv_w[k : k + 1, cols] = jnp.sum(sums[k], axis=0, keepdims=True)
        g_conv_b[:, cols] = jnp.sum(sums[CONV], axis=0, keepdims=True)

    @pl.loop(0, 4)
    def _(j):
        cols = pl.ds(pl.multiple_of(j * 256, 256), 256)
        for half in range(2):
            src = pl.ds(pl.multiple_of(j * 256 + half * HALF1, 256), 256)
            g = dot_tn(hidden[...], d_proj[:, src]).astype(BF16)
            side = jnp.where(core == half, 0, 1)
            for zx in range(16):
                grads[side, slot_of(half, z0, x0, zx), :, cols] = g[zx * 48 : zx * 48 + 48]


def kernel_d(d_proj, w1, d_hid, tokens, gain, cot, grad_tokens, gain_grad, d_full):
    @pl.loop(0, 3)
    def _(j):
        cols = pl.ds(pl.multiple_of(j * 256, 256), 256)
        d_full[:, cols] = d_hid[:, cols] + dot_nt(d_proj[...], w1[cols])

    def chunk(i, total):
        rows = pl.ds(pl.multiple_of(i * 32, 32), 32)
        t = tokens[rows].astype(F32)
        inv = lax.rsqrt(jnp.mean(t * t, axis=1, keepdims=True) + EPS)
        normal = t * inv
        dh = d_full[rows]
        prod = dh * normal
        dn = dh * gain[...]
        mean = jnp.mean(dn * normal, axis=1, keepdims=True)
        grad_tokens[rows] = cot[rows].astype(F32) + inv * (dn - normal * mean)
        return total + (prod[0:8] + prod[8:16]) + (prod[16:24] + prod[24:32])

    total = lax.fori_loop(0, ROWS // 32, chunk, jnp.zeros((8, D), F32))
    gain_grad[...] = jnp.sum(total, axis=0, keepdims=True)


VM = pl.BlockSpec(memory_space=pltpu.VMEM)
SM = pl.BlockSpec(memory_space=pltpu.SMEM)
HB = pl.BlockSpec(memory_space=pl.ANY)


def call(kernel, name, ins, outs, scratch, args, flops, nbytes):
    return pl.pallas_call(
        kernel,
        name=name,
        in_specs=ins,
        out_specs=[VM] * len(outs),
        out_shape=[jax.ShapeDtypeStruct(s, d) for s, d in outs],
        scratch_shapes=scratch,
        compiler_params=pltpu.CompilerParams(vmem_limit_bytes=LIMIT),
        cost_estimate=pl.CostEstimate(flops=flops, bytes_accessed=nbytes, transcendentals=0),
    )(*args)


def lanes24(v):
    return jnp.pad(v, (0, 128 - NH)).reshape(1, 128)


def per_device(
    tokens,
    in_weight,
    out_weight,
    norm_gain,
    conv_weight,
    conv_bias,
    dt_bias,
    a_log,
    d_skip,
    gated_gain,
    cotangent,
):
    me = lax.axis_index("fsdp")
    core = lax.rem(me, 2)
    pos = jnp.stack([me // 32, lax.rem(me // 8, 4), core]).astype(jnp.int32)

    win = in_weight.reshape(6, NCOL)
    conv_cols = jnp.pad(win[:, DI:], ((0, 0), (0, WIDE1 - (NCOL - DI))))
    halves = jnp.stack(
        [
            jnp.concatenate([conv_cols[:, :HALF1], win[:, :DI]], axis=1),
            jnp.concatenate([conv_cols[:, HALF1:], out_weight.reshape(6, DI)], axis=1),
        ]
    )
    sent = jnp.broadcast_to(halves[None], (4, 2, 6, HALF1 + DI)).reshape(8, 6, HALF1 + DI)
    eight = lax.all_to_all(sent, "fsdp", 0, 0, axis_index_groups=EIGHTS)
    first = eight[:, :, :HALF1].reshape(48, HALF1)
    second = eight[:, :, HALF1:]
    as_gate = jnp.concatenate(
        [second[:, :, :D].reshape(48, D), second[:, :, D:].reshape(48, D)], axis=0
    )
    second = jnp.where(core == 0, as_gate, second.reshape(96, D))

    own1 = ring_gather(jnp.concatenate(ring_gather(first, False), axis=0), True)
    other1 = [swap_core(v) for v in own1]
    own2 = ring_gather(jnp.concatenate(ring_gather(second, False), axis=0), True)
    other2 = [swap_core(v) for v in own2]

    gain = norm_gain.reshape(1, D)
    rate = lanes24(-jnp.exp(a_log))
    skip = jnp.repeat(d_skip, HEAD).reshape(1, DI)
    tap_bias = conv_bias.reshape(1, CONV_CH)

    hidden, w1, conv_in, slope, xs, bc, dt_pre, acum, bcum, y = call(
        kernel_a,
        "forward_ssd",
        [SM] + [VM] * 7 + [HB] * 8,
        [
            ((ROWS, D), BF16),
            ((D, WIDE1), BF16),
            ((SEQS, PADLEN, CONV_CH), F32),
            ((ROWS, CONV_CH), F32),
            ((ROWS, DI), BF16),
            ((ROWS, 2 * DS), BF16),
            ((ROWS, 128), F32),
            ((ROWS, 128), F32),
            ((ROWS, 128), F32),
            ((ROWS, DI), F32),
        ],
        [
            pltpu.VMEM((LEN, LEN), F32),
            pltpu.VMEM((128, LEN), F32),
            pltpu.SemaphoreType.DMA((2, 4, 4)),
        ],
        [pos, tokens, gain, conv_weight, tap_bias, lanes24(dt_bias), rate, skip] + own1 + other1,
        8_000_000_000,
        20_000_000,
    )

    out, d_y, grads2, d_hid, g_gated = call(
        kernel_b,
        "gate_output",
        [SM] + [VM] * 5 + [HB] * 8,
        [
            ((ROWS, D), BF16),
            ((ROWS, DI), F32),
            ((2, 16, 96, D), BF16),
            ((ROWS, D), F32),
            ((1, DI), F32),
        ],
        [
            pltpu.VMEM((2 * DI, D), BF16),
            pltpu.VMEM((ROWS, DI), F32),
            pltpu.VMEM((ROWS, DI), F32),
            pltpu.VMEM((ROWS, DI), BF16),
            pltpu.VMEM((ROWS, DI), BF16),
            pltpu.VMEM((ROWS, 128), F32),
            pltpu.VMEM((16, DI), F32),
            pltpu.SemaphoreType.DMA((2, 4, 4, 2)),
        ],
        [pos, hidden, y, tokens, cotangent, gated_gain.reshape(1, DI)] + own2 + other2,
        9_000_000_000,
        20_000_000,
    )

    sum2 = grads2[0].astype(F32) + swap_core(grads2[1]).astype(F32)
    sum2 = sum2.reshape(4, 4, 96, D)
    sum2 = ring_reduce([sum2[r] for r in range(4)], True)
    sum2 = ring_reduce([sum2[r] for r in range(4)], False)
    as_gate = sum2.reshape(2, 8, 6, D).swapaxes(0, 1).reshape(8, 12, D)
    sum2 = jnp.where(core == 0, as_gate, sum2.reshape(8, 12, D)).astype(BF16)
    back2 = lax.all_to_all(sum2, "fsdp", 0, 0, axis_index_groups=EIGHTS)
    back2 = jnp.sum(back2.reshape(4, 2, 12, D).astype(F32), axis=0)
    grad_gate = back2[0].reshape(2, 6, D).swapaxes(0, 1).reshape(6, DI)
    grad_out = back2[1].reshape(-1)

    grads1, d_proj, g_conv_w, g_conv_b, g_skip, g_dt, g_alog = call(
        kernel_c,
        "backward_ssd",
        [SM] + [VM] * 13,
        [
            ((2, 16, 48, HALF1), BF16),
            ((ROWS, WIDE1), BF16),
            ((CONV, CONV_CH), F32),
            ((1, CONV_CH), F32),
            ((1, DI), F32),
            ((1, 128), F32),
            ((1, 128), F32),
        ],
        [
            pltpu.VMEM((SEQS, PADLEN, CONV_CH), F32),
            pltpu.VMEM((LEN, LEN), F32),
            pltpu.VMEM((128, LEN), F32),
            pltpu.VMEM((LEN, LEN), F32),
            pltpu.VMEM((LEN, 128), F32),
            pltpu.VMEM((LEN, 128), F32),
        ],
        [pos, xs, bc, acum, bcum, dt_pre, d_y, y, conv_in, slope, conv_weight, rate, skip, hidden],
        8_000_000_000,
        30_000_000,
    )

    grad_tokens, g_norm = call(
        kernel_d,
        "grad_tokens",
        [VM] * 6,
        [((ROWS, D), F32), ((1, D), F32)],
        [pltpu.VMEM((ROWS, D), F32)],
        [d_proj, w1, d_hid, tokens, gain, cotangent],
        2_000_000_000,
        10_000_000,
    )

    small = jnp.concatenate(
        [
            g_norm.reshape(-1),
            g_conv_w.reshape(-1),
            g_conv_b.reshape(-1),
            g_dt[0, :NH],
            g_alog[0, :NH],
            jnp.sum(g_skip.reshape(NH, HEAD), axis=1),
            g_gated.reshape(-1),
        ]
    )
    count = small.shape[0]
    small = jnp.pad(small, (0, 12 * HALF1 - count)).reshape(12, HALF1)

    def split(v):
        hi = lax.reduce_precision(v, 8, 7)
        return jnp.concatenate([hi.astype(BF16), (v - hi).astype(BF16)], axis=0)

    def joined(v):
        return v[..., :12, :].astype(F32) + v[..., 12:, :].astype(F32)

    def reduce_with_small(parts, extra, last):
        packed = jnp.pad(split(extra), ((0, 8), (0, 0)))
        got, more = [parts[0].astype(F32)], [joined(packed[:24])]
        for r in (1, 2, 3):
            there = lax.ppermute(
                jnp.concatenate([parts[r].astype(BF16), packed], axis=0),
                "fsdp",
                ring_pairs(r, last),
            )
            got.append(there[:-32].astype(F32))
            more.append(joined(there[-32:-8]))
        return (got[0] + got[2]) + (got[1] + got[3]), (more[0] + more[2]) + (more[1] + more[3])

    sum1 = grads1[0].astype(F32) + swap_core(grads1[1]).astype(F32)
    sum1 = sum1.reshape(4, 192, HALF1)
    sum1, small = reduce_with_small([sum1[r] for r in range(4)], small, True)
    sum1 = sum1.reshape(4, 48, HALF1)
    sum1, small = reduce_with_small([sum1[r] for r in range(4)], small, False)
    packed = jnp.concatenate(
        [
            jnp.broadcast_to(split(small)[None], (8, 24, HALF1)),
            sum1.reshape(8, 6, HALF1).astype(BF16),
            jnp.zeros((8, 2, HALF1), BF16),
        ],
        axis=1,
    )
    back1 = lax.all_to_all(packed, "fsdp", 0, 0, axis_index_groups=EIGHTS)
    small = jnp.sum(joined(back1[:, :24]), axis=0).reshape(-1)
    back1 = jnp.sum(back1[:, 24:30].reshape(4, 2, 6, HALF1).astype(F32), axis=0)
    grad_in = jnp.concatenate(
        [grad_gate, back1[0], back1[1][:, : NCOL - DI - HALF1]], axis=1
    ).reshape(-1)

    pieces = []
    start = 0
    for size in (D, CONV * CONV_CH, CONV_CH, NH, NH, NH, DI):
        pieces.append(small[start : start + size])
        start += size
    pieces[1] = pieces[1].reshape(CONV, CONV_CH)
    return (out, grad_tokens, grad_in, grad_out) + tuple(pieces)


def solution(mesh):
    rows = P("fsdp", None)
    flat = P("fsdp")
    same = P()
    return jax.shard_map(
        per_device,
        mesh=mesh,
        in_specs=(rows, flat, flat) + (same,) * 7 + (rows,),
        out_specs=(rows, rows, flat, flat) + (same,) * 7,
        check_vma=False,
    )
```

```python
import functools

import jax
import jax.numpy as jnp
from jax import lax
from jax.experimental import pallas as pl
from jax.experimental.pallas import tpu as pltpu
from jax.sharding import PartitionSpec as P

D = 768
NH = 24
DS = 128
HEAD = 64
CONV = 4
LEN = 256
DI = 1536
CONV_CH = 1792
NCOL = 3352
ROWS = 512
SEQS = 2
PADLEN = LEN + 8
HALF1 = 1024
WIDE1 = 2048
EPS = 1e-5
LOG2E = 1.4426950408889634
P_GAIN, P_CONV, P_BIAS, P_DT, P_RATE, P_SKIP, P_GATED, P_ROWS = 0, 1, 5, 6, 7, 8, 9, 16
LIMIT = 63 * 1024 * 1024
F32 = jnp.float32
BF16 = jnp.bfloat16
HIGHEST = lax.Precision.HIGHEST


def index_of(z, x, y, c):
    return ((z % 4 * 4 + x % 4) * 4 + y % 4) * 2 + c


def everyone():
    for z in range(4):
        for x in range(4):
            for y in range(4):
                for c in range(2):
                    yield z, x, y, c


def ring_pairs(shift, last):
    pairs = []
    for z, x, y, c in everyone():
        along_z = (c == 0) == last
        to = (z + shift, x, y, c) if along_z else (z, x + shift, y, c)
        pairs.append((index_of(z, x, y, c), index_of(*to)))
    return pairs


CORE_PAIRS = [(index_of(*p), index_of(*p[:3], 1 - p[3])) for p in everyone()]
SIXTEENS = [[k * 8 + j for k in range(16)] for j in range(8)]
EIGHTS = [[(z * 4 + x) * 8 + k for k in range(8)] for z in range(4) for x in range(4)]


def ring_gather(value, last):
    return [value] + [
        lax.ppermute(value, "fsdp", ring_pairs(shift, last)) for shift in (1, 2, 3)
    ]


def swap_core(value):
    return lax.ppermute(value, "fsdp", CORE_PAIRS)


def dot_nn(a, b):
    return jnp.dot(a, b, preferred_element_type=F32)


def dot_nt(a, b):
    return lax.dot_general(a, b, (((1,), (1,)), ((), ())), preferred_element_type=F32)


def dot_tn(a, b):
    return lax.dot_general(a, b, (((0,), (0,)), ((), ())), preferred_element_type=F32)


def dot_exact(a, b):
    return jnp.dot(a, b, preferred_element_type=F32, precision=HIGHEST)


def sigmoid(v):
    return 0.5 * jnp.tanh(0.5 * v) + 0.5


def softplus(v):
    e = jnp.exp(-jnp.abs(v))
    small = e * (1.0 - e * (0.5 - e * (1.0 / 3.0)))
    return jnp.maximum(v, 0.0) + jnp.where(e < 1e-3, small, jnp.log(1.0 + e))


def iota(shape, dim):
    return lax.broadcasted_iota(jnp.int32, shape, dim)


def source_zx(half, z0, x0, r3, r2):
    zr = jnp.where(half == 0, r3, r2)
    xr = jnp.where(half == 0, r2, r3)
    return lax.rem(z0 - zr + 4, 4) * 4 + lax.rem(x0 - xr + 4, 4)


def head_masks():
    lane = iota((1, 128), 1)
    first = jnp.where(lane < 64, 1.0, 0.0).astype(BF16)
    second = jnp.where(lane < 64, 0.0, 1.0).astype(BF16)
    return first, second


def kernel_a(
    ready, flush, pos, tokens, params,
    b0, b1, b2, b3, q0, q1, q2, q3,
    hidden_o, turned_o, w1_o, conv_in_o, slope_o, xs_o, bc, dt_pre, acum, bcum,
    hidden, turned, w1, conv_in, slope, xs, sems, out_sems, tile_sems,
):
    z0, x0, core = pos[0], pos[1], pos[2]
    copies = []
    for side, refs in enumerate(((b0, b1, b2, b3), (q0, q1, q2, q3))):
        half = core if side == 0 else 1 - core
        col = pl.multiple_of(half * HALF1, HALF1)
        for r3 in range(4):
            for r2 in range(4):
                row = pl.multiple_of(source_zx(half, z0, x0, r3, r2) * 48, 16)
                copies.append(
                    pltpu.make_async_copy(
                        refs[r3].at[pl.ds(r2 * 48, 48)],
                        w1.at[pl.ds(row, 48), pl.ds(col, HALF1)],
                        sems.at[side, r3, r2],
                    )
                )
    for copy in copies:
        copy.start()
    ready()
    gain = params[P_GAIN : P_GAIN + 1, :D]

    @pl.loop(0, ROWS // 64)
    def _(i):
        rows = pl.ds(pl.multiple_of(i * 64, 64), 64)
        t = tokens[rows].astype(F32)
        inv = lax.rsqrt(jnp.mean(t * t, axis=1, keepdims=True) + EPS)
        hidden[rows] = (t * inv * gain).astype(BF16)

    turned[...] = hidden[...].T
    for s in range(SEQS):
        conv_in[s, 0:8] = jnp.zeros((8, CONV_CH), F32)
    for copy in copies:
        copy.wait()
    outs = [
        pltpu.make_async_copy(hidden, hidden_o, out_sems.at[0]),
        pltpu.make_async_copy(w1, w1_o, out_sems.at[1]),
        pltpu.make_async_copy(turned, turned_o, out_sems.at[2]),
    ]
    for copy in outs:
        copy.start()

    def conv_tile(j, cols, emit):
        p = dot_nn(hidden[...], w1[:, cols])
        for s in range(SEQS):
            conv_in[s, 8:PADLEN, cols] = p[s * LEN : (s + 1) * LEN]
        w = params[P_CONV : P_CONV + CONV, cols]
        bias = params[P_BIAS : P_BIAS + 1, cols]
        for s in range(SEQS):

            @pl.loop(0, LEN // 32, unroll=4)
            def _(i):
                base = pl.multiple_of(i * 32, 32)
                near = conv_in[s, pl.ds(base, 40), cols]
                total = bias + w[0:1] * near[5:37]
                for k in range(1, CONV):
                    total = total + w[k : k + 1] * near[5 + k : 37 + k]
                sig = sigmoid(total)
                act = total * sig
                rows = pl.ds(pl.multiple_of(s * LEN + base, 32), 32)
                slope[rows, cols] = sig * (1.0 + total * (1.0 - sig))
                emit(rows, act.astype(BF16))

    def tile_puts(j, cols):
        puts = [
            pltpu.make_async_copy(conv_in.at[s, :, cols], conv_in_o.at[s, :, cols], tile_sems.at[j, s])
            for s in range(SEQS)
        ]
        return puts + [
            pltpu.make_async_copy(slope.at[:, cols], slope_o.at[:, cols], tile_sems.at[j, 2])
        ]

    def xs_put(j, cols):
        return pltpu.make_async_copy(xs.at[:, cols], xs_o.at[:, cols], tile_sems.at[j, 3])

    def emit_bc(rows, act):
        bc[rows] = act

    last = pl.ds(1536, 256)
    conv_tile(6, last, emit_bc)
    for put in tile_puts(6, last):
        put.start()

    pre = dot_nn(hidden[...], w1[:, CONV_CH : CONV_CH + 128]) + params[P_DT : P_DT + 1, :128]
    dt_pre[...] = pre
    step = softplus(pre)
    inc = step * params[P_RATE : P_RATE + 1, :128] * LOG2E
    log_step = jnp.log(jnp.maximum(step, 1e-37)) * LOG2E
    lower = jnp.where(iota((LEN, LEN), 0) >= iota((LEN, LEN), 1), 1.0, 0.0)
    for s in range(SEQS):
        rows = slice(s * LEN, (s + 1) * LEN)
        a = dot_exact(lower, inc[rows])
        acum[rows] = a
        bcum[rows] = a - log_step[rows]
    flush()

    @pl.loop(0, 6)
    def _(j):
        cols = pl.ds(pl.multiple_of(j * 256, 256), 256)

        def emit(rows, act):
            xs[rows, cols] = act

        conv_tile(j, cols, emit)
        for put in tile_puts(j, cols) + [xs_put(j, cols)]:
            put.start()

    @pl.loop(0, 6)
    def _(j):
        cols = pl.ds(pl.multiple_of(j * 256, 256), 256)
        for put in tile_puts(j, cols) + [xs_put(j, cols)]:
            put.wait()

    for put in tile_puts(6, last) + outs:
        put.wait()


def kernel_s(ready, flush, params, xs_i, bc, acum, bcum, y_o, xs, y, score, bcum_t, in_sems, out_sems):
    gets = [
        pltpu.make_async_copy(xs_i.at[pl.ds(s * LEN, LEN)], xs.at[pl.ds(s * LEN, LEN)], in_sems.at[s])
        for s in range(SEQS)
    ]
    for copy in gets:
        copy.start()
    below = iota((LEN, LEN), 0) >= iota((LEN, LEN), 1)
    mask0, mask1 = head_masks()
    outs = []
    ready()
    for s in range(SEQS):
        rows = slice(s * LEN, (s + 1) * LEN)
        a = acum[rows]
        bcum_t[...] = bcum[rows].T
        score[...] = jnp.where(below, dot_nt(bc[rows, DS:], bc[rows, :DS]), 0.0)
        gets[s].wait()

        @pl.loop(0, NH // 2, unroll=4)
        def _(p):
            lanes = pl.ds(pl.multiple_of(p * 128, 128), 128)
            x = xs[s * LEN : (s + 1) * LEN, lanes]
            turned = pltpu.roll(a, lax.rem(128 - 2 * p, 128), 1)
            top = jnp.zeros((128, 128), F32)
            low = jnp.zeros((128, 128), F32)
            for i, mask in enumerate((mask0, mask1)):
                col = turned[:, i : i + 1]
                row = bcum_t[pl.ds(2 * p + i, 1), :]
                xm = x * mask
                e0 = jnp.exp2(jnp.minimum(col[:128] - row[:, :128], 64.0))
                m0 = (e0 * score[:128, :128]).astype(BF16)
                top = top + dot_nn(m0, xm[:128])
                e1 = jnp.exp2(jnp.minimum(col[128:] - row, 64.0))
                m1 = (e1 * score[128:, :]).astype(BF16)
                low = low + dot_nn(m1, xm)
            skip = params[P_SKIP : P_SKIP + 1, lanes]
            y[s * LEN : s * LEN + 128, lanes] = top + skip * x[:128].astype(F32)
            y[s * LEN + 128 : (s + 1) * LEN, lanes] = low + skip * x[128:].astype(F32)

        span = pl.ds(s * LEN, LEN)
        outs.append(pltpu.make_async_copy(y.at[span], y_o.at[span], out_sems.at[s]))
        outs[-1].start()
    for copy in outs:
        copy.wait()


def store_gate(turned, big, dest, extra):
    @pl.loop(0, 3)
    def _(j):
        cols = pl.ds(pl.multiple_of(j * 256, 256), 256)
        for lr in range(2):
            src = pl.ds(pl.multiple_of(j * 256 + lr * D, 256), 256)
            g = dot_nn(turned[...], big[:, src])
            for zx in range(16):
                part = g[zx * 48 : zx * 48 + 48]
                if extra is not None:
                    part = part + extra[zx, lr * 48 : lr * 48 + 48, cols].astype(F32)
                dest[zx, lr * 48 : lr * 48 + 48, cols] = part.astype(BF16)


def store_out(small, big, dest, extra):
    for t in range(4):
        g = dot_tn(big[:, t * 384 : (t + 1) * 384], small[...])
        for k in range(4):
            part = g[k * 96 : (k + 1) * 96]
            if extra is not None:
                part = part + extra[t * 4 + k].astype(F32)
            dest[t * 4 + k] = part.astype(BF16)


def kernel_b(
    ready, flush, pos, hidden, turned, y_i, tokens_i, cot_i, params,
    b0, b1, b2, b3, q0, q1, q2, q3,
    out_o, d_y_o, grads_o, d_hid_o, normed_o, d_gate_o, gain_grad,
    y, tokens, cot, out, d_y, grads, d_hid,
    weights, gate_in, d_normed, normed, d_gate, gate_inv, acc, sems, io_sems,
):
    core = pos[2]
    z0, x0 = pos[0], pos[1]
    copies = ([], [])
    for side, refs in enumerate(((b0, b1, b2, b3), (q0, q1, q2, q3))):
        half = core if side == 0 else 1 - core
        for r3 in range(4):
            for r2 in range(4):
                zx = source_zx(half, z0, x0, r3, r2)
                for lr in range(2):
                    row = jnp.where(half == 0, lr * D + zx * 48, DI + zx * 96 + lr * 48)
                    copies[side].append(
                        pltpu.make_async_copy(
                            refs[r3].at[pl.ds(r2 * 96 + lr * 48, 48)],
                            weights.at[pl.ds(pl.multiple_of(row, 16), 48)],
                            sems.at[side, r3, r2, lr],
                        )
                    )

    def each(side, act):
        @pl.when(core == side)
        def _():
            for copy in copies[0]:
                act(copy)

        @pl.when(core != side)
        def _():
            for copy in copies[1]:
                act(copy)

    get_y = pltpu.make_async_copy(y_i, y, io_sems.at[0])
    get_tokens = pltpu.make_async_copy(tokens_i, tokens, io_sems.at[1])
    get_cot = pltpu.make_async_copy(cot_i, cot, io_sems.at[2])
    put_out = pltpu.make_async_copy(out, out_o, io_sems.at[3])
    put_dy = pltpu.make_async_copy(d_y, d_y_o, io_sems.at[4])
    put_dhid = pltpu.make_async_copy(d_hid, d_hid_o, io_sems.at[5])
    each(0, lambda copy: copy.start())
    get_y.start()
    each(1, lambda copy: copy.start())
    get_tokens.start()
    get_cot.start()
    ready()
    gain = params[P_GATED : P_GATED + 1, :DI]
    each(0, lambda copy: copy.wait())

    @pl.loop(0, 3)
    def _(j):
        cols = pl.ds(pl.multiple_of(j * 256, 256), 256)
        right = pl.ds(pl.multiple_of(j * 256 + D, 256), 256)
        gate_in[:, cols] = dot_nn(hidden[...], weights[0:D, cols])
        gate_in[:, right] = dot_nn(hidden[...], weights[D:DI, cols])

    get_y.wait()

    @pl.loop(0, ROWS // 16, unroll=4)
    def _(i):
        rows = pl.ds(pl.multiple_of(i * 16, 16), 16)
        g = gate_in[rows]
        gated = y[rows] * (g * sigmoid(g))
        inv = lax.rsqrt(jnp.mean(gated * gated, axis=1, keepdims=True) + EPS)
        gate_inv[rows] = jnp.broadcast_to(inv, (16, 128))
        normed[rows] = (gated * inv * gain).astype(BF16)

    put_normed = pltpu.make_async_copy(normed, normed_o, io_sems.at[6])
    put_normed.start()
    each(1, lambda copy: copy.wait())
    get_tokens.wait()
    get_cot.wait()

    @pl.loop(0, 3)
    def _(j):
        cols = pl.ds(pl.multiple_of(j * 256, 256), 256)
        mixed = dot_nn(normed[...], weights[DI:, cols])
        out[:, cols] = (tokens[:, cols].astype(F32) + mixed).astype(BF16)

    put_out.start()

    @pl.loop(0, 6)
    def _(j):
        cols = pl.ds(pl.multiple_of(j * 256, 256), 256)
        d_normed[:, cols] = dot_nt(cot[...], weights[pl.ds(pl.multiple_of(j * 256 + DI, 256), 256)])

    acc[...] = jnp.zeros_like(acc)

    @pl.loop(0, ROWS // 16, unroll=4)
    def _(i):
        rows = pl.ds(pl.multiple_of(i * 16, 16), 16)
        g = gate_in[rows]
        sig = sigmoid(g)
        act = g * sig
        yv = y[rows]
        inv = gate_inv[rows][:, 0:1]
        gnorm = yv * act * inv
        dn = d_normed[rows]
        prod = dn * gnorm
        acc[...] += prod
        dgn = dn * gain
        mean = jnp.mean(dgn * gnorm, axis=1, keepdims=True)
        d_gated = inv * (dgn - gnorm * mean)
        d_y[rows] = d_gated * act
        d_gate[rows] = (d_gated * yv * (sig * (1.0 + g * (1.0 - sig)))).astype(BF16)

    put_dy.start()
    put_gate = pltpu.make_async_copy(d_gate, d_gate_o, io_sems.at[7])
    put_gate.start()
    gain_grad[...] = jnp.sum(acc[...], axis=0, keepdims=True)
    flush()

    @pl.when(core == 0)
    def _():
        store_out(cot, normed, grads, None)

    @pl.when(core != 0)
    def _():
        store_gate(turned, d_gate, grads, None)

    put_grads = pltpu.make_async_copy(grads, grads_o, io_sems.at[8])
    put_grads.start()

    @pl.loop(0, 3)
    def _(j):
        cols = pl.ds(pl.multiple_of(j * 256, 256), 256)
        right = pl.ds(pl.multiple_of(j * 256 + D, 256), 256)
        d_hid[:, cols] = dot_nt(d_gate[:, :D], weights[cols]) + dot_nt(
            d_gate[:, D:], weights[right]
        )

    put_dhid.start()
    for copy in (put_out, put_dy, put_normed, put_gate, put_grads, put_dhid):
        copy.wait()


def kernel_f(ready, _, pos, turned_i, cot_i, d_gate, normed, got, total_o, turned, cot, big, total, sems):
    core = pos[2]

    @pl.when(core == 0)
    def _():
        gets = [
            pltpu.make_async_copy(turned_i, turned, sems.at[0]),
            pltpu.make_async_copy(d_gate, big, sems.at[1]),
        ]
        for get in gets:
            get.start()
        for get in gets:
            get.wait()
        ready()
        store_gate(turned, big, total, got)

    @pl.when(core != 0)
    def _():
        gets = [
            pltpu.make_async_copy(cot_i, cot, sems.at[0]),
            pltpu.make_async_copy(normed, big, sems.at[1]),
        ]
        for get in gets:
            get.start()
        for get in gets:
            get.wait()
        ready()
        store_out(cot, big, total, got)

    put = pltpu.make_async_copy(total, total_o, sems.at[2])
    put.start()
    put.wait()


def split_dot(v, pick):
    hi = v.astype(BF16)
    lo = (v - hi.astype(F32)).astype(BF16)
    return dot_nn(jnp.concatenate([hi, lo], axis=1), pick)


def kernel_c(
    ready, flush, xs_i, bc, acum, bcum, dt_pre, d_y_i, y_i, params,
    d_act_o, d_pre_o, g_skip, g_dt, g_alog,
    xs, d_y, y, d_act, score_t, acum_t, d_score, rsum, csum, in_sems, out_sems,
):
    gets = [
        [
            pltpu.make_async_copy(
                src.at[pl.ds(s * LEN, LEN)], dst.at[pl.ds(s * LEN, LEN)], in_sems.at[s, k]
            )
            for k, (src, dst) in enumerate(((xs_i, xs), (d_y_i, d_y), (y_i, y)))
        ]
        for s in range(SEQS)
    ]
    for copy in gets[0] + gets[1]:
        copy.start()
    above = iota((LEN, LEN), 0) <= iota((LEN, LEN), 1)
    upper = jnp.where(above, 1.0, 0.0)
    mask0, mask1 = head_masks()
    lane_head = iota((256, 128), 0) % 128 // 64
    head_col = iota((256, 128), 1)
    lane = iota((1, 128), 1)
    g_skip[...] = jnp.zeros_like(g_skip)
    g_dt[...] = jnp.zeros_like(g_dt)
    g_alog[...] = jnp.zeros_like(g_alog)
    ready()
    rate = params[P_RATE : P_RATE + 1, :128]
    puts = []
    for s in range(SEQS):
        rows = pl.ds(s * LEN, LEN)
        acum_t[...] = acum[rows].T
        score_t[...] = jnp.where(above, dot_nt(bc[rows, :DS], bc[rows, DS:]), 0.0)
        d_score[...] = jnp.zeros_like(d_score)
        rsum[...] = jnp.zeros_like(rsum)
        csum[...] = jnp.zeros_like(csum)
        b = bcum[rows]
        for copy in gets[s]:
            copy.wait()

        @pl.loop(0, NH // 2, unroll=4)
        def _(p):
            lanes = pl.ds(pl.multiple_of(p * 128, 128), 128)
            x = xs[rows, lanes]
            dy = d_y[rows, lanes]
            ds = dy.astype(BF16)
            turned = pltpu.roll(b, lax.rem(128 - 2 * p, 128), 1)
            top = jnp.zeros((128, 128), F32)
            low = jnp.zeros((128, 128), F32)
            for i, mask in enumerate((mask0, mask1)):
                col = turned[:, i : i + 1]
                row = acum_t[pl.ds(2 * p + i, 1), :]
                dm = ds * mask
                xm = x * mask
                e0 = jnp.exp2(jnp.minimum(row - col[:128], 64.0))
                m0 = (e0 * score_t[:128, :]).astype(BF16)
                top = top + dot_nn(m0, dm)
                d_score[:128, :] += dot_nt(xm[:128], ds) * e0
                e1 = jnp.exp2(jnp.minimum(row[:, 128:] - col[128:], 64.0))
                m1 = (e1 * score_t[128:, 128:]).astype(BF16)
                low = low + dot_nn(m1, dm[128:])
                d_score[128:, 128:] += dot_nt(xm[128:], ds[128:]) * e1
            dxs = jnp.concatenate([top, low], axis=0)
            skip = params[P_SKIP : P_SKIP + 1, lanes]
            xf = x.astype(F32)
            own = ds.astype(F32) * (y[rows, lanes] - skip * xf)
            across = xf * dxs
            pick = jnp.where(lane_head + 2 * p == head_col, 1.0, 0.0).astype(BF16)
            rsum[...] += split_dot(own, pick)
            csum[...] += split_dot(across, pick)
            both = jnp.sum(dy * xf, axis=0, keepdims=True)
            first = jnp.sum(jnp.where(lane < 64, both, 0.0), axis=1, keepdims=True)
            second = jnp.sum(jnp.where(lane < 64, 0.0, both), axis=1, keepdims=True)
            g_skip[...] += jnp.where(lane == 2 * p, first, 0.0) + jnp.where(
                lane == 2 * p + 1, second, 0.0
            )
            d_act[rows, lanes] = skip * dy + dxs

        pre = dt_pre[rows]
        step = softplus(pre)
        sig = 1.0 / (1.0 + jnp.exp(-pre))
        ratio = jnp.where(pre < -20.0, 1.0, sig / jnp.maximum(step, 1e-30))
        d_cum = rsum[...] - csum[...]
        d_inc = dot_exact(upper, d_cum)
        g_alog[...] += jnp.sum(d_inc * step, axis=0, keepdims=True) * rate
        d_pre = csum[...] * ratio + d_inc * rate * sig
        g_dt[...] += jnp.sum(d_pre, axis=0, keepdims=True)
        d_pre_o[rows] = d_pre.astype(BF16)
        dsc = jnp.where(above, d_score[...], 0.0).astype(BF16)
        d_act[rows, DI : DI + DS] = dot_nn(dsc, bc[rows, DS:])
        d_act[rows, DI + DS :] = dot_tn(dsc, bc[rows, :DS])
        puts.append(pltpu.make_async_copy(d_act.at[rows], d_act_o.at[rows], out_sems.at[s]))
        puts[-1].start()
    flush()
    for put in puts:
        put.wait()


def kernel_e(
    ready, flush, pos, act_i, d_pre, conv_in_i, slope_i, params, turned, _,
    grads_o, d_proj_o, g_conv_w, g_conv_b,
    d_proj, d_act, slope, conv_in, grads, sems, out_sems, proj_sems,
):
    core = pos[2]

    def tile_copies(j):
        cols = pl.ds(pl.multiple_of(j * 256, 256), 256)
        pairs = []
        for s in range(SEQS):
            pairs.append((act_i.at[pl.ds(s * LEN, LEN), cols], d_act.at[s, 0:LEN, cols]))
            pairs.append((slope_i.at[pl.ds(s * LEN, LEN), cols], slope.at[s, 0:LEN, cols]))
            pairs.append((conv_in_i.at[s, :, cols], conv_in.at[s, :, cols]))
        return [
            pltpu.make_async_copy(src, dst, sems.at[j, k]) for k, (src, dst) in enumerate(pairs)
        ]

    for j in range(CONV_CH // 256):
        for copy in tile_copies(j):
            copy.start()
    for s in range(SEQS):
        d_act[s, LEN:] = jnp.zeros((8, CONV_CH), F32)
        slope[s, LEN:] = jnp.zeros((8, CONV_CH), F32)
    ready()
    d_proj[:, CONV_CH : CONV_CH + 128] = d_pre[...]
    d_proj[:, CONV_CH + 128 :] = jnp.zeros((ROWS, 128), BF16)

    def put_tile(j):
        cols = pl.ds(pl.multiple_of(j * 256, 256), 256)
        return pltpu.make_async_copy(d_proj.at[:, cols], d_proj_o.at[:, cols], proj_sems.at[j])

    put_tile(7).start()

    @pl.loop(0, CONV_CH // 256)
    def _(j):
        cols = pl.ds(pl.multiple_of(j * 256, 256), 256)
        for copy in tile_copies(j):
            copy.wait()
        w = params[P_CONV : P_CONV + CONV, cols]
        zero = jnp.zeros((8, 256), F32)
        sums = (zero,) * (CONV + 1)
        for s in range(SEQS):

            def chunk(i, sums):
                base = pl.multiple_of(i * 32, 32)
                later = d_act[s, pl.ds(base, 40), cols] * slope[s, pl.ds(base, 40), cols]
                near = conv_in[s, pl.ds(base, 40), cols]
                here = later[0:32]
                back = w[CONV - 1 : CONV] * here
                for k in range(CONV - 1):
                    back = back + w[k : k + 1] * later[3 - k : 35 - k]
                d_proj[pl.ds(pl.multiple_of(s * LEN + base, 32), 32), cols] = back.astype(BF16)

                def fold(v):
                    return (v[0:8] + v[8:16]) + (v[16:24] + v[24:32])

                new = [sums[k] + fold(here * near[5 + k : 37 + k]) for k in range(CONV)]
                return tuple(new) + (sums[CONV] + fold(here),)

            sums = lax.fori_loop(0, LEN // 32, chunk, sums, unroll=4)
        for k in range(CONV):
            g_conv_w[k : k + 1, cols] = jnp.sum(sums[k], axis=0, keepdims=True)
        g_conv_b[:, cols] = jnp.sum(sums[CONV], axis=0, keepdims=True)
        put_tile(j).start()

    flush()

    def put_grads(j):
        cols = pl.ds(pl.multiple_of(j * 256, 256), 256)
        return pltpu.make_async_copy(grads.at[:, cols], grads_o.at[:, cols], out_sems.at[j])

    @pl.loop(0, 4)
    def _(j):
        cols = pl.ds(pl.multiple_of(j * 256, 256), 256)
        src = pl.ds(pl.multiple_of(j * 256 + (1 - core) * HALF1, 256), 256)
        grads[:, cols] = dot_nn(turned[...], d_proj[:, src]).astype(BF16)
        put_grads(j).start()

    for j in range(8):
        put_tile(j).wait()
    for j in range(4):
        put_grads(j).wait()


def kernel_g(
    ready, _, pos, turned, d_proj_i, got, g_conv_w, g_conv_b, g_gated, g_norm,
    g_dt, g_alog, g_skip, __, out0, out1, out2, out3,
    total, d_proj, small, sem, out_sems,
):
    z0, x0, core = pos[0], pos[1], pos[2]
    src = pl.ds(pl.multiple_of(core * HALF1, HALF1), HALF1)
    get = pltpu.make_async_copy(d_proj_i.at[:, src], d_proj, sem)
    get.start()
    rest = CONV_CH - HALF1
    small[...] = jnp.zeros_like(small)
    ready()
    small[0:4] = g_conv_w[:, :HALF1]
    small[4:8, :rest] = g_conv_w[:, HALF1:]
    small[8:9] = g_conv_b[:, :HALF1]
    small[9:10, :rest] = g_conv_b[:, HALF1:]
    small[10:11] = g_gated[:, :HALF1]
    small[11:12, : DI - HALF1] = g_gated[:, HALF1:]
    small[12:13, :D] = g_norm[...]
    small[12:13, D : D + 128] = g_dt[...]
    small[12:13, D + 128 :] = g_alog[...]
    small[14:15, :128] = g_skip[...]
    for k in (12, 14):
        exact = small[k : k + 1]
        small[k + 1 : k + 2] = exact - exact.astype(BF16).astype(F32)
    sent = small[...].astype(BF16)
    for r3 in range(4):
        total[r3, 192:208] = sent
    get.wait()

    @pl.loop(0, 4)
    def _(j):
        cols = pl.ds(pl.multiple_of(j * 256, 256), 256)
        g = dot_nn(turned[...], d_proj[:, cols]) + got[:, cols].astype(F32)
        g = g.astype(BF16)
        for zx in range(16):
            dz = lax.rem(zx // 4 - z0 + 4, 4)
            dx = lax.rem(zx % 4 - x0 + 4, 4)
            r3 = jnp.where(core == 0, dz, dx)
            r2 = jnp.where(core == 0, dx, dz)
            rows = pl.ds(pl.multiple_of(r2 * 48, 16), 48)
            total[r3, rows, cols] = g[zx * 48 : zx * 48 + 48]

    puts = [
        pltpu.make_async_copy(total.at[r], out, out_sems.at[r])
        for r, out in enumerate((out0, out1, out2, out3))
    ]
    for put in puts:
        put.start()
    for put in puts:
        put.wait()


def sum_of_four(a, b, c, d):
    return (a[...].astype(F32) + c[...].astype(F32)) + (b[...].astype(F32) + d[...].astype(F32))


def kernel_k(ready, flush, own, got1, got2, got3, *outs):
    ready()
    total = sum_of_four(own, got1, got2, got3).astype(BF16)
    for r2, out in enumerate(outs):
        out[0:48] = total[r2 * 48 : r2 * 48 + 48]
        out[48:64] = total[192:208]
    flush()


def kernel_l(ready, flush, own, got1, got2, got3, two, out):
    ready()
    total = sum_of_four(own, got1, got2, got3)
    rides = jnp.concatenate([total[48:56], total[56:64]], axis=1).astype(BF16)
    zero = jnp.zeros((2, HALF1), F32)
    for d in range(8):
        eight = slice(d * 8, d * 8 + 8)
        out[eight, :DI] = two[eight]
        piece = jnp.concatenate([total[d * 6 : d * 6 + 6], zero], axis=0)
        out[eight, DI : DI + HALF1] = piece.astype(BF16)
        out[eight, DI + HALF1 :] = rides
    flush()


def kernel_d(
    ready, flush, d_proj_i, w1_i, d_hid_i, tokens_i, params, cot_i, grad_tokens_o, gain_grad,
    d_proj, w1, d_hid, tokens, cot, d_full, grad_tokens, sems, out_sems,
):
    gets = [
        pltpu.make_async_copy(src, dst, sems.at[k])
        for k, (src, dst) in enumerate(
            (
                (w1_i, w1), (d_proj_i, d_proj), (d_hid_i, d_hid),
                (tokens_i, tokens), (cot_i, cot),
            )
        )
    ]
    for copy in gets:
        copy.start()
    for copy in gets[:3]:
        copy.wait()

    @pl.loop(0, 3)
    def _(j):
        cols = pl.ds(pl.multiple_of(j * 256, 256), 256)
        d_full[:, cols] = d_hid[:, cols] + dot_nt(d_proj[...], w1[cols])

    gets[3].wait()
    gets[4].wait()
    ready()
    gain = params[P_GAIN : P_GAIN + 1, :D]

    def chunk(i, total):
        rows = pl.ds(pl.multiple_of(i * 32, 32), 32)
        t = tokens[rows].astype(F32)
        inv = lax.rsqrt(jnp.mean(t * t, axis=1, keepdims=True) + EPS)
        normal = t * inv
        dh = d_full[rows]
        prod = dh * normal
        dn = dh * gain
        mean = jnp.mean(dn * normal, axis=1, keepdims=True)
        grad_tokens[rows] = cot[rows].astype(F32) + inv * (dn - normal * mean)
        return total + (prod[0:8] + prod[8:16]) + (prod[16:24] + prod[24:32])

    total = jnp.zeros((8, D), F32)
    puts = []
    for s in range(SEQS):
        total = lax.fori_loop(s * LEN // 32, (s + 1) * LEN // 32, chunk, total, unroll=4)
        span = pl.ds(s * LEN, LEN)
        puts.append(
            pltpu.make_async_copy(grad_tokens.at[span], grad_tokens_o.at[span], out_sems.at[s])
        )
        puts[-1].start()
    gain_grad[...] = jnp.sum(total, axis=0, keepdims=True)
    flush()
    for put in puts:
        put.wait()


def kernel_h(
    ready, flush, got, g_in, g_out, g_norm, g_conv_w, g_conv_b, g_dt, g_alog, g_skip, g_gated, rows,
):
    def added(core, start, size):
        parts = [
            got[16 * y + 8 * core : 16 * y + 8 * core + 8, start : start + size].astype(F32)
            for y in range(4)
        ]
        return (parts[0] + parts[1]) + (parts[2] + parts[3])

    ready()
    rows[:, :DI] = added(0, 0, DI)
    rows[:, DI : DI + HALF1] = added(0, DI, HALF1)
    rows[:, DI + HALF1 :] = added(1, DI, HALF1)
    outs = added(1, 0, DI)
    for r in range(6):
        g_in[pl.ds(r * NCOL, NCOL)] = rows[r : r + 1, :NCOL].reshape(NCOL)
        g_out[pl.ds(r * DI, DI)] = outs[r : r + 1].reshape(DI)
    base = DI + HALF1
    top = added(0, base, HALF1) + added(1, base, HALF1)
    low = added(0, base + HALF1, HALF1) + added(1, base + HALF1, HALF1)
    rest = CONV_CH - HALF1
    g_conv_w[:, :HALF1] = top[0:4]
    g_conv_w[:, HALF1:] = top[4:8, :rest]
    g_conv_b[...] = jnp.concatenate([low[0:1], low[1:2, :rest]], axis=1).reshape(CONV_CH)
    g_gated[...] = jnp.concatenate([low[2:3], low[3:4, : DI - HALF1]], axis=1).reshape(DI)
    exact = low[4:5] + low[5:6]
    skip = low[6:7, :128] + low[7:8, :128]
    g_norm[...] = exact[:, :D].reshape(D)
    g_dt[...] = exact[0, D : D + NH]
    g_alog[...] = exact[0, D + 128 : D + 128 + NH]
    g_skip[...] = skip[0, :NH]
    flush()


VM = pl.BlockSpec(memory_space=pltpu.VMEM)
SM = pl.BlockSpec(memory_space=pltpu.SMEM)
HB = pl.BlockSpec(memory_space=pl.ANY)


def call(kernel, name, ins, outs, scratch, args, us=0.01):
    taken = [k for k, spec in enumerate(ins) if spec is VM]
    given = [k for k, out in enumerate(outs) if out[2] is VM]
    n_in, n_out, n_scratch = len(ins), len(outs), len(scratch)

    def body(*refs):
        in_refs = list(refs[:n_in])
        out_refs = list(refs[n_in : n_in + n_out])
        own = refs[n_in + n_out : n_in + n_out + n_scratch]
        rest = refs[n_in + n_out + n_scratch :]
        in_bufs, rest = rest[: len(taken)], rest[len(taken) :]
        out_bufs, rest = rest[: len(given)], rest[len(given) :]
        gets, puts = [], []
        for n, k in enumerate(taken):
            gets.append(pltpu.make_async_copy(in_refs[k], in_bufs[n], rest[0].at[n]))
            in_refs[k] = in_bufs[n]
        for n, k in enumerate(given):
            puts.append(pltpu.make_async_copy(out_bufs[n], out_refs[k], rest[1].at[n]))
            out_refs[k] = out_bufs[n]
        for copy in gets:
            copy.start()

        def ready():
            for copy in gets:
                copy.wait()

        def flush():
            for copy in puts:
                copy.start()

        kernel(ready, flush, *in_refs, *out_refs, *own)
        for copy in puts:
            copy.wait()

    dma = pltpu.SemaphoreType.DMA
    extra = [pltpu.VMEM(args[k].shape, args[k].dtype) for k in taken]
    extra += [pltpu.VMEM(outs[k][0], outs[k][1]) for k in given]
    extra += [dma((max(len(taken), 1),)), dma((max(len(given), 1),))]
    return pl.pallas_call(
        body,
        name=name,
        in_specs=[HB if spec is VM else spec for spec in ins],
        out_specs=[HB] * n_out,
        out_shape=[jax.ShapeDtypeStruct(o[0], o[1]) for o in outs],
        scratch_shapes=list(scratch) + extra,
        compiler_params=pltpu.CompilerParams(vmem_limit_bytes=LIMIT),
        cost_estimate=pl.CostEstimate(
            flops=int(us * 1.1e9), bytes_accessed=100_000, transcendentals=0
        ),
    )(*args)


def per_device(
    tokens,
    in_weight,
    out_weight,
    norm_gain,
    conv_weight,
    conv_bias,
    dt_bias,
    a_log,
    d_skip,
    gated_gain,
    cotangent,
):
    me = lax.axis_index("fsdp")
    core = lax.rem(me, 2)
    pos = jnp.stack([me // 32, lax.rem(me // 8, 4), core]).astype(jnp.int32)

    win = in_weight.reshape(6, NCOL)
    conv_cols = jnp.pad(win[:, DI:], ((0, 0), (0, WIDE1 - (NCOL - DI))))
    halves = jnp.stack(
        [
            jnp.concatenate([conv_cols[:, :HALF1], win[:, :DI]], axis=1),
            jnp.concatenate([conv_cols[:, HALF1:], out_weight.reshape(6, DI)], axis=1),
        ]
    )
    sent = jnp.broadcast_to(halves[None], (4, 2, 6, HALF1 + DI)).reshape(8, 6, HALF1 + DI)
    eight = lax.all_to_all(sent, "fsdp", 0, 0, axis_index_groups=EIGHTS)

    def row(v):
        return jnp.pad(v, (0, CONV_CH - v.shape[0]))[None]

    params = jnp.concatenate(
        [
            row(norm_gain), conv_weight, row(conv_bias), row(dt_bias), row(-jnp.exp(a_log)),
            row(jnp.repeat(d_skip, HEAD)), row(gated_gain),
            jnp.zeros((P_ROWS - P_GATED - 1, CONV_CH), F32),
        ],
        axis=0,
    )
    eight, params, pos = lax.optimization_barrier((eight, params, pos))
    near = ring_gather(eight.reshape(48, HALF1 + DI), False)
    own1 = ring_gather(jnp.concatenate([v[:, :HALF1] for v in near], axis=0), True)

    def second_part(v):
        as_gate = jnp.concatenate([v[:, HALF1 : HALF1 + D], v[:, HALF1 + D :]], axis=0)
        return jnp.where(core == 0, as_gate, v[:, HALF1:].reshape(96, D))

    near2 = jnp.concatenate([second_part(v) for v in near], axis=0)
    own1, near2 = lax.optimization_barrier((own1, near2))
    other1 = [swap_core(v) for v in own1]
    own2 = ring_gather(near2, True)
    dma = pltpu.SemaphoreType.DMA

    hidden, turned, w1, conv_in, slope, xs, bc, dt_pre, acum, bcum = call(
        kernel_a,
        "forward_conv",
        [SM] + [VM] * 2 + [HB] * 8,
        [
            ((ROWS, D), BF16, HB),
            ((D, ROWS), BF16, HB),
            ((D, WIDE1), BF16, HB),
            ((SEQS, PADLEN, CONV_CH), F32, HB),
            ((ROWS, CONV_CH), F32, HB),
            ((ROWS, DI), BF16, HB),
            ((ROWS, 2 * DS), BF16, VM),
            ((ROWS, 128), F32, VM),
            ((ROWS, 128), F32, VM),
            ((ROWS, 128), F32, VM),
        ],
        [
            pltpu.VMEM((ROWS, D), BF16),
            pltpu.VMEM((D, ROWS), BF16),
            pltpu.VMEM((D, WIDE1), BF16),
            pltpu.VMEM((SEQS, PADLEN, CONV_CH), F32),
            pltpu.VMEM((ROWS, CONV_CH), F32),
            pltpu.VMEM((ROWS, DI), BF16),
            dma((2, 4, 4)),
            dma((3,)),
            dma((7, 4)),
        ],
        [pos, tokens, params] + own1 + other1,
        14,
    )
    other2 = [swap_core(v) for v in own2]
    (y,) = call(
        kernel_s,
        "forward_ssd",
        [VM, HB, VM, VM, VM],
        [((ROWS, DI), F32, HB)],
        [
            pltpu.VMEM((ROWS, DI), BF16),
            pltpu.VMEM((ROWS, DI), F32),
            pltpu.VMEM((LEN, LEN), F32),
            pltpu.VMEM((128, LEN), F32),
            dma((2,)),
            dma((2,)),
        ],
        [params, xs, bc, acum, bcum],
        9,
    )

    out, d_y, grads2, d_hid, normed, d_gate, g_gated = call(
        kernel_b,
        "gate_output",
        [SM, VM, VM, HB, HB, HB, VM] + [HB] * 8,
        [
            ((ROWS, D), BF16, HB),
            ((ROWS, DI), F32, HB),
            ((16, 96, D), BF16, HB),
            ((ROWS, D), F32, HB),
            ((ROWS, DI), BF16, HB),
            ((ROWS, DI), BF16, HB),
            ((1, DI), F32, VM),
        ],
        [
            pltpu.VMEM((ROWS, DI), F32),
            pltpu.VMEM((ROWS, D), BF16),
            pltpu.VMEM((ROWS, D), BF16),
            pltpu.VMEM((ROWS, D), BF16),
            pltpu.VMEM((ROWS, DI), F32),
            pltpu.VMEM((16, 96, D), BF16),
            pltpu.VMEM((ROWS, D), F32),
            pltpu.VMEM((2 * DI, D), BF16),
            pltpu.VMEM((ROWS, DI), F32),
            pltpu.VMEM((ROWS, DI), F32),
            pltpu.VMEM((ROWS, DI), BF16),
            pltpu.VMEM((ROWS, DI), BF16),
            pltpu.VMEM((ROWS, 128), F32),
            pltpu.VMEM((16, DI), F32),
            dma((2, 4, 4, 2)),
            dma((9,)),
        ],
        [pos, hidden, turned, y, tokens, cotangent, params] + own2 + other2,
        18,
    )

    got2 = swap_core(grads2)
    d_act, d_pre, g_skip, g_dt, g_alog = call(
        kernel_c,
        "backward_ssd",
        [HB, VM, VM, VM, VM, HB, HB, VM],
        [
            ((ROWS, CONV_CH), F32, HB),
            ((ROWS, 128), BF16, VM),
            ((1, 128), F32, VM),
            ((1, 128), F32, VM),
            ((1, 128), F32, VM),
        ],
        [
            pltpu.VMEM((ROWS, DI), BF16),
            pltpu.VMEM((ROWS, DI), F32),
            pltpu.VMEM((ROWS, DI), F32),
            pltpu.VMEM((ROWS, CONV_CH), F32),
            pltpu.VMEM((LEN, LEN), F32),
            pltpu.VMEM((128, LEN), F32),
            pltpu.VMEM((LEN, LEN), F32),
            pltpu.VMEM((LEN, 128), F32),
            pltpu.VMEM((LEN, 128), F32),
            dma((2, 3)),
            dma((2,)),
        ],
        [xs, bc, acum, bcum, dt_pre, d_y, y, params],
        14,
    )

    (sum2,) = call(
        kernel_f,
        "grad_gate_out",
        [SM, HB, HB, HB, HB, VM],
        [((16, 96, D), BF16, HB)],
        [
            pltpu.VMEM((D, ROWS), BF16),
            pltpu.VMEM((ROWS, D), BF16),
            pltpu.VMEM((ROWS, DI), BF16),
            pltpu.VMEM((16, 96, D), BF16),
            dma((3,)),
        ],
        [pos, turned, cotangent, d_gate, normed, got2],
    )
    before = sum2
    sum2 = lax.all_to_all(sum2, "fsdp", 0, 0, axis_index_groups=SIXTEENS)

    grads1, d_proj, g_conv_w, g_conv_b = call(
        kernel_e,
        "backward_conv",
        [SM, HB, VM, HB, HB, VM, VM, HB],
        [
            ((D, HALF1), BF16, HB),
            ((ROWS, WIDE1), BF16, HB),
            ((CONV, CONV_CH), F32, VM),
            ((1, CONV_CH), F32, VM),
        ],
        [
            pltpu.VMEM((ROWS, WIDE1), BF16),
            pltpu.VMEM((SEQS, PADLEN, CONV_CH), F32),
            pltpu.VMEM((SEQS, PADLEN, CONV_CH), F32),
            pltpu.VMEM((SEQS, PADLEN, CONV_CH), F32),
            pltpu.VMEM((D, HALF1), BF16),
            dma((7, 6)),
            dma((4,)),
            dma((8,)),
        ],
        [pos, d_act, d_pre, conv_in, slope, params, turned, before],
    )

    got1 = swap_core(grads1)
    grad_tokens, g_norm = call(
        kernel_d,
        "grad_tokens",
        [HB, HB, HB, HB, VM, HB],
        [((ROWS, D), F32, HB), ((1, D), F32, VM)],
        [
            pltpu.VMEM((ROWS, WIDE1), BF16),
            pltpu.VMEM((D, WIDE1), BF16),
            pltpu.VMEM((ROWS, D), F32),
            pltpu.VMEM((ROWS, D), BF16),
            pltpu.VMEM((ROWS, D), BF16),
            pltpu.VMEM((ROWS, D), F32),
            pltpu.VMEM((ROWS, D), F32),
            dma((5,)),
            dma((2,)),
        ],
        [d_proj, w1, d_hid, tokens, params, cotangent],
        8,
    )
    sum1 = call(
        kernel_g,
        "grad_conv_columns",
        [SM, VM, HB] + [VM] * 8 + [HB],
        [((208, HALF1), BF16, HB)] * 4,
        [
            pltpu.VMEM((4, 208, HALF1), BF16),
            pltpu.VMEM((ROWS, HALF1), BF16),
            pltpu.VMEM((16, HALF1), F32),
            dma,
            dma((4,)),
        ],
        [pos, turned, d_proj, got1, g_conv_w, g_conv_b, g_gated, g_norm]
        + [g_dt, g_alog, g_skip, sum2],
    )

    def ring(blocks, last):
        return [blocks[0]] + [
            lax.ppermute(blocks[r], "fsdp", ring_pairs(r, last)) for r in (1, 2, 3)
        ]

    sum1 = call(
        kernel_k, "ring_sums", [VM] * 4, [((64, HALF1), BF16, VM)] * 4, [], ring(sum1, True)
    )
    sum2 = jnp.sum(sum2.astype(F32), axis=0)
    as_gate = jnp.concatenate([sum2[:48], sum2[48:]], axis=1)
    sum2 = jnp.where(core == 0, as_gate, sum2.reshape(48, DI)).astype(BF16).reshape(8, 6, DI)
    sum2 = jnp.pad(sum2, ((0, 0), (0, 2), (0, 0))).reshape(64, DI)

    (both,) = call(
        kernel_l,
        "pieces_of_eight",
        [VM] * 5,
        [((64, DI + 3 * HALF1), BF16, VM)],
        [],
        ring(sum1, False) + [sum2],
    )
    both = lax.all_to_all(
        both.reshape(8, 8, DI + 3 * HALF1), "fsdp", 0, 0, axis_index_groups=EIGHTS
    ).reshape(64, DI + 3 * HALF1)
    return (out, grad_tokens) + tuple(
        call(
            kernel_h,
            "last_sums",
            [VM],
            [
                ((6 * NCOL,), F32, VM),
                ((6 * DI,), F32, VM),
                ((D,), F32, VM),
                ((CONV, CONV_CH), F32, VM),
                ((CONV_CH,), F32, VM),
                ((NH,), F32, VM),
                ((NH,), F32, VM),
                ((NH,), F32, VM),
                ((DI,), F32, VM),
            ],
            [pltpu.VMEM((8, DI + 2 * HALF1), F32)],
            [both],
        )
    )


def solution(mesh):
    rows = P("fsdp", None)
    flat = P("fsdp")
    same = P()
    return jax.shard_map(
        per_device,
        mesh=mesh,
        in_specs=(rows, flat, flat) + (same,) * 7 + (rows,),
        out_specs=(rows, rows, flat, flat) + (same,) * 7,
        check_vma=False,
    )
```

```python
import functools

import jax
import jax.numpy as jnp
from jax import lax
from jax.experimental import pallas as pl
from jax.experimental.pallas import tpu as pltpu
from jax.sharding import PartitionSpec as P

D = 768
NH = 24
DS = 128
HEAD = 64
CONV = 4
LEN = 256
DI = 1536
CONV_CH = 1792
NCOL = 3352
ROWS = 512
SEQS = 2
PADLEN = LEN + 8
HALF1 = 1024
WIDE1 = 2048
EPS = 1e-5
LOG2E = 1.4426950408889634
P_GAIN, P_CONV, P_BIAS, P_DT, P_RATE, P_SKIP, P_GATED, P_ROWS = 0, 1, 5, 6, 7, 8, 9, 16
LIMIT = 63 * 1024 * 1024
F32 = jnp.float32
BF16 = jnp.bfloat16
HIGHEST = lax.Precision.HIGHEST


def index_of(z, x, y, c):
    return ((z % 4 * 4 + x % 4) * 4 + y % 4) * 2 + c


def everyone():
    for z in range(4):
        for x in range(4):
            for y in range(4):
                for c in range(2):
                    yield z, x, y, c


def ring_pairs(shift, last):
    pairs = []
    for z, x, y, c in everyone():
        along_z = (c == 0) == last
        to = (z + shift, x, y, c) if along_z else (z, x + shift, y, c)
        pairs.append((index_of(z, x, y, c), index_of(*to)))
    return pairs


CORE_PAIRS = [(index_of(*p), index_of(*p[:3], 1 - p[3])) for p in everyone()]
SIXTEENS = [[k * 8 + j for k in range(16)] for j in range(8)]
EIGHTS = [[(z * 4 + x) * 8 + k for k in range(8)] for z in range(4) for x in range(4)]


def ring_gather(value, last):
    return [value] + [
        lax.ppermute(value, "fsdp", ring_pairs(shift, last)) for shift in (1, 2, 3)
    ]


def swap_core(value):
    return lax.ppermute(value, "fsdp", CORE_PAIRS)


def dot_nn(a, b):
    return jnp.dot(a, b, preferred_element_type=F32)


def dot_nt(a, b):
    return lax.dot_general(a, b, (((1,), (1,)), ((), ())), preferred_element_type=F32)


def dot_tn(a, b):
    return lax.dot_general(a, b, (((0,), (0,)), ((), ())), preferred_element_type=F32)


def dot_exact(a, b):
    return jnp.dot(a, b, preferred_element_type=F32, precision=HIGHEST)


def sigmoid(v):
    return 0.5 * jnp.tanh(0.5 * v) + 0.5


def softplus(v):
    e = jnp.exp(-jnp.abs(v))
    small = e * (1.0 - e * (0.5 - e * (1.0 / 3.0)))
    return jnp.maximum(v, 0.0) + jnp.where(e < 1e-3, small, jnp.log(1.0 + e))


def iota(shape, dim):
    return lax.broadcasted_iota(jnp.int32, shape, dim)


def source_zx(half, z0, x0, r3, r2):
    zr = jnp.where(half == 0, r3, r2)
    xr = jnp.where(half == 0, r2, r3)
    return lax.rem(z0 - zr + 4, 4) * 4 + lax.rem(x0 - xr + 4, 4)


def head_masks():
    lane = iota((1, 128), 1)
    first = jnp.where(lane < 64, 1.0, 0.0).astype(BF16)
    second = jnp.where(lane < 64, 0.0, 1.0).astype(BF16)
    return first, second


def kernel_a(
    ready, flush, pos, tokens, params,
    b0, b1, b2, b3, q0, q1, q2, q3,
    hidden_o, turned_o, w1_o, conv_in_o, slope_o, xs_o, bc, dt_pre, acum, bcum,
    hidden, turned, w1, conv_in, slope, xs, sems, out_sems, tile_sems,
):
    z0, x0, core = pos[0], pos[1], pos[2]
    copies = []
    for side, refs in enumerate(((b0, b1, b2, b3), (q0, q1, q2, q3))):
        half = core if side == 0 else 1 - core
        col = pl.multiple_of(half * HALF1, HALF1)
        for r3 in range(4):
            for r2 in range(4):
                row = pl.multiple_of(source_zx(half, z0, x0, r3, r2) * 48, 16)
                copies.append(
                    pltpu.make_async_copy(
                        refs[r3].at[pl.ds(r2 * 48, 48)],
                        w1.at[pl.ds(row, 48), pl.ds(col, HALF1)],
                        sems.at[side, r3, r2],
                    )
                )
    for copy in copies:
        copy.start()
    ready()
    gain = params[P_GAIN : P_GAIN + 1, :D]

    @pl.loop(0, ROWS // 64)
    def _(i):
        rows = pl.ds(pl.multiple_of(i * 64, 64), 64)
        t = tokens[rows].astype(F32)
        inv = lax.rsqrt(jnp.mean(t * t, axis=1, keepdims=True) + EPS)
        hidden[rows] = (t * inv * gain).astype(BF16)

    turned[...] = hidden[...].T
    for s in range(SEQS):
        conv_in[s, 0:8] = jnp.zeros((8, CONV_CH), F32)
    for copy in copies:
        copy.wait()
    outs = [
        pltpu.make_async_copy(hidden, hidden_o, out_sems.at[0]),
        pltpu.make_async_copy(w1, w1_o, out_sems.at[1]),
        pltpu.make_async_copy(turned, turned_o, out_sems.at[2]),
    ]
    for copy in outs:
        copy.start()

    def conv_tile(j, cols, emit):
        p = dot_nn(hidden[...], w1[:, cols])
        for s in range(SEQS):
            conv_in[s, 8:PADLEN, cols] = p[s * LEN : (s + 1) * LEN]
        w = params[P_CONV : P_CONV + CONV, cols]
        bias = params[P_BIAS : P_BIAS + 1, cols]
        for s in range(SEQS):

            @pl.loop(0, LEN // 32, unroll=8)
            def _(i):
                base = pl.multiple_of(i * 32, 32)
                near = conv_in[s, pl.ds(base, 40), cols]
                total = bias + w[0:1] * near[5:37]
                for k in range(1, CONV):
                    total = total + w[k : k + 1] * near[5 + k : 37 + k]
                sig = sigmoid(total)
                act = total * sig
                rows = pl.ds(pl.multiple_of(s * LEN + base, 32), 32)
                slope[rows, cols] = sig * (1.0 + total * (1.0 - sig))
                emit(rows, act.astype(BF16))

    def tile_puts(j, cols):
        puts = [
            pltpu.make_async_copy(conv_in.at[s, :, cols], conv_in_o.at[s, :, cols], tile_sems.at[j, s])
            for s in range(SEQS)
        ]
        return puts + [
            pltpu.make_async_copy(slope.at[:, cols], slope_o.at[:, cols], tile_sems.at[j, 2])
        ]

    def xs_put(j, cols):
        return pltpu.make_async_copy(xs.at[:, cols], xs_o.at[:, cols], tile_sems.at[j, 3])

    def emit_bc(rows, act):
        bc[rows] = act

    last = pl.ds(1536, 256)
    conv_tile(6, last, emit_bc)
    for put in tile_puts(6, last):
        put.start()

    pre = dot_nn(hidden[...], w1[:, CONV_CH : CONV_CH + 128]) + params[P_DT : P_DT + 1, :128]
    dt_pre[...] = pre
    step = softplus(pre)
    inc = step * params[P_RATE : P_RATE + 1, :128] * LOG2E
    log_step = jnp.log(jnp.maximum(step, 1e-37)) * LOG2E
    lower = jnp.where(iota((LEN, LEN), 0) >= iota((LEN, LEN), 1), 1.0, 0.0)
    for s in range(SEQS):
        rows = slice(s * LEN, (s + 1) * LEN)
        a = dot_exact(lower, inc[rows])
        acum[rows] = a
        bcum[rows] = a - log_step[rows]
    flush()

    @pl.loop(0, 6)
    def _(j):
        cols = pl.ds(pl.multiple_of(j * 256, 256), 256)

        def emit(rows, act):
            xs[rows, cols] = act

        conv_tile(j, cols, emit)
        for put in tile_puts(j, cols) + [xs_put(j, cols)]:
            put.start()

    @pl.loop(0, 6)
    def _(j):
        cols = pl.ds(pl.multiple_of(j * 256, 256), 256)
        for put in tile_puts(j, cols) + [xs_put(j, cols)]:
            put.wait()

    for put in tile_puts(6, last) + outs:
        put.wait()


def kernel_s(ready, flush, params, xs_i, bc, acum, bcum, y_o, xs, y, score, bcum_t, in_sems, out_sems):
    gets = [
        pltpu.make_async_copy(xs_i.at[pl.ds(s * LEN, LEN)], xs.at[pl.ds(s * LEN, LEN)], in_sems.at[s])
        for s in range(SEQS)
    ]
    for copy in gets:
        copy.start()
    below = iota((LEN, LEN), 0) >= iota((LEN, LEN), 1)
    mask0, mask1 = head_masks()
    outs = []
    ready()
    for s in range(SEQS):
        rows = slice(s * LEN, (s + 1) * LEN)
        a = acum[rows]
        bcum_t[...] = bcum[rows].T
        score[...] = jnp.where(below, dot_nt(bc[rows, DS:], bc[rows, :DS]), 0.0)
        gets[s].wait()

        @pl.loop(0, NH // 2, unroll=12)
        def _(p):
            lanes = pl.ds(pl.multiple_of(p * 128, 128), 128)
            x = xs[s * LEN : (s + 1) * LEN, lanes]
            turned = pltpu.roll(a, lax.rem(128 - 2 * p, 128), 1)
            top = jnp.zeros((128, 128), F32)
            low = jnp.zeros((128, 128), F32)
            for i, mask in enumerate((mask0, mask1)):
                col = turned[:, i : i + 1]
                row = bcum_t[pl.ds(2 * p + i, 1), :]
                xm = x * mask
                e0 = jnp.exp2(jnp.minimum(col[:128] - row[:, :128], 64.0))
                m0 = (e0 * score[:128, :128]).astype(BF16)
                top = top + dot_nn(m0, xm[:128])
                e1 = jnp.exp2(jnp.minimum(col[128:] - row, 64.0))
                m1 = (e1 * score[128:, :]).astype(BF16)
                low = low + dot_nn(m1, xm)
            skip = params[P_SKIP : P_SKIP + 1, lanes]
            y[s * LEN : s * LEN + 128, lanes] = top + skip * x[:128].astype(F32)
            y[s * LEN + 128 : (s + 1) * LEN, lanes] = low + skip * x[128:].astype(F32)

        span = pl.ds(s * LEN, LEN)
        outs.append(pltpu.make_async_copy(y.at[span], y_o.at[span], out_sems.at[s]))
        outs[-1].start()
    for copy in outs:
        copy.wait()


def nothing(t):
    return None


def store_gate(turned, big, dest, extra, before=nothing, after=nothing):
    for t in range(4):
        g = dot_nn(turned[t * 192 : (t + 1) * 192], big[...])
        before(t)
        for k in range(4):
            zx = t * 4 + k
            for lr in range(2):
                half = slice(lr * 48, lr * 48 + 48)
                part = g[k * 48 : k * 48 + 48, lr * D : (lr + 1) * D]
                if extra is not None:
                    part = part + extra[zx, half].astype(F32)
                dest[zx, half] = part.astype(BF16)
        after(t)


def store_out(small, big, dest, extra, before=nothing, after=nothing):
    for t in range(4):
        g = dot_tn(big[:, t * 384 : (t + 1) * 384], small[...])
        before(t)
        for k in range(4):
            part = g[k * 96 : (k + 1) * 96]
            if extra is not None:
                part = part + extra[t * 4 + k].astype(F32)
            dest[t * 4 + k] = part.astype(BF16)
        after(t)


def quarter(t):
    return pl.ds(t * 4, 4)


def kernel_b(
    ready, flush, pos, hidden, turned, y_i, tokens_i, cot_i, params,
    b0, b1, b2, b3, q0, q1, q2, q3,
    out_o, d_y_o, grads_o, d_hid_o, normed_o, d_gate_o, gain_grad,
    y, tokens, cot, out, d_y, grads, d_hid,
    weights, gate_in, d_normed, normed, d_gate, gate_inv, acc, sems, io_sems,
):
    core = pos[2]
    z0, x0 = pos[0], pos[1]
    copies = ([], [])
    for side, refs in enumerate(((b0, b1, b2, b3), (q0, q1, q2, q3))):
        half = core if side == 0 else 1 - core
        for r3 in range(4):
            for r2 in range(4):
                zx = source_zx(half, z0, x0, r3, r2)
                for lr in range(2):
                    row = jnp.where(half == 0, lr * D + zx * 48, DI + zx * 96 + lr * 48)
                    copies[side].append(
                        pltpu.make_async_copy(
                            refs[r3].at[pl.ds(r2 * 96 + lr * 48, 48)],
                            weights.at[pl.ds(pl.multiple_of(row, 16), 48)],
                            sems.at[side, r3, r2, lr],
                        )
                    )

    def each(side, act):
        @pl.when(core == side)
        def _():
            for copy in copies[0]:
                act(copy)

        @pl.when(core != side)
        def _():
            for copy in copies[1]:
                act(copy)

    get_y = pltpu.make_async_copy(y_i, y, io_sems.at[0])
    get_tokens = pltpu.make_async_copy(tokens_i, tokens, io_sems.at[1])
    get_cot = pltpu.make_async_copy(cot_i, cot, io_sems.at[2])
    put_out = pltpu.make_async_copy(out, out_o, io_sems.at[3])
    put_dy = pltpu.make_async_copy(d_y, d_y_o, io_sems.at[4])
    put_dhid = pltpu.make_async_copy(d_hid, d_hid_o, io_sems.at[5])
    each(0, lambda copy: copy.start())
    get_y.start()
    each(1, lambda copy: copy.start())
    get_tokens.start()
    get_cot.start()
    ready()
    gain = params[P_GATED : P_GATED + 1, :DI]
    each(0, lambda copy: copy.wait())

    @pl.loop(0, 3)
    def _(j):
        cols = pl.ds(pl.multiple_of(j * 256, 256), 256)
        right = pl.ds(pl.multiple_of(j * 256 + D, 256), 256)
        gate_in[:, cols] = dot_nn(hidden[...], weights[0:D, cols])
        gate_in[:, right] = dot_nn(hidden[...], weights[D:DI, cols])

    get_y.wait()

    @pl.loop(0, ROWS // 16, unroll=8)
    def _(i):
        rows = pl.ds(pl.multiple_of(i * 16, 16), 16)
        g = gate_in[rows]
        gated = y[rows] * (g * sigmoid(g))
        inv = lax.rsqrt(jnp.mean(gated * gated, axis=1, keepdims=True) + EPS)
        gate_inv[rows] = jnp.broadcast_to(inv, (16, 128))
        normed[rows] = (gated * inv * gain).astype(BF16)

    put_normed = pltpu.make_async_copy(normed, normed_o, io_sems.at[6])
    put_normed.start()
    each(1, lambda copy: copy.wait())
    get_tokens.wait()
    get_cot.wait()

    @pl.loop(0, 3)
    def _(j):
        cols = pl.ds(pl.multiple_of(j * 256, 256), 256)
        mixed = dot_nn(normed[...], weights[DI:, cols])
        out[:, cols] = (tokens[:, cols].astype(F32) + mixed).astype(BF16)

    put_out.start()

    @pl.loop(0, 6)
    def _(j):
        cols = pl.ds(pl.multiple_of(j * 256, 256), 256)
        d_normed[:, cols] = dot_nt(cot[...], weights[pl.ds(pl.multiple_of(j * 256 + DI, 256), 256)])

    acc[...] = jnp.zeros_like(acc)

    @pl.loop(0, ROWS // 16, unroll=8)
    def _(i):
        rows = pl.ds(pl.multiple_of(i * 16, 16), 16)
        g = gate_in[rows]
        sig = sigmoid(g)
        act = g * sig
        yv = y[rows]
        inv = gate_inv[rows][:, 0:1]
        gnorm = yv * act * inv
        dn = d_normed[rows]
        prod = dn * gnorm
        acc[...] += prod
        dgn = dn * gain
        mean = jnp.mean(dgn * gnorm, axis=1, keepdims=True)
        d_gated = inv * (dgn - gnorm * mean)
        d_y[rows] = d_gated * act
        d_gate[rows] = (d_gated * yv * (sig * (1.0 + g * (1.0 - sig)))).astype(BF16)

    put_dy.start()
    put_gate = pltpu.make_async_copy(d_gate, d_gate_o, io_sems.at[7])
    put_gate.start()
    gain_grad[...] = jnp.sum(acc[...], axis=0, keepdims=True)
    flush()

    def put_quarter(t):
        pltpu.make_async_copy(
            grads.at[quarter(t)], grads_o.at[quarter(t)], io_sems.at[8 + t]
        ).start()


    @pl.when(core == 0)
    def _():
        store_out(cot, normed, grads, None, after=put_quarter)

    @pl.when(core != 0)
    def _():
        store_gate(turned, d_gate, grads, None, after=put_quarter)

    put_grads = [
        pltpu.make_async_copy(grads.at[quarter(t)], grads_o.at[quarter(t)], io_sems.at[8 + t])
        for t in range(4)
    ]

    @pl.loop(0, 3)
    def _(j):
        cols = pl.ds(pl.multiple_of(j * 256, 256), 256)
        right = pl.ds(pl.multiple_of(j * 256 + D, 256), 256)
        d_hid[:, cols] = dot_nt(d_gate[:, :D], weights[cols]) + dot_nt(
            d_gate[:, D:], weights[right]
        )

    put_dhid.start()
    for copy in [put_out, put_dy, put_normed, put_gate, put_dhid] + put_grads:
        copy.wait()


def kernel_f(
    _, __, pos, turned_i, cot_i, d_gate, normed, got_i, total_o, turned, cot, big, got, total, sems
):
    core = pos[2]

    def more(t):
        return pltpu.make_async_copy(got_i.at[quarter(t)], got.at[quarter(t)], sems.at[2 + t])

    def put(t):
        return pltpu.make_async_copy(total.at[quarter(t)], total_o.at[quarter(t)], sems.at[6 + t])

    def run(small_i, small, big_i, store):
        gets = [
            pltpu.make_async_copy(small_i, small, sems.at[0]),
            pltpu.make_async_copy(big_i, big, sems.at[1]),
        ]
        for get in gets:
            get.start()
        for t in range(4):
            more(t).start()
        for get in gets:
            get.wait()
        store(small, big, total, got, lambda t: more(t).wait(), lambda t: put(t).start())

    @pl.when(core == 0)
    def _():
        run(turned_i, turned, d_gate, store_gate)

    @pl.when(core != 0)
    def _():
        run(cot_i, cot, normed, store_out)

    for t in range(4):
        put(t).wait()


def split_dot(v, pick):
    hi = v.astype(BF16)
    lo = (v - hi.astype(F32)).astype(BF16)
    return dot_nn(jnp.concatenate([hi, lo], axis=1), pick)


def kernel_c(
    ready, flush, pos, xs_i, bc, acum, bcum, dt_pre, d_y_i, y_i, params,
    conv_in_i, slope_i, wide_turned, _,
    grads_o, d_proj_o, g_conv_w, g_conv_b, g_skip, g_dt, g_alog,
    xs, d_y, y, d_act, score_t, acum_t, d_score, rsum, csum, in_sems,
    d_proj, slope, conv_in, grads, sems, out_sems, proj_sems,
):
    core = pos[2]
    later_gets = []
    for s in range(SEQS):
        later_gets.append(
            pltpu.make_async_copy(slope_i.at[pl.ds(s * LEN, LEN)], slope.at[s, 0:LEN], sems.at[s, 0])
        )
        later_gets.append(pltpu.make_async_copy(conv_in_i.at[s], conv_in.at[s], sems.at[s, 1]))
    gets = [
        [
            pltpu.make_async_copy(
                src.at[pl.ds(s * LEN, LEN)], dst.at[pl.ds(s * LEN, LEN)], in_sems.at[s, k]
            )
            for k, (src, dst) in enumerate(((xs_i, xs), (d_y_i, d_y), (y_i, y)))
        ]
        for s in range(SEQS)
    ]
    for copy in gets[0] + gets[1] + later_gets:
        copy.start()
    for s in range(SEQS):
        d_act[s, LEN:] = jnp.zeros((8, CONV_CH), F32)
        slope[s, LEN:] = jnp.zeros((8, CONV_CH), F32)
    d_proj[:, CONV_CH + 128 :] = jnp.zeros((ROWS, 128), BF16)
    above = iota((LEN, LEN), 0) <= iota((LEN, LEN), 1)
    upper = jnp.where(above, 1.0, 0.0)
    mask0, mask1 = head_masks()
    lane_head = iota((256, 128), 0) % 128 // 64
    head_col = iota((256, 128), 1)
    lane = iota((1, 128), 1)
    g_skip[...] = jnp.zeros_like(g_skip)
    g_dt[...] = jnp.zeros_like(g_dt)
    g_alog[...] = jnp.zeros_like(g_alog)
    ready()
    rate = params[P_RATE : P_RATE + 1, :128]
    for s in range(SEQS):
        rows = pl.ds(s * LEN, LEN)
        acum_t[...] = acum[rows].T
        score_t[...] = jnp.where(above, dot_nt(bc[rows, :DS], bc[rows, DS:]), 0.0)
        d_score[...] = jnp.zeros_like(d_score)
        rsum[...] = jnp.zeros_like(rsum)
        csum[...] = jnp.zeros_like(csum)
        b = bcum[rows]
        for copy in gets[s]:
            copy.wait()

        @pl.loop(0, NH // 2, unroll=12)
        def _(p):
            lanes = pl.ds(pl.multiple_of(p * 128, 128), 128)
            x = xs[rows, lanes]
            dy = d_y[rows, lanes]
            ds = dy.astype(BF16)
            turned = pltpu.roll(b, lax.rem(128 - 2 * p, 128), 1)
            top = jnp.zeros((128, 128), F32)
            low = jnp.zeros((128, 128), F32)
            grad0 = jnp.zeros((128, LEN), F32)
            grad1 = jnp.zeros((128, 128), F32)
            for i, mask in enumerate((mask0, mask1)):
                col = turned[:, i : i + 1]
                row = acum_t[pl.ds(2 * p + i, 1), :]
                dm = ds * mask
                xm = x * mask
                e0 = jnp.exp2(jnp.minimum(row - col[:128], 64.0))
                m0 = (e0 * score_t[:128, :]).astype(BF16)
                top = top + dot_nn(m0, dm)
                grad0 = grad0 + dot_nt(xm[:128], ds) * e0
                e1 = jnp.exp2(jnp.minimum(row[:, 128:] - col[128:], 64.0))
                m1 = (e1 * score_t[128:, 128:]).astype(BF16)
                low = low + dot_nn(m1, dm[128:])
                grad1 = grad1 + dot_nt(xm[128:], ds[128:]) * e1
            d_score[:128, :] += grad0
            d_score[128:, 128:] += grad1
            dxs = jnp.concatenate([top, low], axis=0)
            skip = params[P_SKIP : P_SKIP + 1, lanes]
            xf = x.astype(F32)
            own = ds.astype(F32) * (y[rows, lanes] - skip * xf)
            across = xf * dxs
            pick = jnp.where(lane_head + 2 * p == head_col, 1.0, 0.0).astype(BF16)
            rsum[...] += split_dot(own, pick)
            csum[...] += split_dot(across, pick)
            both = jnp.sum(dy * xf, axis=0, keepdims=True)
            first = jnp.sum(jnp.where(lane < 64, both, 0.0), axis=1, keepdims=True)
            second = jnp.sum(jnp.where(lane < 64, 0.0, both), axis=1, keepdims=True)
            g_skip[...] += jnp.where(lane == 2 * p, first, 0.0) + jnp.where(
                lane == 2 * p + 1, second, 0.0
            )
            d_act[s, 0:LEN, lanes] = skip * dy + dxs

        pre = dt_pre[rows]
        step = softplus(pre)
        sig = 1.0 / (1.0 + jnp.exp(-pre))
        ratio = jnp.where(pre < -20.0, 1.0, sig / jnp.maximum(step, 1e-30))
        d_cum = rsum[...] - csum[...]
        d_inc = dot_exact(upper, d_cum)
        g_alog[...] += jnp.sum(d_inc * step, axis=0, keepdims=True) * rate
        d_pre = csum[...] * ratio + d_inc * rate * sig
        g_dt[...] += jnp.sum(d_pre, axis=0, keepdims=True)
        d_proj[rows, CONV_CH : CONV_CH + 128] = d_pre.astype(BF16)
        dsc = jnp.where(above, d_score[...], 0.0).astype(BF16)
        d_act[s, 0:LEN, DI : DI + DS] = dot_nn(dsc, bc[rows, DS:])
        d_act[s, 0:LEN, DI + DS :] = dot_tn(dsc, bc[rows, :DS])

    for copy in later_gets:
        copy.wait()

    def put_tile(j):
        cols = pl.ds(pl.multiple_of(j * 256, 256), 256)
        return pltpu.make_async_copy(d_proj.at[:, cols], d_proj_o.at[:, cols], proj_sems.at[j])

    put_tile(7).start()

    @pl.loop(0, CONV_CH // 256)
    def _(j):
        cols = pl.ds(pl.multiple_of(j * 256, 256), 256)
        w = params[P_CONV : P_CONV + CONV, cols]
        zero = jnp.zeros((8, 256), F32)
        sums = (zero,) * (CONV + 1)
        for s in range(SEQS):

            def chunk(i, sums):
                base = pl.multiple_of(i * 32, 32)
                later = d_act[s, pl.ds(base, 40), cols] * slope[s, pl.ds(base, 40), cols]
                near = conv_in[s, pl.ds(base, 40), cols]
                here = later[0:32]
                back = w[CONV - 1 : CONV] * here
                for k in range(CONV - 1):
                    back = back + w[k : k + 1] * later[3 - k : 35 - k]
                d_proj[pl.ds(pl.multiple_of(s * LEN + base, 32), 32), cols] = back.astype(BF16)

                def fold(v):
                    return (v[0:8] + v[8:16]) + (v[16:24] + v[24:32])

                new = [sums[k] + fold(here * near[5 + k : 37 + k]) for k in range(CONV)]
                return tuple(new) + (sums[CONV] + fold(here),)

            sums = lax.fori_loop(0, LEN // 32, chunk, sums, unroll=8)
        for k in range(CONV):
            g_conv_w[k : k + 1, cols] = jnp.sum(sums[k], axis=0, keepdims=True)
        g_conv_b[:, cols] = jnp.sum(sums[CONV], axis=0, keepdims=True)
        put_tile(j).start()

    flush()

    def put_grads(j):
        cols = pl.ds(pl.multiple_of(j * 256, 256), 256)
        return pltpu.make_async_copy(grads.at[:, cols], grads_o.at[:, cols], out_sems.at[j])

    @pl.loop(0, 4)
    def _(j):
        cols = pl.ds(pl.multiple_of(j * 256, 256), 256)
        src = pl.ds(pl.multiple_of(j * 256 + (1 - core) * HALF1, 256), 256)
        grads[:, cols] = dot_nn(wide_turned[...], d_proj[:, src]).astype(BF16)
        put_grads(j).start()

    for j in range(8):
        put_tile(j).wait()
    for j in range(4):
        put_grads(j).wait()


def kernel_g(
    ready, _, pos, turned, d_proj_i, got, g_conv_w, g_conv_b, g_gated, g_norm,
    g_dt, g_alog, g_skip, out0, out1, out2, out3,
    total, d_proj, small, sem, out_sems,
):
    z0, x0, core = pos[0], pos[1], pos[2]
    src = pl.ds(pl.multiple_of(core * HALF1, HALF1), HALF1)
    get = pltpu.make_async_copy(d_proj_i.at[:, src], d_proj, sem)
    get.start()
    rest = CONV_CH - HALF1
    small[...] = jnp.zeros_like(small)
    ready()
    small[0:4] = g_conv_w[:, :HALF1]
    small[4:8, :rest] = g_conv_w[:, HALF1:]
    small[8:9] = g_conv_b[:, :HALF1]
    small[9:10, :rest] = g_conv_b[:, HALF1:]
    small[10:11] = g_gated[:, :HALF1]
    small[11:12, : DI - HALF1] = g_gated[:, HALF1:]
    small[12:13, :D] = g_norm[...]
    small[12:13, D : D + 128] = g_dt[...]
    small[12:13, D + 128 :] = g_alog[...]
    small[14:15, :128] = g_skip[...]
    for k in (12, 14):
        exact = small[k : k + 1]
        small[k + 1 : k + 2] = exact - exact.astype(BF16).astype(F32)
    sent = small[...].astype(BF16)
    for r3 in range(4):
        total[r3, 192:208] = sent
    get.wait()

    @pl.loop(0, 4)
    def _(j):
        cols = pl.ds(pl.multiple_of(j * 256, 256), 256)
        g = dot_nn(turned[...], d_proj[:, cols]) + got[:, cols].astype(F32)
        g = g.astype(BF16)
        for zx in range(16):
            dz = lax.rem(zx // 4 - z0 + 4, 4)
            dx = lax.rem(zx % 4 - x0 + 4, 4)
            r3 = jnp.where(core == 0, dz, dx)
            r2 = jnp.where(core == 0, dx, dz)
            rows = pl.ds(pl.multiple_of(r2 * 48, 16), 48)
            total[r3, rows, cols] = g[zx * 48 : zx * 48 + 48]

    puts = [
        pltpu.make_async_copy(total.at[r], out, out_sems.at[r])
        for r, out in enumerate((out0, out1, out2, out3))
    ]
    for put in puts:
        put.start()
    for put in puts:
        put.wait()


def sum_of_four(a, b, c, d):
    return (a[...].astype(F32) + c[...].astype(F32)) + (b[...].astype(F32) + d[...].astype(F32))


def kernel_k(ready, flush, own, got1, got2, got3, _, *outs):
    ready()
    total = sum_of_four(own, got1, got2, got3).astype(BF16)
    for r2, out in enumerate(outs):
        out[0:48] = total[r2 * 48 : r2 * 48 + 48]
        out[48:64] = total[192:208]
    flush()


def kernel_l(ready, flush, own, got1, got2, got3, two, out):
    ready()
    total = sum_of_four(own, got1, got2, got3)
    rides = jnp.concatenate([total[48:56], total[56:64]], axis=1).astype(BF16)
    zero = jnp.zeros((2, HALF1), F32)
    for d in range(8):
        eight = slice(d * 8, d * 8 + 8)
        out[eight, :DI] = two[eight]
        piece = jnp.concatenate([total[d * 6 : d * 6 + 6], zero], axis=0)
        out[eight, DI : DI + HALF1] = piece.astype(BF16)
        out[eight, DI + HALF1 :] = rides
    flush()


def kernel_d(
    ready, flush, d_proj_i, w1_i, d_hid_i, tokens_i, params, cot_i, grad_tokens_o, gain_grad,
    d_proj, w1, d_hid, tokens, cot, d_full, grad_tokens, sems, out_sems,
):
    gets = [
        pltpu.make_async_copy(src, dst, sems.at[k])
        for k, (src, dst) in enumerate(
            (
                (d_proj_i, d_proj),
                (w1_i.at[0:256], w1.at[0:256]),
                (w1_i.at[256:512], w1.at[256:512]),
                (w1_i.at[512:768], w1.at[512:768]),
                (d_hid_i, d_hid), (tokens_i, tokens), (cot_i, cot),
            )
        )
    ]
    for copy in gets:
        copy.start()
    gets[0].wait()
    for j in range(3):
        cols = slice(j * 256, (j + 1) * 256)
        gets[1 + j].wait()
        d_full[:, cols] = dot_nt(d_proj[...], w1[cols])

    for copy in gets[4:]:
        copy.wait()
    ready()
    gain = params[P_GAIN : P_GAIN + 1, :D]

    def chunk(i, total):
        rows = pl.ds(pl.multiple_of(i * 32, 32), 32)
        t = tokens[rows].astype(F32)
        inv = lax.rsqrt(jnp.mean(t * t, axis=1, keepdims=True) + EPS)
        normal = t * inv
        dh = d_full[rows] + d_hid[rows]
        prod = dh * normal
        dn = dh * gain
        mean = jnp.mean(dn * normal, axis=1, keepdims=True)
        grad_tokens[rows] = cot[rows].astype(F32) + inv * (dn - normal * mean)
        return total + (prod[0:8] + prod[8:16]) + (prod[16:24] + prod[24:32])

    total = jnp.zeros((8, D), F32)
    puts = []
    for s in range(SEQS):
        total = lax.fori_loop(s * LEN // 32, (s + 1) * LEN // 32, chunk, total, unroll=4)
        span = pl.ds(s * LEN, LEN)
        puts.append(
            pltpu.make_async_copy(grad_tokens.at[span], grad_tokens_o.at[span], out_sems.at[s])
        )
        puts[-1].start()
    gain_grad[...] = jnp.sum(total, axis=0, keepdims=True)
    flush()
    for put in puts:
        put.wait()


def kernel_h(
    ready, flush, got, g_in, g_out, g_norm, g_conv_w, g_conv_b, g_dt, g_alog, g_skip, g_gated, rows,
):
    def added(core, start, size):
        parts = [
            got[16 * y + 8 * core : 16 * y + 8 * core + 8, start : start + size].astype(F32)
            for y in range(4)
        ]
        return (parts[0] + parts[1]) + (parts[2] + parts[3])

    ready()
    rows[:, :DI] = added(0, 0, DI)
    rows[:, DI : DI + HALF1] = added(0, DI, HALF1)
    rows[:, DI + HALF1 :] = added(1, DI, HALF1)
    outs = added(1, 0, DI)
    for r in range(6):
        g_in[pl.ds(r * NCOL, NCOL)] = rows[r : r + 1, :NCOL].reshape(NCOL)
        g_out[pl.ds(r * DI, DI)] = outs[r : r + 1].reshape(DI)
    base = DI + HALF1
    top = added(0, base, HALF1) + added(1, base, HALF1)
    low = added(0, base + HALF1, HALF1) + added(1, base + HALF1, HALF1)
    rest = CONV_CH - HALF1
    g_conv_w[:, :HALF1] = top[0:4]
    g_conv_w[:, HALF1:] = top[4:8, :rest]
    g_conv_b[...] = jnp.concatenate([low[0:1], low[1:2, :rest]], axis=1).reshape(CONV_CH)
    g_gated[...] = jnp.concatenate([low[2:3], low[3:4, : DI - HALF1]], axis=1).reshape(DI)
    exact = low[4:5] + low[5:6]
    skip = low[6:7, :128] + low[7:8, :128]
    g_norm[...] = exact[:, :D].reshape(D)
    g_dt[...] = exact[0, D : D + NH]
    g_alog[...] = exact[0, D + 128 : D + 128 + NH]
    g_skip[...] = skip[0, :NH]
    flush()


VM = pl.BlockSpec(memory_space=pltpu.VMEM)
SM = pl.BlockSpec(memory_space=pltpu.SMEM)
HB = pl.BlockSpec(memory_space=pl.ANY)


def call(kernel, name, ins, outs, scratch, args, us=0.01):
    taken = [k for k, spec in enumerate(ins) if spec is VM]
    given = [k for k, out in enumerate(outs) if out[2] is VM]
    n_in, n_out, n_scratch = len(ins), len(outs), len(scratch)

    def body(*refs):
        in_refs = list(refs[:n_in])
        out_refs = list(refs[n_in : n_in + n_out])
        own = refs[n_in + n_out : n_in + n_out + n_scratch]
        rest = refs[n_in + n_out + n_scratch :]
        in_bufs, rest = rest[: len(taken)], rest[len(taken) :]
        out_bufs, rest = rest[: len(given)], rest[len(given) :]
        gets, puts = [], []
        for n, k in enumerate(taken):
            gets.append(pltpu.make_async_copy(in_refs[k], in_bufs[n], rest[0].at[n]))
            in_refs[k] = in_bufs[n]
        for n, k in enumerate(given):
            puts.append(pltpu.make_async_copy(out_bufs[n], out_refs[k], rest[1].at[n]))
            out_refs[k] = out_bufs[n]
        for copy in gets:
            copy.start()

        def ready():
            for copy in gets:
                copy.wait()

        def flush():
            for copy in puts:
                copy.start()

        kernel(ready, flush, *in_refs, *out_refs, *own)
        for copy in puts:
            copy.wait()

    dma = pltpu.SemaphoreType.DMA
    extra = [pltpu.VMEM(args[k].shape, args[k].dtype) for k in taken]
    extra += [pltpu.VMEM(outs[k][0], outs[k][1]) for k in given]
    extra += [dma((max(len(taken), 1),)), dma((max(len(given), 1),))]
    return pl.pallas_call(
        body,
        name=name,
        in_specs=[HB if spec is VM else spec for spec in ins],
        out_specs=[HB] * n_out,
        out_shape=[jax.ShapeDtypeStruct(o[0], o[1]) for o in outs],
        scratch_shapes=list(scratch) + extra,
        compiler_params=pltpu.CompilerParams(vmem_limit_bytes=LIMIT),
        cost_estimate=pl.CostEstimate(
            flops=int(us * 1.1e9), bytes_accessed=100_000, transcendentals=0
        ),
    )(*args)


def per_device(
    tokens,
    in_weight,
    out_weight,
    norm_gain,
    conv_weight,
    conv_bias,
    dt_bias,
    a_log,
    d_skip,
    gated_gain,
    cotangent,
):
    me = lax.axis_index("fsdp")
    core = lax.rem(me, 2)
    pos = jnp.stack([me // 32, lax.rem(me // 8, 4), core]).astype(jnp.int32)

    win = in_weight.reshape(6, NCOL)
    conv_cols = jnp.pad(win[:, DI:], ((0, 0), (0, WIDE1 - (NCOL - DI))))
    halves = jnp.stack(
        [
            jnp.concatenate([conv_cols[:, :HALF1], win[:, :DI]], axis=1),
            jnp.concatenate([conv_cols[:, HALF1:], out_weight.reshape(6, DI)], axis=1),
        ]
    )
    sent = jnp.broadcast_to(halves[None], (4, 2, 6, HALF1 + DI)).reshape(8, 6, HALF1 + DI)
    eight = lax.all_to_all(sent, "fsdp", 0, 0, axis_index_groups=EIGHTS)

    def row(v):
        return jnp.pad(v, (0, CONV_CH - v.shape[0]))[None]

    params = jnp.concatenate(
        [
            row(norm_gain), conv_weight, row(conv_bias), row(dt_bias), row(-jnp.exp(a_log)),
            row(jnp.repeat(d_skip, HEAD)), row(gated_gain),
            jnp.zeros((P_ROWS - P_GATED - 1, CONV_CH), F32),
        ],
        axis=0,
    )
    eight, params, pos = lax.optimization_barrier((eight, params, pos))
    near = ring_gather(eight.reshape(48, HALF1 + DI), False)
    own1 = ring_gather(jnp.concatenate([v[:, :HALF1] for v in near], axis=0), True)

    def second_part(v):
        as_gate = jnp.concatenate([v[:, HALF1 : HALF1 + D], v[:, HALF1 + D :]], axis=0)
        return jnp.where(core == 0, as_gate, v[:, HALF1:].reshape(96, D))

    near2 = jnp.concatenate([second_part(v) for v in near], axis=0)
    own1, near2 = lax.optimization_barrier((own1, near2))
    other1 = [swap_core(v) for v in own1]
    own2 = ring_gather(near2, True)
    dma = pltpu.SemaphoreType.DMA

    hidden, turned, w1, conv_in, slope, xs, bc, dt_pre, acum, bcum = call(
        kernel_a,
        "forward_conv",
        [SM] + [VM] * 2 + [HB] * 8,
        [
            ((ROWS, D), BF16, HB),
            ((D, ROWS), BF16, HB),
            ((D, WIDE1), BF16, HB),
            ((SEQS, PADLEN, CONV_CH), F32, HB),
            ((ROWS, CONV_CH), F32, HB),
            ((ROWS, DI), BF16, HB),
            ((ROWS, 2 * DS), BF16, VM),
            ((ROWS, 128), F32, VM),
            ((ROWS, 128), F32, VM),
            ((ROWS, 128), F32, VM),
        ],
        [
            pltpu.VMEM((ROWS, D), BF16),
            pltpu.VMEM((D, ROWS), BF16),
            pltpu.VMEM((D, WIDE1), BF16),
            pltpu.VMEM((SEQS, PADLEN, CONV_CH), F32),
            pltpu.VMEM((ROWS, CONV_CH), F32),
            pltpu.VMEM((ROWS, DI), BF16),
            dma((2, 4, 4)),
            dma((3,)),
            dma((7, 4)),
        ],
        [pos, tokens, params] + own1 + other1,
        14,
    )
    other2 = [swap_core(v) for v in own2]
    (y,) = call(
        kernel_s,
        "forward_ssd",
        [VM, HB, VM, VM, VM],
        [((ROWS, DI), F32, HB)],
        [
            pltpu.VMEM((ROWS, DI), BF16),
            pltpu.VMEM((ROWS, DI), F32),
            pltpu.VMEM((LEN, LEN), F32),
            pltpu.VMEM((128, LEN), F32),
            dma((2,)),
            dma((2,)),
        ],
        [params, xs, bc, acum, bcum],
        9,
    )

    out, d_y, grads2, d_hid, normed, d_gate, g_gated = call(
        kernel_b,
        "gate_output",
        [SM, VM, VM, HB, HB, HB, VM] + [HB] * 8,
        [
            ((ROWS, D), BF16, HB),
            ((ROWS, DI), F32, HB),
            ((16, 96, D), BF16, HB),
            ((ROWS, D), F32, HB),
            ((ROWS, DI), BF16, HB),
            ((ROWS, DI), BF16, HB),
            ((1, DI), F32, VM),
        ],
        [
            pltpu.VMEM((ROWS, DI), F32),
            pltpu.VMEM((ROWS, D), BF16),
            pltpu.VMEM((ROWS, D), BF16),
            pltpu.VMEM((ROWS, D), BF16),
            pltpu.VMEM((ROWS, DI), F32),
            pltpu.VMEM((16, 96, D), BF16),
            pltpu.VMEM((ROWS, D), F32),
            pltpu.VMEM((2 * DI, D), BF16),
            pltpu.VMEM((ROWS, DI), F32),
            pltpu.VMEM((ROWS, DI), F32),
            pltpu.VMEM((ROWS, DI), BF16),
            pltpu.VMEM((ROWS, DI), BF16),
            pltpu.VMEM((ROWS, 128), F32),
            pltpu.VMEM((16, DI), F32),
            dma((2, 4, 4, 2)),
            dma((12,)),
        ],
        [pos, hidden, turned, y, tokens, cotangent, params] + own2 + other2,
        18,
    )

    got2 = swap_core(grads2)

    (sum2,) = call(
        kernel_f,
        "grad_gate_out",
        [SM, HB, HB, HB, HB, HB],
        [((16, 96, D), BF16, HB)],
        [
            pltpu.VMEM((D, ROWS), BF16),
            pltpu.VMEM((ROWS, D), BF16),
            pltpu.VMEM((ROWS, DI), BF16),
            pltpu.VMEM((16, 96, D), BF16),
            pltpu.VMEM((16, 96, D), BF16),
            dma((10,)),
        ],
        [pos, turned, cotangent, d_gate, normed, got2],
    )
    before = sum2
    sum2 = lax.all_to_all(sum2, "fsdp", 0, 0, axis_index_groups=SIXTEENS)

    grads1, d_proj, g_conv_w, g_conv_b, g_skip, g_dt, g_alog = call(
        kernel_c,
        "backward_ssd_conv",
        [SM, HB, VM, VM, VM, VM, HB, HB, VM, HB, HB, VM, HB],
        [
            ((D, HALF1), BF16, HB),
            ((ROWS, WIDE1), BF16, HB),
            ((CONV, CONV_CH), F32, VM),
            ((1, CONV_CH), F32, VM),
            ((1, 128), F32, VM),
            ((1, 128), F32, VM),
            ((1, 128), F32, VM),
        ],
        [
            pltpu.VMEM((ROWS, DI), BF16),
            pltpu.VMEM((ROWS, DI), F32),
            pltpu.VMEM((ROWS, DI), F32),
            pltpu.VMEM((SEQS, PADLEN, CONV_CH), F32),
            pltpu.VMEM((LEN, LEN), F32),
            pltpu.VMEM((128, LEN), F32),
            pltpu.VMEM((LEN, LEN), F32),
            pltpu.VMEM((LEN, 128), F32),
            pltpu.VMEM((LEN, 128), F32),
            dma((2, 3)),
            pltpu.VMEM((ROWS, WIDE1), BF16),
            pltpu.VMEM((SEQS, PADLEN, CONV_CH), F32),
            pltpu.VMEM((SEQS, PADLEN, CONV_CH), F32),
            pltpu.VMEM((D, HALF1), BF16),
            dma((2, 2)),
            dma((4,)),
            dma((8,)),
        ],
        [pos, xs, bc, acum, bcum, dt_pre, d_y, y, params, conv_in, slope, turned, before],
    )

    got1 = swap_core(grads1)
    grad_tokens, g_norm = call(
        kernel_d,
        "grad_tokens",
        [HB, HB, HB, HB, VM, HB],
        [((ROWS, D), F32, HB), ((1, D), F32, VM)],
        [
            pltpu.VMEM((ROWS, WIDE1), BF16),
            pltpu.VMEM((D, WIDE1), BF16),
            pltpu.VMEM((ROWS, D), F32),
            pltpu.VMEM((ROWS, D), BF16),
            pltpu.VMEM((ROWS, D), BF16),
            pltpu.VMEM((ROWS, D), F32),
            pltpu.VMEM((ROWS, D), F32),
            dma((7,)),
            dma((2,)),
        ],
        [d_proj, w1, d_hid, tokens, params, cotangent],
    )
    sum1 = call(
        kernel_g,
        "grad_conv_columns",
        [SM, VM, HB] + [VM] * 8,
        [((208, HALF1), BF16, HB)] * 4,
        [
            pltpu.VMEM((4, 208, HALF1), BF16),
            pltpu.VMEM((ROWS, HALF1), BF16),
            pltpu.VMEM((16, HALF1), F32),
            dma,
            dma((4,)),
        ],
        [pos, turned, d_proj, got1, g_conv_w, g_conv_b, g_gated, g_norm]
        + [g_dt, g_alog, g_skip],
    )

    def ring(blocks, last):
        return [blocks[0]] + [
            lax.ppermute(blocks[r], "fsdp", ring_pairs(r, last)) for r in (1, 2, 3)
        ]

    sum1 = call(
        kernel_k,
        "ring_sums",
        [VM] * 4 + [HB],
        [((64, HALF1), BF16, VM)] * 4,
        [],
        ring(sum1, True) + [sum2],
    )
    sum2 = jnp.sum(sum2.astype(F32), axis=0)
    as_gate = jnp.concatenate([sum2[:48], sum2[48:]], axis=1)
    sum2 = jnp.where(core == 0, as_gate, sum2.reshape(48, DI)).astype(BF16).reshape(8, 6, DI)
    sum2 = jnp.pad(sum2, ((0, 0), (0, 2), (0, 0))).reshape(64, DI)

    (both,) = call(
        kernel_l,
        "pieces_of_eight",
        [VM] * 5,
        [((64, DI + 3 * HALF1), BF16, VM)],
        [],
        ring(sum1, False) + [sum2],
    )
    both = lax.all_to_all(
        both.reshape(8, 8, DI + 3 * HALF1), "fsdp", 0, 0, axis_index_groups=EIGHTS
    ).reshape(64, DI + 3 * HALF1)
    return (out, grad_tokens) + tuple(
        call(
            kernel_h,
            "last_sums",
            [VM],
            [
                ((6 * NCOL,), F32, VM),
                ((6 * DI,), F32, VM),
                ((D,), F32, VM),
                ((CONV, CONV_CH), F32, VM),
                ((CONV_CH,), F32, VM),
                ((NH,), F32, VM),
                ((NH,), F32, VM),
                ((NH,), F32, VM),
                ((DI,), F32, VM),
            ],
            [pltpu.VMEM((8, DI + 2 * HALF1), F32)],
            [both],
        )
    )


def solution(mesh):
    rows = P("fsdp", None)
    flat = P("fsdp")
    same = P()
    return jax.shard_map(
        per_device,
        mesh=mesh,
        in_specs=(rows, flat, flat) + (same,) * 7 + (rows,),
        out_specs=(rows, rows, flat, flat) + (same,) * 7,
        check_vma=False,
    )
```

```python
import functools

import jax
import jax.numpy as jnp
from jax import lax
from jax.experimental import pallas as pl
from jax.experimental.pallas import tpu as pltpu
from jax.sharding import PartitionSpec as P

D = 768
NH = 24
DS = 128
HEAD = 64
CONV = 4
LEN = 256
DI = 1536
CONV_CH = 1792
NCOL = 3352
ROWS = 512
SEQS = 2
PADLEN = LEN + 8
HALF1 = 1024
WIDE1 = 2048
EPS = 1e-5
LOG2E = 1.4426950408889634
P_GAIN, P_CONV, P_BIAS, P_DT, P_RATE, P_SKIP, P_GATED, P_ROWS = 0, 1, 5, 6, 7, 8, 9, 16
LIMIT = 63 * 1024 * 1024
F32 = jnp.float32
BF16 = jnp.bfloat16
HIGHEST = lax.Precision.HIGHEST


def index_of(z, x, y, c):
    return ((z % 4 * 4 + x % 4) * 4 + y % 4) * 2 + c


def everyone():
    for z in range(4):
        for x in range(4):
            for y in range(4):
                for c in range(2):
                    yield z, x, y, c


def ring_pairs(shift, last):
    pairs = []
    for z, x, y, c in everyone():
        along_z = (c == 0) == last
        to = (z + shift, x, y, c) if along_z else (z, x + shift, y, c)
        pairs.append((index_of(z, x, y, c), index_of(*to)))
    return pairs


CORE_PAIRS = [(index_of(*p), index_of(*p[:3], 1 - p[3])) for p in everyone()]
SIXTEENS = [[k * 8 + j for k in range(16)] for j in range(8)]
EIGHTS = [[(z * 4 + x) * 8 + k for k in range(8)] for z in range(4) for x in range(4)]


def ring_gather(value, last):
    return [value] + [
        lax.ppermute(value, "fsdp", ring_pairs(shift, last)) for shift in (1, 2, 3)
    ]


def swap_core(value):
    return lax.ppermute(value, "fsdp", CORE_PAIRS)


def dot_nn(a, b):
    return jnp.dot(a, b, preferred_element_type=F32)


def dot_nt(a, b):
    return lax.dot_general(a, b, (((1,), (1,)), ((), ())), preferred_element_type=F32)


def dot_tn(a, b):
    return lax.dot_general(a, b, (((0,), (0,)), ((), ())), preferred_element_type=F32)


def dot_exact(a, b):
    return jnp.dot(a, b, preferred_element_type=F32, precision=HIGHEST)


def sigmoid(v):
    return 0.5 * jnp.tanh(0.5 * v) + 0.5


def softplus(v):
    e = jnp.exp(-jnp.abs(v))
    small = e * (1.0 - e * (0.5 - e * (1.0 / 3.0)))
    return jnp.maximum(v, 0.0) + jnp.where(e < 1e-3, small, jnp.log(1.0 + e))


def iota(shape, dim):
    return lax.broadcasted_iota(jnp.int32, shape, dim)


def source_zx(half, z0, x0, r3, r2):
    zr = jnp.where(half == 0, r3, r2)
    xr = jnp.where(half == 0, r2, r3)
    return lax.rem(z0 - zr + 4, 4) * 4 + lax.rem(x0 - xr + 4, 4)


def head_masks():
    lane = iota((1, 128), 1)
    first = jnp.where(lane < 64, 1.0, 0.0).astype(BF16)
    second = jnp.where(lane < 64, 0.0, 1.0).astype(BF16)
    return first, second


def kernel_a(
    ready, flush, pos, tokens, params,
    b0, b1, b2, b3, q0, q1, q2, q3,
    hidden_o, turned_o, w1_o, conv_in_o, slope_o, xs_o, bc, dt_pre, acum, bcum,
    hidden, turned, w1, conv_in, slope, xs, sems, out_sems, tile_sems,
):
    z0, x0, core = pos[0], pos[1], pos[2]
    copies = []
    for side, refs in enumerate(((b0, b1, b2, b3), (q0, q1, q2, q3))):
        half = core if side == 0 else 1 - core
        col = pl.multiple_of(half * HALF1, HALF1)
        for r3 in range(4):
            for r2 in range(4):
                row = pl.multiple_of(source_zx(half, z0, x0, r3, r2) * 48, 16)
                copies.append(
                    pltpu.make_async_copy(
                        refs[r3].at[pl.ds(r2 * 48, 48)],
                        w1.at[pl.ds(row, 48), pl.ds(col, HALF1)],
                        sems.at[side, r3, r2],
                    )
                )
    for copy in copies:
        copy.start()
    ready()
    gain = params[P_GAIN : P_GAIN + 1, :D]

    @pl.loop(0, ROWS // 64, unroll=4)
    def _(i):
        rows = pl.ds(pl.multiple_of(i * 64, 64), 64)
        t = tokens[rows].astype(F32)
        inv = lax.rsqrt(jnp.mean(t * t, axis=1, keepdims=True) + EPS)
        hidden[rows] = (t * inv * gain).astype(BF16)

    turned[...] = hidden[...].T
    for s in range(SEQS):
        conv_in[s, 0:8] = jnp.zeros((8, CONV_CH), F32)
    for copy in copies:
        copy.wait()
    outs = [
        pltpu.make_async_copy(hidden, hidden_o, out_sems.at[0]),
        pltpu.make_async_copy(w1, w1_o, out_sems.at[1]),
        pltpu.make_async_copy(turned, turned_o, out_sems.at[2]),
    ]
    for copy in outs:
        copy.start()

    def conv_tile(j, cols, emit):
        p = dot_nn(hidden[...], w1[:, cols])
        for s in range(SEQS):
            conv_in[s, 8:PADLEN, cols] = p[s * LEN : (s + 1) * LEN]
        w = params[P_CONV : P_CONV + CONV, cols]
        bias = params[P_BIAS : P_BIAS + 1, cols]
        for s in range(SEQS):

            @pl.loop(0, LEN // 32, unroll=8)
            def _(i):
                base = pl.multiple_of(i * 32, 32)
                near = conv_in[s, pl.ds(base, 40), cols]
                total = bias + w[0:1] * near[5:37]
                for k in range(1, CONV):
                    total = total + w[k : k + 1] * near[5 + k : 37 + k]
                sig = sigmoid(total)
                act = total * sig
                rows = pl.ds(pl.multiple_of(s * LEN + base, 32), 32)
                slope[rows, cols] = sig * (1.0 + total * (1.0 - sig))
                emit(rows, act.astype(BF16))

    def tile_puts(j, cols):
        puts = [
            pltpu.make_async_copy(conv_in.at[s, :, cols], conv_in_o.at[s, :, cols], tile_sems.at[j, s])
            for s in range(SEQS)
        ]
        return puts + [
            pltpu.make_async_copy(slope.at[:, cols], slope_o.at[:, cols], tile_sems.at[j, 2])
        ]

    def xs_put(j, cols):
        return pltpu.make_async_copy(xs.at[:, cols], xs_o.at[:, cols], tile_sems.at[j, 3])

    def emit_bc(rows, act):
        bc[rows] = act

    last = pl.ds(1536, 256)
    conv_tile(6, last, emit_bc)
    for put in tile_puts(6, last):
        put.start()

    pre = dot_nn(hidden[...], w1[:, CONV_CH : CONV_CH + 128]) + params[P_DT : P_DT + 1, :128]
    dt_pre[...] = pre
    step = softplus(pre)
    inc = step * params[P_RATE : P_RATE + 1, :128] * LOG2E
    log_step = jnp.log(jnp.maximum(step, 1e-37)) * LOG2E
    lower = jnp.where(iota((LEN, LEN), 0) >= iota((LEN, LEN), 1), 1.0, 0.0)
    for s in range(SEQS):
        rows = slice(s * LEN, (s + 1) * LEN)
        a = dot_exact(lower, inc[rows])
        acum[rows] = a
        bcum[rows] = a - log_step[rows]
    flush()

    @pl.loop(0, 6, unroll=2)
    def _(j):
        cols = pl.ds(pl.multiple_of(j * 256, 256), 256)

        def emit(rows, act):
            xs[rows, cols] = act

        conv_tile(j, cols, emit)
        for put in tile_puts(j, cols) + [xs_put(j, cols)]:
            put.start()

    @pl.loop(0, 6)
    def _(j):
        cols = pl.ds(pl.multiple_of(j * 256, 256), 256)
        for put in tile_puts(j, cols) + [xs_put(j, cols)]:
            put.wait()

    for put in tile_puts(6, last) + outs:
        put.wait()


def kernel_s(ready, flush, params, xs_i, bc, acum, bcum, y_o, xs, y, score, bcum_t, in_sems, out_sems):
    gets = [
        pltpu.make_async_copy(xs_i.at[pl.ds(s * LEN, LEN)], xs.at[pl.ds(s * LEN, LEN)], in_sems.at[s])
        for s in range(SEQS)
    ]
    for copy in gets:
        copy.start()
    below = iota((LEN, LEN), 0) >= iota((LEN, LEN), 1)
    mask0, mask1 = head_masks()
    outs = []
    ready()
    for s in range(SEQS):
        rows = slice(s * LEN, (s + 1) * LEN)
        a = acum[rows]
        bcum_t[...] = bcum[rows].T
        score[...] = jnp.where(below, dot_nt(bc[rows, DS:], bc[rows, :DS]), 0.0)
        gets[s].wait()

        @pl.loop(0, NH // 2, unroll=12)
        def _(p):
            lanes = pl.ds(pl.multiple_of(p * 128, 128), 128)
            x = xs[s * LEN : (s + 1) * LEN, lanes]
            turned = pltpu.roll(a, lax.rem(128 - 2 * p, 128), 1)
            top = jnp.zeros((128, 128), F32)
            low = jnp.zeros((128, 128), F32)
            for i, mask in enumerate((mask0, mask1)):
                col = turned[:, i : i + 1]
                row = bcum_t[pl.ds(2 * p + i, 1), :]
                xm = x * mask
                e0 = jnp.exp2(jnp.minimum(col[:128] - row[:, :128], 64.0))
                m0 = (e0 * score[:128, :128]).astype(BF16)
                top = top + dot_nn(m0, xm[:128])
                e1 = jnp.exp2(jnp.minimum(col[128:] - row, 64.0))
                m1 = (e1 * score[128:, :]).astype(BF16)
                low = low + dot_nn(m1, xm)
            skip = params[P_SKIP : P_SKIP + 1, lanes]
            y[s * LEN : s * LEN + 128, lanes] = top + skip * x[:128].astype(F32)
            y[s * LEN + 128 : (s + 1) * LEN, lanes] = low + skip * x[128:].astype(F32)

        span = pl.ds(s * LEN, LEN)
        outs.append(pltpu.make_async_copy(y.at[span], y_o.at[span], out_sems.at[s]))
        outs[-1].start()
    for copy in outs:
        copy.wait()


def nothing(t):
    return None


def store_gate(turned, big, dest, extra, before=nothing, after=nothing):
    for t in range(4):
        g = dot_nn(turned[t * 192 : (t + 1) * 192], big[...])
        before(t)
        for k in range(4):
            zx = t * 4 + k
            for lr in range(2):
                half = slice(lr * 48, lr * 48 + 48)
                part = g[k * 48 : k * 48 + 48, lr * D : (lr + 1) * D]
                if extra is not None:
                    part = part + extra[zx, half].astype(F32)
                dest[zx, half] = part.astype(BF16)
        after(t)


def store_out(small, big, dest, extra, before=nothing, after=nothing):
    for t in range(4):
        g = dot_tn(big[:, t * 384 : (t + 1) * 384], small[...])
        before(t)
        for k in range(4):
            part = g[k * 96 : (k + 1) * 96]
            if extra is not None:
                part = part + extra[t * 4 + k].astype(F32)
            dest[t * 4 + k] = part.astype(BF16)
        after(t)


def quarter(t):
    return pl.ds(t * 4, 4)


def kernel_b(
    ready, flush, pos, hidden, turned, y_i, tokens_i, cot_i, params,
    b0, b1, b2, b3, q0, q1, q2, q3,
    out_o, d_y_o, grads_o, d_hid_o, normed_o, d_gate_o, gain_grad,
    y, tokens, cot, out, d_y, grads, d_hid,
    weights, gate_in, d_normed, normed, d_gate, gate_inv, acc, sems, io_sems,
):
    core = pos[2]
    z0, x0 = pos[0], pos[1]
    copies = ([], [])
    for side, refs in enumerate(((b0, b1, b2, b3), (q0, q1, q2, q3))):
        half = core if side == 0 else 1 - core
        for r3 in range(4):
            for r2 in range(4):
                zx = source_zx(half, z0, x0, r3, r2)
                for lr in range(2):
                    row = jnp.where(half == 0, lr * D + zx * 48, DI + zx * 96 + lr * 48)
                    copies[side].append(
                        pltpu.make_async_copy(
                            refs[r3].at[pl.ds(r2 * 96 + lr * 48, 48)],
                            weights.at[pl.ds(pl.multiple_of(row, 16), 48)],
                            sems.at[side, r3, r2, lr],
                        )
                    )

    def each(side, act):
        @pl.when(core == side)
        def _():
            for copy in copies[0]:
                act(copy)

        @pl.when(core != side)
        def _():
            for copy in copies[1]:
                act(copy)

    get_y = pltpu.make_async_copy(y_i, y, io_sems.at[0])
    get_tokens = pltpu.make_async_copy(tokens_i, tokens, io_sems.at[1])
    get_cot = pltpu.make_async_copy(cot_i, cot, io_sems.at[2])
    put_out = pltpu.make_async_copy(out, out_o, io_sems.at[3])
    put_dy = pltpu.make_async_copy(d_y, d_y_o, io_sems.at[4])
    put_dhid = pltpu.make_async_copy(d_hid, d_hid_o, io_sems.at[5])
    each(0, lambda copy: copy.start())
    get_y.start()
    each(1, lambda copy: copy.start())
    get_tokens.start()
    get_cot.start()
    ready()
    gain = params[P_GATED : P_GATED + 1, :DI]
    each(0, lambda copy: copy.wait())

    @pl.loop(0, 3, unroll=3)
    def _(j):
        cols = pl.ds(pl.multiple_of(j * 256, 256), 256)
        right = pl.ds(pl.multiple_of(j * 256 + D, 256), 256)
        gate_in[:, cols] = dot_nn(hidden[...], weights[0:D, cols])
        gate_in[:, right] = dot_nn(hidden[...], weights[D:DI, cols])

    get_y.wait()

    @pl.loop(0, ROWS // 16, unroll=8)
    def _(i):
        rows = pl.ds(pl.multiple_of(i * 16, 16), 16)
        g = gate_in[rows]
        gated = y[rows] * (g * sigmoid(g))
        inv = lax.rsqrt(jnp.mean(gated * gated, axis=1, keepdims=True) + EPS)
        gate_inv[rows] = jnp.broadcast_to(inv, (16, 128))
        normed[rows] = (gated * inv * gain).astype(BF16)

    put_normed = pltpu.make_async_copy(normed, normed_o, io_sems.at[6])
    put_normed.start()
    each(1, lambda copy: copy.wait())
    get_tokens.wait()
    get_cot.wait()

    @pl.loop(0, 3, unroll=3)
    def _(j):
        cols = pl.ds(pl.multiple_of(j * 256, 256), 256)
        mixed = dot_nn(normed[...], weights[DI:, cols])
        out[:, cols] = (tokens[:, cols].astype(F32) + mixed).astype(BF16)

    put_out.start()

    @pl.loop(0, 6, unroll=3)
    def _(j):
        cols = pl.ds(pl.multiple_of(j * 256, 256), 256)
        d_normed[:, cols] = dot_nt(cot[...], weights[pl.ds(pl.multiple_of(j * 256 + DI, 256), 256)])

    acc[...] = jnp.zeros_like(acc)

    @pl.loop(0, ROWS // 16, unroll=8)
    def _(i):
        rows = pl.ds(pl.multiple_of(i * 16, 16), 16)
        g = gate_in[rows]
        sig = sigmoid(g)
        act = g * sig
        yv = y[rows]
        inv = gate_inv[rows][:, 0:1]
        gnorm = yv * act * inv
        dn = d_normed[rows]
        prod = dn * gnorm
        acc[...] += prod
        dgn = dn * gain
        mean = jnp.mean(dgn * gnorm, axis=1, keepdims=True)
        d_gated = inv * (dgn - gnorm * mean)
        d_y[rows] = d_gated * act
        d_gate[rows] = (d_gated * yv * (sig * (1.0 + g * (1.0 - sig)))).astype(BF16)

    put_dy.start()
    put_gate = pltpu.make_async_copy(d_gate, d_gate_o, io_sems.at[7])
    put_gate.start()
    gain_grad[...] = jnp.sum(acc[...], axis=0, keepdims=True)
    flush()

    def put_quarter(t):
        pltpu.make_async_copy(
            grads.at[quarter(t)], grads_o.at[quarter(t)], io_sems.at[8 + t]
        ).start()


    @pl.when(core == 0)
    def _():
        store_out(cot, normed, grads, None, after=put_quarter)

    @pl.when(core != 0)
    def _():
        store_gate(turned, d_gate, grads, None, after=put_quarter)

    put_grads = [
        pltpu.make_async_copy(grads.at[quarter(t)], grads_o.at[quarter(t)], io_sems.at[8 + t])
        for t in range(4)
    ]

    @pl.loop(0, 3, unroll=3)
    def _(j):
        cols = pl.ds(pl.multiple_of(j * 256, 256), 256)
        right = pl.ds(pl.multiple_of(j * 256 + D, 256), 256)
        d_hid[:, cols] = dot_nt(d_gate[:, :D], weights[cols]) + dot_nt(
            d_gate[:, D:], weights[right]
        )

    put_dhid.start()
    for copy in [put_out, put_dy, put_normed, put_gate, put_dhid] + put_grads:
        copy.wait()


def kernel_f(
    _, __, pos, turned_i, cot_i, d_gate, normed, got_i, total_o, turned, cot, big, got, total, sems
):
    core = pos[2]

    def more(t):
        return pltpu.make_async_copy(got_i.at[quarter(t)], got.at[quarter(t)], sems.at[2 + t])

    def put(t):
        return pltpu.make_async_copy(total.at[quarter(t)], total_o.at[quarter(t)], sems.at[6 + t])

    def run(small_i, small, big_i, store):
        gets = [
            pltpu.make_async_copy(small_i, small, sems.at[0]),
            pltpu.make_async_copy(big_i, big, sems.at[1]),
        ]
        for get in gets:
            get.start()
        for t in range(4):
            more(t).start()
        for get in gets:
            get.wait()
        store(small, big, total, got, lambda t: more(t).wait(), lambda t: put(t).start())

    @pl.when(core == 0)
    def _():
        run(turned_i, turned, d_gate, store_gate)

    @pl.when(core != 0)
    def _():
        run(cot_i, cot, normed, store_out)

    for t in range(4):
        put(t).wait()


def split_dot(v, pick):
    hi = v.astype(BF16)
    lo = (v - hi.astype(F32)).astype(BF16)
    return dot_nn(jnp.concatenate([hi, lo], axis=1), pick)


def kernel_c(
    ready, flush, pos, xs_i, bc, acum, bcum, dt_pre, d_y_i, y_i, params,
    conv_in_i, slope_i, wide_turned, _,
    grads_o, d_proj_o, g_conv_w, g_conv_b, g_skip, g_dt, g_alog,
    xs, d_y, y, d_act, score_t, acum_t, d_score, rsum, csum, in_sems,
    d_proj, slope, conv_in, grads, sems, out_sems, proj_sems,
):
    core = pos[2]
    later_gets = []
    for s in range(SEQS):
        later_gets.append(
            pltpu.make_async_copy(slope_i.at[pl.ds(s * LEN, LEN)], slope.at[s, 0:LEN], sems.at[s, 0])
        )
        later_gets.append(pltpu.make_async_copy(conv_in_i.at[s], conv_in.at[s], sems.at[s, 1]))
    gets = [
        [
            pltpu.make_async_copy(
                src.at[pl.ds(s * LEN, LEN)], dst.at[pl.ds(s * LEN, LEN)], in_sems.at[s, k]
            )
            for k, (src, dst) in enumerate(((xs_i, xs), (d_y_i, d_y), (y_i, y)))
        ]
        for s in range(SEQS)
    ]
    for copy in gets[0] + gets[1] + later_gets:
        copy.start()
    for s in range(SEQS):
        d_act[s, LEN:] = jnp.zeros((8, CONV_CH), F32)
        slope[s, LEN:] = jnp.zeros((8, CONV_CH), F32)
    d_proj[:, CONV_CH + 128 :] = jnp.zeros((ROWS, 128), BF16)
    above = iota((LEN, LEN), 0) <= iota((LEN, LEN), 1)
    upper = jnp.where(above, 1.0, 0.0)
    mask0, mask1 = head_masks()
    lane_head = iota((256, 128), 0) % 128 // 64
    head_col = iota((256, 128), 1)
    lane = iota((1, 128), 1)
    g_skip[...] = jnp.zeros_like(g_skip)
    g_dt[...] = jnp.zeros_like(g_dt)
    g_alog[...] = jnp.zeros_like(g_alog)
    ready()
    rate = params[P_RATE : P_RATE + 1, :128]
    for s in range(SEQS):
        rows = pl.ds(s * LEN, LEN)
        acum_t[...] = acum[rows].T
        score_t[...] = jnp.where(above, dot_nt(bc[rows, :DS], bc[rows, DS:]), 0.0)
        d_score[...] = jnp.zeros_like(d_score)
        rsum[...] = jnp.zeros_like(rsum)
        csum[...] = jnp.zeros_like(csum)
        b = bcum[rows]
        for copy in gets[s]:
            copy.wait()

        @pl.loop(0, NH // 2, unroll=12)
        def _(p):
            lanes = pl.ds(pl.multiple_of(p * 128, 128), 128)
            x = xs[rows, lanes]
            dy = d_y[rows, lanes]
            ds = dy.astype(BF16)
            turned = pltpu.roll(b, lax.rem(128 - 2 * p, 128), 1)
            top = jnp.zeros((128, 128), F32)
            low = jnp.zeros((128, 128), F32)
            grad0 = jnp.zeros((128, LEN), F32)
            grad1 = jnp.zeros((128, 128), F32)
            for i, mask in enumerate((mask0, mask1)):
                col = turned[:, i : i + 1]
                row = acum_t[pl.ds(2 * p + i, 1), :]
                dm = ds * mask
                xm = x * mask
                e0 = jnp.exp2(jnp.minimum(row - col[:128], 64.0))
                m0 = (e0 * score_t[:128, :]).astype(BF16)
                top = top + dot_nn(m0, dm)
                grad0 = grad0 + dot_nt(xm[:128], ds) * e0
                e1 = jnp.exp2(jnp.minimum(row[:, 128:] - col[128:], 64.0))
                m1 = (e1 * score_t[128:, 128:]).astype(BF16)
                low = low + dot_nn(m1, dm[128:])
                grad1 = grad1 + dot_nt(xm[128:], ds[128:]) * e1
            d_score[:128, :] += grad0
            d_score[128:, 128:] += grad1
            dxs = jnp.concatenate([top, low], axis=0)
            skip = params[P_SKIP : P_SKIP + 1, lanes]
            xf = x.astype(F32)
            own = ds.astype(F32) * (y[rows, lanes] - skip * xf)
            across = xf * dxs
            pick = jnp.where(lane_head + 2 * p == head_col, 1.0, 0.0).astype(BF16)
            rsum[...] += split_dot(own, pick)
            csum[...] += split_dot(across, pick)
            both = jnp.sum(dy * xf, axis=0, keepdims=True)
            first = jnp.sum(jnp.where(lane < 64, both, 0.0), axis=1, keepdims=True)
            second = jnp.sum(jnp.where(lane < 64, 0.0, both), axis=1, keepdims=True)
            g_skip[...] += jnp.where(lane == 2 * p, first, 0.0) + jnp.where(
                lane == 2 * p + 1, second, 0.0
            )
            d_act[s, 0:LEN, lanes] = skip * dy + dxs

        pre = dt_pre[rows]
        step = softplus(pre)
        sig = 1.0 / (1.0 + jnp.exp(-pre))
        ratio = jnp.where(pre < -20.0, 1.0, sig / jnp.maximum(step, 1e-30))
        d_cum = rsum[...] - csum[...]
        d_inc = dot_exact(upper, d_cum)
        g_alog[...] += jnp.sum(d_inc * step, axis=0, keepdims=True) * rate
        d_pre = csum[...] * ratio + d_inc * rate * sig
        g_dt[...] += jnp.sum(d_pre, axis=0, keepdims=True)
        d_proj[rows, CONV_CH : CONV_CH + 128] = d_pre.astype(BF16)
        dsc = jnp.where(above, d_score[...], 0.0).astype(BF16)
        d_act[s, 0:LEN, DI : DI + DS] = dot_nn(dsc, bc[rows, DS:])
        d_act[s, 0:LEN, DI + DS :] = dot_tn(dsc, bc[rows, :DS])

    for copy in later_gets:
        copy.wait()

    def put_tile(j):
        cols = pl.ds(pl.multiple_of(j * 256, 256), 256)
        return pltpu.make_async_copy(d_proj.at[:, cols], d_proj_o.at[:, cols], proj_sems.at[j])

    put_tile(7).start()

    @pl.loop(0, CONV_CH // 256)
    def _(j):
        cols = pl.ds(pl.multiple_of(j * 256, 256), 256)
        w = params[P_CONV : P_CONV + CONV, cols]
        zero = jnp.zeros((8, 256), F32)
        sums = (zero,) * (CONV + 1)
        for s in range(SEQS):

            def chunk(i, sums):
                base = pl.multiple_of(i * 32, 32)
                later = d_act[s, pl.ds(base, 40), cols] * slope[s, pl.ds(base, 40), cols]
                near = conv_in[s, pl.ds(base, 40), cols]
                here = later[0:32]
                back = w[CONV - 1 : CONV] * here
                for k in range(CONV - 1):
                    back = back + w[k : k + 1] * later[3 - k : 35 - k]
                d_proj[pl.ds(pl.multiple_of(s * LEN + base, 32), 32), cols] = back.astype(BF16)

                def fold(v):
                    return (v[0:8] + v[8:16]) + (v[16:24] + v[24:32])

                new = [sums[k] + fold(here * near[5 + k : 37 + k]) for k in range(CONV)]
                return tuple(new) + (sums[CONV] + fold(here),)

            sums = lax.fori_loop(0, LEN // 32, chunk, sums, unroll=8)
        for k in range(CONV):
            g_conv_w[k : k + 1, cols] = jnp.sum(sums[k], axis=0, keepdims=True)
        g_conv_b[:, cols] = jnp.sum(sums[CONV], axis=0, keepdims=True)
        put_tile(j).start()

    flush()

    def put_grads(j):
        cols = pl.ds(pl.multiple_of(j * 256, 256), 256)
        return pltpu.make_async_copy(grads.at[:, cols], grads_o.at[:, cols], out_sems.at[j])

    @pl.loop(0, 4, unroll=4)
    def _(j):
        cols = pl.ds(pl.multiple_of(j * 256, 256), 256)
        src = pl.ds(pl.multiple_of(j * 256 + (1 - core) * HALF1, 256), 256)
        grads[:, cols] = dot_nn(wide_turned[...], d_proj[:, src]).astype(BF16)
        put_grads(j).start()

    for j in range(8):
        put_tile(j).wait()
    for j in range(4):
        put_grads(j).wait()


def kernel_g(
    ready, _, pos, turned, d_proj_i, got, g_conv_w, g_conv_b, g_gated, g_norm,
    g_dt, g_alog, g_skip, out0, out1, out2, out3,
    total, d_proj, small, sem, out_sems,
):
    z0, x0, core = pos[0], pos[1], pos[2]
    src = pl.ds(pl.multiple_of(core * HALF1, HALF1), HALF1)
    get = pltpu.make_async_copy(d_proj_i.at[:, src], d_proj, sem)
    get.start()
    rest = CONV_CH - HALF1
    small[...] = jnp.zeros_like(small)
    ready()
    small[0:4] = g_conv_w[:, :HALF1]
    small[4:8, :rest] = g_conv_w[:, HALF1:]
    small[8:9] = g_conv_b[:, :HALF1]
    small[9:10, :rest] = g_conv_b[:, HALF1:]
    small[10:11] = g_gated[:, :HALF1]
    small[11:12, : DI - HALF1] = g_gated[:, HALF1:]
    small[12:13, :D] = g_norm[...]
    small[12:13, D : D + 128] = g_dt[...]
    small[12:13, D + 128 :] = g_alog[...]
    small[14:15, :128] = g_skip[...]
    for k in (12, 14):
        exact = small[k : k + 1]
        small[k + 1 : k + 2] = exact - exact.astype(BF16).astype(F32)
    sent = small[...].astype(BF16)
    for r3 in range(4):
        total[r3, 192:208] = sent
    get.wait()

    @pl.loop(0, 4, unroll=4)
    def _(j):
        cols = pl.ds(pl.multiple_of(j * 256, 256), 256)
        g = dot_nn(turned[...], d_proj[:, cols]) + got[:, cols].astype(F32)
        g = g.astype(BF16)
        for zx in range(16):
            dz = lax.rem(zx // 4 - z0 + 4, 4)
            dx = lax.rem(zx % 4 - x0 + 4, 4)
            r3 = jnp.where(core == 0, dz, dx)
            r2 = jnp.where(core == 0, dx, dz)
            rows = pl.ds(pl.multiple_of(r2 * 48, 16), 48)
            total[r3, rows, cols] = g[zx * 48 : zx * 48 + 48]

    puts = [
        pltpu.make_async_copy(total.at[r], out, out_sems.at[r])
        for r, out in enumerate((out0, out1, out2, out3))
    ]
    for put in puts:
        put.start()
    for put in puts:
        put.wait()


def sum_of_four(a, b, c, d):
    return (a[...].astype(F32) + c[...].astype(F32)) + (b[...].astype(F32) + d[...].astype(F32))


def kernel_k(ready, flush, own, got1, got2, got3, _, *outs):
    ready()
    total = sum_of_four(own, got1, got2, got3).astype(BF16)
    for r2, out in enumerate(outs):
        out[0:48] = total[r2 * 48 : r2 * 48 + 48]
        out[48:64] = total[192:208]
    flush()


def kernel_l(ready, flush, own, got1, got2, got3, two, out):
    ready()
    total = sum_of_four(own, got1, got2, got3)
    rides = jnp.concatenate([total[48:56], total[56:64]], axis=1).astype(BF16)
    zero = jnp.zeros((2, HALF1), F32)
    for d in range(8):
        eight = slice(d * 8, d * 8 + 8)
        out[eight, :DI] = two[eight]
        piece = jnp.concatenate([total[d * 6 : d * 6 + 6], zero], axis=0)
        out[eight, DI : DI + HALF1] = piece.astype(BF16)
        out[eight, DI + HALF1 :] = rides
    flush()


def kernel_d(
    ready, flush, d_proj_i, w1_i, d_hid_i, tokens_i, params, cot_i, grad_tokens_o, gain_grad,
    d_proj, w1, d_hid, tokens, cot, d_full, grad_tokens, sems, out_sems,
):
    gets = [
        pltpu.make_async_copy(src, dst, sems.at[k])
        for k, (src, dst) in enumerate(
            (
                (d_proj_i, d_proj),
                (w1_i.at[0:256], w1.at[0:256]),
                (w1_i.at[256:512], w1.at[256:512]),
                (w1_i.at[512:768], w1.at[512:768]),
                (d_hid_i, d_hid), (tokens_i, tokens), (cot_i, cot),
            )
        )
    ]
    for copy in gets:
        copy.start()
    gets[0].wait()
    for j in range(3):
        cols = slice(j * 256, (j + 1) * 256)
        gets[1 + j].wait()
        d_full[:, cols] = dot_nt(d_proj[...], w1[cols])

    for copy in gets[4:]:
        copy.wait()
    ready()
    gain = params[P_GAIN : P_GAIN + 1, :D]

    def chunk(i, total):
        rows = pl.ds(pl.multiple_of(i * 32, 32), 32)
        t = tokens[rows].astype(F32)
        inv = lax.rsqrt(jnp.mean(t * t, axis=1, keepdims=True) + EPS)
        normal = t * inv
        dh = d_full[rows] + d_hid[rows]
        prod = dh * normal
        dn = dh * gain
        mean = jnp.mean(dn * normal, axis=1, keepdims=True)
        grad_tokens[rows] = cot[rows].astype(F32) + inv * (dn - normal * mean)
        return total + (prod[0:8] + prod[8:16]) + (prod[16:24] + prod[24:32])

    total = jnp.zeros((8, D), F32)
    puts = []
    for s in range(4):
        total = lax.fori_loop(s * 4, s * 4 + 4, chunk, total, unroll=4)
        span = pl.ds(s * 128, 128)
        puts.append(
            pltpu.make_async_copy(grad_tokens.at[span], grad_tokens_o.at[span], out_sems.at[s])
        )
        puts[-1].start()
    gain_grad[...] = jnp.sum(total, axis=0, keepdims=True)
    flush()
    for put in puts:
        put.wait()


def kernel_h(
    ready, flush, got, g_in, g_out, g_norm, g_conv_w, g_conv_b, g_dt, g_alog, g_skip, g_gated, rows,
):
    def added(core, start, size):
        parts = [
            got[16 * y + 8 * core : 16 * y + 8 * core + 8, start : start + size].astype(F32)
            for y in range(4)
        ]
        return (parts[0] + parts[1]) + (parts[2] + parts[3])

    ready()
    rows[:, :DI] = added(0, 0, DI)
    rows[:, DI : DI + HALF1] = added(0, DI, HALF1)
    rows[:, DI + HALF1 :] = added(1, DI, HALF1)
    outs = added(1, 0, DI)
    for r in range(6):
        g_in[pl.ds(r * NCOL, NCOL)] = rows[r : r + 1, :NCOL].reshape(NCOL)
        g_out[pl.ds(r * DI, DI)] = outs[r : r + 1].reshape(DI)
    base = DI + HALF1
    top = added(0, base, HALF1) + added(1, base, HALF1)
    low = added(0, base + HALF1, HALF1) + added(1, base + HALF1, HALF1)
    rest = CONV_CH - HALF1
    g_conv_w[:, :HALF1] = top[0:4]
    g_conv_w[:, HALF1:] = top[4:8, :rest]
    g_conv_b[...] = jnp.concatenate([low[0:1], low[1:2, :rest]], axis=1).reshape(CONV_CH)
    g_gated[...] = jnp.concatenate([low[2:3], low[3:4, : DI - HALF1]], axis=1).reshape(DI)
    exact = low[4:5] + low[5:6]
    skip = low[6:7, :128] + low[7:8, :128]
    g_norm[...] = exact[:, :D].reshape(D)
    g_dt[...] = exact[0, D : D + NH]
    g_alog[...] = exact[0, D + 128 : D + 128 + NH]
    g_skip[...] = skip[0, :NH]
    flush()


VM = pl.BlockSpec(memory_space=pltpu.VMEM)
SM = pl.BlockSpec(memory_space=pltpu.SMEM)
HB = pl.BlockSpec(memory_space=pl.ANY)


def call(kernel, name, ins, outs, scratch, args, us=0.01):
    taken = [k for k, spec in enumerate(ins) if spec is VM]
    given = [k for k, out in enumerate(outs) if out[2] is VM]
    n_in, n_out, n_scratch = len(ins), len(outs), len(scratch)

    def body(*refs):
        in_refs = list(refs[:n_in])
        out_refs = list(refs[n_in : n_in + n_out])
        own = refs[n_in + n_out : n_in + n_out + n_scratch]
        rest = refs[n_in + n_out + n_scratch :]
        in_bufs, rest = rest[: len(taken)], rest[len(taken) :]
        out_bufs, rest = rest[: len(given)], rest[len(given) :]
        gets, puts = [], []
        for n, k in enumerate(taken):
            gets.append(pltpu.make_async_copy(in_refs[k], in_bufs[n], rest[0].at[n]))
            in_refs[k] = in_bufs[n]
        for n, k in enumerate(given):
            puts.append(pltpu.make_async_copy(out_bufs[n], out_refs[k], rest[1].at[n]))
            out_refs[k] = out_bufs[n]
        for copy in gets:
            copy.start()

        def ready():
            for copy in gets:
                copy.wait()

        def flush():
            for copy in puts:
                copy.start()

        kernel(ready, flush, *in_refs, *out_refs, *own)
        for copy in puts:
            copy.wait()

    dma = pltpu.SemaphoreType.DMA
    extra = [pltpu.VMEM(args[k].shape, args[k].dtype) for k in taken]
    extra += [pltpu.VMEM(outs[k][0], outs[k][1]) for k in given]
    extra += [dma((max(len(taken), 1),)), dma((max(len(given), 1),))]
    return pl.pallas_call(
        body,
        name=name,
        in_specs=[HB if spec is VM else spec for spec in ins],
        out_specs=[HB] * n_out,
        out_shape=[jax.ShapeDtypeStruct(o[0], o[1]) for o in outs],
        scratch_shapes=list(scratch) + extra,
        compiler_params=pltpu.CompilerParams(vmem_limit_bytes=LIMIT),
        cost_estimate=pl.CostEstimate(
            flops=int(us * 1.1e9), bytes_accessed=100_000, transcendentals=0
        ),
    )(*args)


def per_device(
    tokens,
    in_weight,
    out_weight,
    norm_gain,
    conv_weight,
    conv_bias,
    dt_bias,
    a_log,
    d_skip,
    gated_gain,
    cotangent,
):
    me = lax.axis_index("fsdp")
    core = lax.rem(me, 2)
    pos = jnp.stack([me // 32, lax.rem(me // 8, 4), core]).astype(jnp.int32)

    win = in_weight.reshape(6, NCOL)
    conv_cols = jnp.pad(win[:, DI:], ((0, 0), (0, WIDE1 - (NCOL - DI))))
    halves = jnp.stack(
        [
            jnp.concatenate([conv_cols[:, :HALF1], win[:, :DI]], axis=1),
            jnp.concatenate([conv_cols[:, HALF1:], out_weight.reshape(6, DI)], axis=1),
        ]
    )
    sent = jnp.broadcast_to(halves[None], (4, 2, 6, HALF1 + DI)).reshape(8, 6, HALF1 + DI)
    eight = lax.all_to_all(sent, "fsdp", 0, 0, axis_index_groups=EIGHTS)

    def row(v):
        return jnp.pad(v, (0, CONV_CH - v.shape[0]))[None]

    params = jnp.concatenate(
        [
            row(norm_gain), conv_weight, row(conv_bias), row(dt_bias), row(-jnp.exp(a_log)),
            row(jnp.repeat(d_skip, HEAD)), row(gated_gain),
            jnp.zeros((P_ROWS - P_GATED - 1, CONV_CH), F32),
        ],
        axis=0,
    )
    eight, params, pos = lax.optimization_barrier((eight, params, pos))
    near = ring_gather(eight.reshape(48, HALF1 + DI), False)
    own1 = ring_gather(jnp.concatenate([v[:, :HALF1] for v in near], axis=0), True)

    def second_part(v):
        as_gate = jnp.concatenate([v[:, HALF1 : HALF1 + D], v[:, HALF1 + D :]], axis=0)
        return jnp.where(core == 0, as_gate, v[:, HALF1:].reshape(96, D))

    near2 = jnp.concatenate([second_part(v) for v in near], axis=0)
    own1, near2 = lax.optimization_barrier((own1, near2))
    other1 = [swap_core(v) for v in own1]
    own2 = ring_gather(near2, True)
    dma = pltpu.SemaphoreType.DMA

    hidden, turned, w1, conv_in, slope, xs, bc, dt_pre, acum, bcum = call(
        kernel_a,
        "forward_conv",
        [SM] + [VM] * 2 + [HB] * 8,
        [
            ((ROWS, D), BF16, HB),
            ((D, ROWS), BF16, HB),
            ((D, WIDE1), BF16, HB),
            ((SEQS, PADLEN, CONV_CH), F32, HB),
            ((ROWS, CONV_CH), F32, HB),
            ((ROWS, DI), BF16, HB),
            ((ROWS, 2 * DS), BF16, VM),
            ((ROWS, 128), F32, VM),
            ((ROWS, 128), F32, VM),
            ((ROWS, 128), F32, VM),
        ],
        [
            pltpu.VMEM((ROWS, D), BF16),
            pltpu.VMEM((D, ROWS), BF16),
            pltpu.VMEM((D, WIDE1), BF16),
            pltpu.VMEM((SEQS, PADLEN, CONV_CH), F32),
            pltpu.VMEM((ROWS, CONV_CH), F32),
            pltpu.VMEM((ROWS, DI), BF16),
            dma((2, 4, 4)),
            dma((3,)),
            dma((7, 4)),
        ],
        [pos, tokens, params] + own1 + other1,
        14,
    )
    other2 = [swap_core(v) for v in own2]
    (y,) = call(
        kernel_s,
        "forward_ssd",
        [VM, HB, VM, VM, VM],
        [((ROWS, DI), F32, HB)],
        [
            pltpu.VMEM((ROWS, DI), BF16),
            pltpu.VMEM((ROWS, DI), F32),
            pltpu.VMEM((LEN, LEN), F32),
            pltpu.VMEM((128, LEN), F32),
            dma((2,)),
            dma((2,)),
        ],
        [params, xs, bc, acum, bcum],
        9,
    )

    out, d_y, grads2, d_hid, normed, d_gate, g_gated = call(
        kernel_b,
        "gate_output",
        [SM, VM, VM, HB, HB, HB, VM] + [HB] * 8,
        [
            ((ROWS, D), BF16, HB),
            ((ROWS, DI), F32, HB),
            ((16, 96, D), BF16, HB),
            ((ROWS, D), F32, HB),
            ((ROWS, DI), BF16, HB),
            ((ROWS, DI), BF16, HB),
            ((1, DI), F32, VM),
        ],
        [
            pltpu.VMEM((ROWS, DI), F32),
            pltpu.VMEM((ROWS, D), BF16),
            pltpu.VMEM((ROWS, D), BF16),
            pltpu.VMEM((ROWS, D), BF16),
            pltpu.VMEM((ROWS, DI), F32),
            pltpu.VMEM((16, 96, D), BF16),
            pltpu.VMEM((ROWS, D), F32),
            pltpu.VMEM((2 * DI, D), BF16),
            pltpu.VMEM((ROWS, DI), F32),
            pltpu.VMEM((ROWS, DI), F32),
            pltpu.VMEM((ROWS, DI), BF16),
            pltpu.VMEM((ROWS, DI), BF16),
            pltpu.VMEM((ROWS, 128), F32),
            pltpu.VMEM((16, DI), F32),
            dma((2, 4, 4, 2)),
            dma((12,)),
        ],
        [pos, hidden, turned, y, tokens, cotangent, params] + own2 + other2,
        18,
    )

    got2 = swap_core(grads2)

    (sum2,) = call(
        kernel_f,
        "grad_gate_out",
        [SM, HB, HB, HB, HB, HB],
        [((16, 96, D), BF16, HB)],
        [
            pltpu.VMEM((D, ROWS), BF16),
            pltpu.VMEM((ROWS, D), BF16),
            pltpu.VMEM((ROWS, DI), BF16),
            pltpu.VMEM((16, 96, D), BF16),
            pltpu.VMEM((16, 96, D), BF16),
            dma((10,)),
        ],
        [pos, turned, cotangent, d_gate, normed, got2],
    )
    before = sum2
    sum2 = lax.all_to_all(sum2, "fsdp", 0, 0, axis_index_groups=SIXTEENS)

    grads1, d_proj, g_conv_w, g_conv_b, g_skip, g_dt, g_alog = call(
        kernel_c,
        "backward_ssd_conv",
        [SM, HB, VM, VM, VM, VM, HB, HB, VM, HB, HB, VM, HB],
        [
            ((D, HALF1), BF16, HB),
            ((ROWS, WIDE1), BF16, HB),
            ((CONV, CONV_CH), F32, VM),
            ((1, CONV_CH), F32, VM),
            ((1, 128), F32, VM),
            ((1, 128), F32, VM),
            ((1, 128), F32, VM),
        ],
        [
            pltpu.VMEM((ROWS, DI), BF16),
            pltpu.VMEM((ROWS, DI), F32),
            pltpu.VMEM((ROWS, DI), F32),
            pltpu.VMEM((SEQS, PADLEN, CONV_CH), F32),
            pltpu.VMEM((LEN, LEN), F32),
            pltpu.VMEM((128, LEN), F32),
            pltpu.VMEM((LEN, LEN), F32),
            pltpu.VMEM((LEN, 128), F32),
            pltpu.VMEM((LEN, 128), F32),
            dma((2, 3)),
            pltpu.VMEM((ROWS, WIDE1), BF16),
            pltpu.VMEM((SEQS, PADLEN, CONV_CH), F32),
            pltpu.VMEM((SEQS, PADLEN, CONV_CH), F32),
            pltpu.VMEM((D, HALF1), BF16),
            dma((2, 2)),
            dma((4,)),
            dma((8,)),
        ],
        [pos, xs, bc, acum, bcum, dt_pre, d_y, y, params, conv_in, slope, turned, before],
    )

    got1 = swap_core(grads1)
    grad_tokens, g_norm = call(
        kernel_d,
        "grad_tokens",
        [HB, HB, HB, HB, VM, HB],
        [((ROWS, D), F32, HB), ((1, D), F32, VM)],
        [
            pltpu.VMEM((ROWS, WIDE1), BF16),
            pltpu.VMEM((D, WIDE1), BF16),
            pltpu.VMEM((ROWS, D), F32),
            pltpu.VMEM((ROWS, D), BF16),
            pltpu.VMEM((ROWS, D), BF16),
            pltpu.VMEM((ROWS, D), F32),
            pltpu.VMEM((ROWS, D), F32),
            dma((7,)),
            dma((4,)),
        ],
        [d_proj, w1, d_hid, tokens, params, cotangent],
    )
    sum1 = call(
        kernel_g,
        "grad_conv_columns",
        [SM, VM, HB] + [VM] * 8,
        [((208, HALF1), BF16, HB)] * 4,
        [
            pltpu.VMEM((4, 208, HALF1), BF16),
            pltpu.VMEM((ROWS, HALF1), BF16),
            pltpu.VMEM((16, HALF1), F32),
            dma,
            dma((4,)),
        ],
        [pos, turned, d_proj, got1, g_conv_w, g_conv_b, g_gated, g_norm]
        + [g_dt, g_alog, g_skip],
    )

    def ring(blocks, last):
        return [blocks[0]] + [
            lax.ppermute(blocks[r], "fsdp", ring_pairs(r, last)) for r in (1, 2, 3)
        ]

    sum1 = call(
        kernel_k,
        "ring_sums",
        [VM] * 4 + [HB],
        [((64, HALF1), BF16, VM)] * 4,
        [],
        ring(sum1, True) + [sum2],
    )
    sum2 = jnp.sum(sum2.astype(F32), axis=0)
    as_gate = jnp.concatenate([sum2[:48], sum2[48:]], axis=1)
    sum2 = jnp.where(core == 0, as_gate, sum2.reshape(48, DI)).astype(BF16).reshape(8, 6, DI)
    sum2 = jnp.pad(sum2, ((0, 0), (0, 2), (0, 0))).reshape(64, DI)

    (both,) = call(
        kernel_l,
        "pieces_of_eight",
        [VM] * 5,
        [((64, DI + 3 * HALF1), BF16, VM)],
        [],
        ring(sum1, False) + [sum2],
    )
    both = lax.all_to_all(
        both.reshape(8, 8, DI + 3 * HALF1), "fsdp", 0, 0, axis_index_groups=EIGHTS
    ).reshape(64, DI + 3 * HALF1)
    return (out, grad_tokens) + tuple(
        call(
            kernel_h,
            "last_sums",
            [VM],
            [
                ((6 * NCOL,), F32, VM),
                ((6 * DI,), F32, VM),
                ((D,), F32, VM),
                ((CONV, CONV_CH), F32, VM),
                ((CONV_CH,), F32, VM),
                ((NH,), F32, VM),
                ((NH,), F32, VM),
                ((NH,), F32, VM),
                ((DI,), F32, VM),
            ],
            [pltpu.VMEM((8, DI + 2 * HALF1), F32)],
            [both],
        )
    )


def solution(mesh):
    rows = P("fsdp", None)
    flat = P("fsdp")
    same = P()
    return jax.shard_map(
        per_device,
        mesh=mesh,
        in_specs=(rows, flat, flat) + (same,) * 7 + (rows,),
        out_specs=(rows, rows, flat, flat) + (same,) * 7,
        check_vma=False,
    )
```

```python
import functools

import jax
import jax.numpy as jnp
from jax import lax
from jax.experimental import pallas as pl
from jax.experimental.pallas import tpu as pltpu
from jax.sharding import PartitionSpec as P

D = 768
NH = 24
DS = 128
HEAD = 64
CONV = 4
LEN = 256
DI = 1536
CONV_CH = 1792
NCOL = 3352
ROWS = 512
SEQS = 2
PADLEN = LEN + 8
HALF1 = 1024
WIDE1 = 2048
EPS = 1e-5
LOG2E = 1.4426950408889634
P_GAIN, P_CONV, P_BIAS, P_DT, P_RATE, P_SKIP, P_GATED, P_ROWS = 0, 1, 5, 6, 7, 8, 9, 16
LIMIT = 63 * 1024 * 1024
F32 = jnp.float32
BF16 = jnp.bfloat16
HIGHEST = lax.Precision.HIGHEST


def index_of(z, x, y, c):
    return ((z % 4 * 4 + x % 4) * 4 + y % 4) * 2 + c


def everyone():
    for z in range(4):
        for x in range(4):
            for y in range(4):
                for c in range(2):
                    yield z, x, y, c


def ring_pairs(shift, last):
    pairs = []
    for z, x, y, c in everyone():
        along_z = (c == 0) == last
        to = (z + shift, x, y, c) if along_z else (z, x + shift, y, c)
        pairs.append((index_of(z, x, y, c), index_of(*to)))
    return pairs


CORE_PAIRS = [(index_of(*p), index_of(*p[:3], 1 - p[3])) for p in everyone()]
SIXTEENS = [[k * 8 + j for k in range(16)] for j in range(8)]
EIGHTS = [[(z * 4 + x) * 8 + k for k in range(8)] for z in range(4) for x in range(4)]


def ring_gather(value, last):
    return [value] + [
        lax.ppermute(value, "fsdp", ring_pairs(shift, last)) for shift in (1, 2, 3)
    ]


def swap_core(value):
    return lax.ppermute(value, "fsdp", CORE_PAIRS)


def dot_nn(a, b):
    return jnp.dot(a, b, preferred_element_type=F32)


def dot_nt(a, b):
    return lax.dot_general(a, b, (((1,), (1,)), ((), ())), preferred_element_type=F32)


def dot_tn(a, b):
    return lax.dot_general(a, b, (((0,), (0,)), ((), ())), preferred_element_type=F32)


def dot_exact(a, b):
    return jnp.dot(a, b, preferred_element_type=F32, precision=HIGHEST)


def sigmoid(v):
    return 0.5 * jnp.tanh(0.5 * v) + 0.5


def softplus(v):
    e = jnp.exp(-jnp.abs(v))
    small = e * (1.0 - e * (0.5 - e * (1.0 / 3.0)))
    return jnp.maximum(v, 0.0) + jnp.where(e < 1e-3, small, jnp.log(1.0 + e))


def iota(shape, dim):
    return lax.broadcasted_iota(jnp.int32, shape, dim)


def source_zx(half, z0, x0, r3, r2):
    zr = jnp.where(half == 0, r3, r2)
    xr = jnp.where(half == 0, r2, r3)
    return lax.rem(z0 - zr + 4, 4) * 4 + lax.rem(x0 - xr + 4, 4)


def head_masks():
    lane = iota((1, 128), 1)
    first = jnp.where(lane < 64, 1.0, 0.0).astype(BF16)
    second = jnp.where(lane < 64, 0.0, 1.0).astype(BF16)
    return first, second


def kernel_a(
    ready, flush, pos, tokens, params,
    b0, b1, b2, b3, q0, q1, q2, q3,
    hidden_o, turned_o, w1_o, conv_in_o, slope_o, xs_o, bc, dt_pre, acum, bcum,
    hidden, turned, w1, conv_in, slope, xs, sems, out_sems, tile_sems,
):
    z0, x0, core = pos[0], pos[1], pos[2]
    copies = []
    for side, refs in enumerate(((b0, b1, b2, b3), (q0, q1, q2, q3))):
        half = core if side == 0 else 1 - core
        col = pl.multiple_of(half * HALF1, HALF1)
        for r3 in range(4):
            for r2 in range(4):
                row = pl.multiple_of(source_zx(half, z0, x0, r3, r2) * 48, 16)
                copies.append(
                    pltpu.make_async_copy(
                        refs[r3].at[pl.ds(r2 * 48, 48)],
                        w1.at[pl.ds(row, 48), pl.ds(col, HALF1)],
                        sems.at[side, r3, r2],
                    )
                )
    for copy in copies:
        copy.start()
    ready()
    gain = params[P_GAIN : P_GAIN + 1, :D]

    @pl.loop(0, ROWS // 64, unroll=4)
    def _(i):
        rows = pl.ds(pl.multiple_of(i * 64, 64), 64)
        t = tokens[rows].astype(F32)
        inv = lax.rsqrt(jnp.mean(t * t, axis=1, keepdims=True) + EPS)
        hidden[rows] = (t * inv * gain).astype(BF16)

    turned[...] = hidden[...].T
    for s in range(SEQS):
        conv_in[s, 0:8] = jnp.zeros((8, CONV_CH), F32)
    for copy in copies:
        copy.wait()
    outs = [
        pltpu.make_async_copy(hidden, hidden_o, out_sems.at[0]),
        pltpu.make_async_copy(w1, w1_o, out_sems.at[1]),
        pltpu.make_async_copy(turned, turned_o, out_sems.at[2]),
    ]
    for copy in outs:
        copy.start()

    def conv_tile(j, cols, emit):
        p = dot_nn(hidden[...], w1[:, cols])
        for s in range(SEQS):
            conv_in[s, 8:PADLEN, cols] = p[s * LEN : (s + 1) * LEN]
        w = params[P_CONV : P_CONV + CONV, cols]
        bias = params[P_BIAS : P_BIAS + 1, cols]
        for s in range(SEQS):

            @pl.loop(0, LEN // 32, unroll=8)
            def _(i):
                base = pl.multiple_of(i * 32, 32)
                near = conv_in[s, pl.ds(base, 40), cols]
                total = bias + w[0:1] * near[5:37]
                for k in range(1, CONV):
                    total = total + w[k : k + 1] * near[5 + k : 37 + k]
                sig = sigmoid(total)
                act = total * sig
                rows = pl.ds(pl.multiple_of(s * LEN + base, 32), 32)
                slope[rows, cols] = sig * (1.0 + total * (1.0 - sig))
                emit(rows, act.astype(BF16))

    def tile_puts(j, cols):
        puts = [
            pltpu.make_async_copy(conv_in.at[s, :, cols], conv_in_o.at[s, :, cols], tile_sems.at[j, s])
            for s in range(SEQS)
        ]
        return puts + [
            pltpu.make_async_copy(slope.at[:, cols], slope_o.at[:, cols], tile_sems.at[j, 2])
        ]

    def xs_put(j, cols):
        return pltpu.make_async_copy(xs.at[:, cols], xs_o.at[:, cols], tile_sems.at[j, 3])

    def emit_bc(rows, act):
        bc[rows] = act

    last = pl.ds(1536, 256)
    conv_tile(6, last, emit_bc)
    for put in tile_puts(6, last):
        put.start()

    pre = dot_nn(hidden[...], w1[:, CONV_CH : CONV_CH + 128]) + params[P_DT : P_DT + 1, :128]
    dt_pre[...] = pre
    step = softplus(pre)
    inc = step * params[P_RATE : P_RATE + 1, :128] * LOG2E
    log_step = jnp.log(jnp.maximum(step, 1e-37)) * LOG2E
    lower = jnp.where(iota((LEN, LEN), 0) >= iota((LEN, LEN), 1), 1.0, 0.0)
    for s in range(SEQS):
        rows = slice(s * LEN, (s + 1) * LEN)
        a = dot_exact(lower, inc[rows])
        acum[rows] = a
        bcum[rows] = a - log_step[rows]
    flush()

    @pl.loop(0, 6, unroll=2)
    def _(j):
        cols = pl.ds(pl.multiple_of(j * 256, 256), 256)

        def emit(rows, act):
            xs[rows, cols] = act

        conv_tile(j, cols, emit)
        for put in tile_puts(j, cols) + [xs_put(j, cols)]:
            put.start()

    @pl.loop(0, 6)
    def _(j):
        cols = pl.ds(pl.multiple_of(j * 256, 256), 256)
        for put in tile_puts(j, cols) + [xs_put(j, cols)]:
            put.wait()

    for put in tile_puts(6, last) + outs:
        put.wait()


def kernel_s(ready, flush, params, xs_i, bc, acum, bcum, y_o, xs, y, score, bcum_t, in_sems, out_sems):
    gets = [
        pltpu.make_async_copy(xs_i.at[pl.ds(s * LEN, LEN)], xs.at[pl.ds(s * LEN, LEN)], in_sems.at[s])
        for s in range(SEQS)
    ]
    for copy in gets:
        copy.start()
    below = iota((LEN, LEN), 0) >= iota((LEN, LEN), 1)
    mask0, mask1 = head_masks()
    outs = []
    ready()
    for s in range(SEQS):
        rows = slice(s * LEN, (s + 1) * LEN)
        a = acum[rows]
        bcum_t[...] = bcum[rows].T
        score[...] = jnp.where(below, dot_nt(bc[rows, DS:], bc[rows, :DS]), 0.0)
        gets[s].wait()

        @pl.loop(0, NH // 2, unroll=4)
        def _(p):
            lanes = pl.ds(pl.multiple_of(p * 128, 128), 128)
            x = xs[s * LEN : (s + 1) * LEN, lanes]
            turned = pltpu.roll(a, lax.rem(128 - 2 * p, 128), 1)
            top = jnp.zeros((128, 128), F32)
            low = jnp.zeros((128, 128), F32)
            for i, mask in enumerate((mask0, mask1)):
                col = turned[:, i : i + 1]
                row = bcum_t[pl.ds(2 * p + i, 1), :]
                xm = x * mask
                e0 = jnp.exp2(jnp.minimum(col[:128] - row[:, :128], 64.0))
                m0 = (e0 * score[:128, :128]).astype(BF16)
                top = top + dot_nn(m0, xm[:128])
                e1 = jnp.exp2(jnp.minimum(col[128:] - row, 64.0))
                m1 = (e1 * score[128:, :]).astype(BF16)
                low = low + dot_nn(m1, xm)
            skip = params[P_SKIP : P_SKIP + 1, lanes]
            y[s * LEN : s * LEN + 128, lanes] = top + skip * x[:128].astype(F32)
            y[s * LEN + 128 : (s + 1) * LEN, lanes] = low + skip * x[128:].astype(F32)

        span = pl.ds(s * LEN, LEN)
        outs.append(pltpu.make_async_copy(y.at[span], y_o.at[span], out_sems.at[s]))
        outs[-1].start()
    for copy in outs:
        copy.wait()


def nothing(t):
    return None


def store_gate(turned, big, dest, extra, before=nothing, after=nothing):
    @pl.loop(0, 4)
    def _(t):
        g = dot_nn(turned[pl.ds(pl.multiple_of(t * 192, 192), 192)], big[...])
        before(t)
        for k in range(4):
            zx = t * 4 + k
            for lr in range(2):
                half = slice(lr * 48, lr * 48 + 48)
                part = g[k * 48 : k * 48 + 48, lr * D : (lr + 1) * D]
                if extra is not None:
                    part = part + extra[zx, half].astype(F32)
                dest[zx, half] = part.astype(BF16)
        after(t)


def store_out(small, big, dest, extra, before=nothing, after=nothing):
    @pl.loop(0, 4)
    def _(t):
        g = dot_tn(big[:, pl.ds(pl.multiple_of(t * 384, 384), 384)], small[...])
        before(t)
        for k in range(4):
            part = g[k * 96 : (k + 1) * 96]
            if extra is not None:
                part = part + extra[t * 4 + k].astype(F32)
            dest[t * 4 + k] = part.astype(BF16)
        after(t)


def quarter(t):
    return pl.ds(t * 4, 4)


def kernel_b(
    ready, flush, pos, hidden, turned, y_i, tokens_i, cot_i, params,
    b0, b1, b2, b3, q0, q1, q2, q3,
    out_o, d_y_o, grads_o, d_hid_o, normed_o, d_gate_o, gain_grad,
    y, tokens, cot, out, d_y, grads, d_hid,
    weights, gate_in, d_normed, normed, d_gate, gate_inv, acc, sems, io_sems,
):
    core = pos[2]
    z0, x0 = pos[0], pos[1]
    copies = ([], [])
    for side, refs in enumerate(((b0, b1, b2, b3), (q0, q1, q2, q3))):
        half = core if side == 0 else 1 - core
        for r3 in range(4):
            for r2 in range(4):
                zx = source_zx(half, z0, x0, r3, r2)
                for lr in range(2):
                    row = jnp.where(half == 0, lr * D + zx * 48, DI + zx * 96 + lr * 48)
                    copies[side].append(
                        pltpu.make_async_copy(
                            refs[r3].at[pl.ds(r2 * 96 + lr * 48, 48)],
                            weights.at[pl.ds(pl.multiple_of(row, 16), 48)],
                            sems.at[side, r3, r2, lr],
                        )
                    )

    def each(side, act):
        @pl.when(core == side)
        def _():
            for copy in copies[0]:
                act(copy)

        @pl.when(core != side)
        def _():
            for copy in copies[1]:
                act(copy)

    get_y = pltpu.make_async_copy(y_i, y, io_sems.at[0])
    get_tokens = pltpu.make_async_copy(tokens_i, tokens, io_sems.at[1])
    get_cot = pltpu.make_async_copy(cot_i, cot, io_sems.at[2])
    put_out = pltpu.make_async_copy(out, out_o, io_sems.at[3])
    put_dy = pltpu.make_async_copy(d_y, d_y_o, io_sems.at[4])
    put_dhid = pltpu.make_async_copy(d_hid, d_hid_o, io_sems.at[5])
    each(0, lambda copy: copy.start())
    get_y.start()
    each(1, lambda copy: copy.start())
    get_tokens.start()
    get_cot.start()
    ready()
    gain = params[P_GATED : P_GATED + 1, :DI]
    each(0, lambda copy: copy.wait())

    @pl.loop(0, 3, unroll=3)
    def _(j):
        cols = pl.ds(pl.multiple_of(j * 256, 256), 256)
        right = pl.ds(pl.multiple_of(j * 256 + D, 256), 256)
        gate_in[:, cols] = dot_nn(hidden[...], weights[0:D, cols])
        gate_in[:, right] = dot_nn(hidden[...], weights[D:DI, cols])

    get_y.wait()

    @pl.loop(0, ROWS // 16, unroll=8)
    def _(i):
        rows = pl.ds(pl.multiple_of(i * 16, 16), 16)
        g = gate_in[rows]
        gated = y[rows] * (g * sigmoid(g))
        inv = lax.rsqrt(jnp.mean(gated * gated, axis=1, keepdims=True) + EPS)
        gate_inv[rows] = jnp.broadcast_to(inv, (16, 128))
        normed[rows] = (gated * inv * gain).astype(BF16)

    put_normed = pltpu.make_async_copy(normed, normed_o, io_sems.at[6])
    put_normed.start()
    each(1, lambda copy: copy.wait())
    get_tokens.wait()
    get_cot.wait()

    @pl.loop(0, 3, unroll=3)
    def _(j):
        cols = pl.ds(pl.multiple_of(j * 256, 256), 256)
        mixed = dot_nn(normed[...], weights[DI:, cols])
        out[:, cols] = (tokens[:, cols].astype(F32) + mixed).astype(BF16)

    put_out.start()

    @pl.loop(0, 6, unroll=3)
    def _(j):
        cols = pl.ds(pl.multiple_of(j * 256, 256), 256)
        d_normed[:, cols] = dot_nt(cot[...], weights[pl.ds(pl.multiple_of(j * 256 + DI, 256), 256)])

    acc[...] = jnp.zeros_like(acc)

    @pl.loop(0, ROWS // 16, unroll=8)
    def _(i):
        rows = pl.ds(pl.multiple_of(i * 16, 16), 16)
        g = gate_in[rows]
        sig = sigmoid(g)
        act = g * sig
        yv = y[rows]
        inv = gate_inv[rows][:, 0:1]
        gnorm = yv * act * inv
        dn = d_normed[rows]
        prod = dn * gnorm
        acc[...] += prod
        dgn = dn * gain
        mean = jnp.mean(dgn * gnorm, axis=1, keepdims=True)
        d_gated = inv * (dgn - gnorm * mean)
        d_y[rows] = d_gated * act
        d_gate[rows] = (d_gated * yv * (sig * (1.0 + g * (1.0 - sig)))).astype(BF16)

    put_dy.start()
    put_gate = pltpu.make_async_copy(d_gate, d_gate_o, io_sems.at[7])
    put_gate.start()
    gain_grad[...] = jnp.sum(acc[...], axis=0, keepdims=True)
    flush()

    def put_quarter(t):
        pltpu.make_async_copy(
            grads.at[quarter(t)], grads_o.at[quarter(t)], io_sems.at[8 + t]
        ).start()


    @pl.when(core == 0)
    def _():
        store_out(cot, normed, grads, None, after=put_quarter)

    @pl.when(core != 0)
    def _():
        store_gate(turned, d_gate, grads, None, after=put_quarter)

    put_grads = [
        pltpu.make_async_copy(grads.at[quarter(t)], grads_o.at[quarter(t)], io_sems.at[8 + t])
        for t in range(4)
    ]

    @pl.loop(0, 3, unroll=3)
    def _(j):
        cols = pl.ds(pl.multiple_of(j * 256, 256), 256)
        right = pl.ds(pl.multiple_of(j * 256 + D, 256), 256)
        d_hid[:, cols] = dot_nt(d_gate[:, :D], weights[cols]) + dot_nt(
            d_gate[:, D:], weights[right]
        )

    put_dhid.start()
    for copy in [put_out, put_dy, put_normed, put_gate, put_dhid] + put_grads:
        copy.wait()


def kernel_f(
    _, __, pos, turned_i, cot_i, d_gate, normed, got_i, total_o, turned, cot, big, got, total, sems
):
    core = pos[2]

    def more(t):
        return pltpu.make_async_copy(got_i.at[quarter(t)], got.at[quarter(t)], sems.at[2 + t])

    def put(t):
        return pltpu.make_async_copy(total.at[quarter(t)], total_o.at[quarter(t)], sems.at[6 + t])

    def run(small_i, small, big_i, store):
        gets = [
            pltpu.make_async_copy(small_i, small, sems.at[0]),
            pltpu.make_async_copy(big_i, big, sems.at[1]),
        ]
        for get in gets:
            get.start()
        for t in range(4):
            more(t).start()
        for get in gets:
            get.wait()
        store(small, big, total, got, lambda t: more(t).wait(), lambda t: put(t).start())

    @pl.when(core == 0)
    def _():
        run(turned_i, turned, d_gate, store_gate)

    @pl.when(core != 0)
    def _():
        run(cot_i, cot, normed, store_out)

    for t in range(4):
        put(t).wait()


def split_dot(v, pick):
    hi = v.astype(BF16)
    lo = (v - hi.astype(F32)).astype(BF16)
    return dot_nn(jnp.concatenate([hi, lo], axis=1), pick)


def kernel_c(
    ready, flush, pos, xs_i, bc, acum, bcum, dt_pre, d_y_i, y_i, params,
    conv_in_i, slope_i, wide_turned, _,
    grads_o, d_proj_o, g_conv_w, g_conv_b, g_skip, g_dt, g_alog,
    xs, d_y, y, d_act, score_t, acum_t, d_score, rsum, csum, in_sems,
    d_proj, slope, conv_in, grads, sems, out_sems, proj_sems,
):
    core = pos[2]
    later_gets = []
    for s in range(SEQS):
        later_gets.append(
            pltpu.make_async_copy(slope_i.at[pl.ds(s * LEN, LEN)], slope.at[s, 0:LEN], sems.at[s, 0])
        )
        later_gets.append(pltpu.make_async_copy(conv_in_i.at[s], conv_in.at[s], sems.at[s, 1]))
    gets = [
        [
            pltpu.make_async_copy(
                src.at[pl.ds(s * LEN, LEN)], dst.at[pl.ds(s * LEN, LEN)], in_sems.at[s, k]
            )
            for k, (src, dst) in enumerate(((xs_i, xs), (d_y_i, d_y), (y_i, y)))
        ]
        for s in range(SEQS)
    ]
    for copy in gets[0] + gets[1] + later_gets:
        copy.start()
    for s in range(SEQS):
        d_act[s, LEN:] = jnp.zeros((8, CONV_CH), F32)
        slope[s, LEN:] = jnp.zeros((8, CONV_CH), F32)
    d_proj[:, CONV_CH + 128 :] = jnp.zeros((ROWS, 128), BF16)
    above = iota((LEN, LEN), 0) <= iota((LEN, LEN), 1)
    upper = jnp.where(above, 1.0, 0.0)
    mask0, mask1 = head_masks()
    lane_head = iota((256, 128), 0) % 128 // 64
    head_col = iota((256, 128), 1)
    lane = iota((1, 128), 1)
    g_skip[...] = jnp.zeros_like(g_skip)
    g_dt[...] = jnp.zeros_like(g_dt)
    g_alog[...] = jnp.zeros_like(g_alog)
    ready()
    rate = params[P_RATE : P_RATE + 1, :128]
    for s in range(SEQS):
        rows = pl.ds(s * LEN, LEN)
        acum_t[...] = acum[rows].T
        score_t[...] = jnp.where(above, dot_nt(bc[rows, :DS], bc[rows, DS:]), 0.0)
        d_score[...] = jnp.zeros_like(d_score)
        rsum[...] = jnp.zeros_like(rsum)
        csum[...] = jnp.zeros_like(csum)
        b = bcum[rows]
        for copy in gets[s]:
            copy.wait()

        @pl.loop(0, NH // 2, unroll=4)
        def _(p):
            lanes = pl.ds(pl.multiple_of(p * 128, 128), 128)
            x = xs[rows, lanes]
            dy = d_y[rows, lanes]
            ds = dy.astype(BF16)
            turned = pltpu.roll(b, lax.rem(128 - 2 * p, 128), 1)
            top = jnp.zeros((128, 128), F32)
            low = jnp.zeros((128, 128), F32)
            grad0 = jnp.zeros((128, LEN), F32)
            grad1 = jnp.zeros((128, 128), F32)
            for i, mask in enumerate((mask0, mask1)):
                col = turned[:, i : i + 1]
                row = acum_t[pl.ds(2 * p + i, 1), :]
                dm = ds * mask
                xm = x * mask
                e0 = jnp.exp2(jnp.minimum(row - col[:128], 64.0))
                m0 = (e0 * score_t[:128, :]).astype(BF16)
                top = top + dot_nn(m0, dm)
                grad0 = grad0 + dot_nt(xm[:128], ds) * e0
                e1 = jnp.exp2(jnp.minimum(row[:, 128:] - col[128:], 64.0))
                m1 = (e1 * score_t[128:, 128:]).astype(BF16)
                low = low + dot_nn(m1, dm[128:])
                grad1 = grad1 + dot_nt(xm[128:], ds[128:]) * e1
            d_score[:128, :] += grad0
            d_score[128:, 128:] += grad1
            dxs = jnp.concatenate([top, low], axis=0)
            skip = params[P_SKIP : P_SKIP + 1, lanes]
            xf = x.astype(F32)
            own = ds.astype(F32) * (y[rows, lanes] - skip * xf)
            across = xf * dxs
            pick = jnp.where(lane_head + 2 * p == head_col, 1.0, 0.0).astype(BF16)
            rsum[...] += split_dot(own, pick)
            csum[...] += split_dot(across, pick)
            both = jnp.sum(dy * xf, axis=0, keepdims=True)
            first = jnp.sum(jnp.where(lane < 64, both, 0.0), axis=1, keepdims=True)
            second = jnp.sum(jnp.where(lane < 64, 0.0, both), axis=1, keepdims=True)
            g_skip[...] += jnp.where(lane == 2 * p, first, 0.0) + jnp.where(
                lane == 2 * p + 1, second, 0.0
            )
            d_act[s, 0:LEN, lanes] = skip * dy + dxs

        pre = dt_pre[rows]
        step = softplus(pre)
        sig = 1.0 / (1.0 + jnp.exp(-pre))
        ratio = jnp.where(pre < -20.0, 1.0, sig / jnp.maximum(step, 1e-30))
        d_cum = rsum[...] - csum[...]
        d_inc = dot_exact(upper, d_cum)
        g_alog[...] += jnp.sum(d_inc * step, axis=0, keepdims=True) * rate
        d_pre = csum[...] * ratio + d_inc * rate * sig
        g_dt[...] += jnp.sum(d_pre, axis=0, keepdims=True)
        d_proj[rows, CONV_CH : CONV_CH + 128] = d_pre.astype(BF16)
        dsc = jnp.where(above, d_score[...], 0.0).astype(BF16)
        d_act[s, 0:LEN, DI : DI + DS] = dot_nn(dsc, bc[rows, DS:])
        d_act[s, 0:LEN, DI + DS :] = dot_tn(dsc, bc[rows, :DS])

    for copy in later_gets:
        copy.wait()

    def put_tile(j):
        cols = pl.ds(pl.multiple_of(j * 256, 256), 256)
        return pltpu.make_async_copy(d_proj.at[:, cols], d_proj_o.at[:, cols], proj_sems.at[j])

    put_tile(7).start()

    @pl.loop(0, CONV_CH // 256)
    def _(j):
        cols = pl.ds(pl.multiple_of(j * 256, 256), 256)
        w = params[P_CONV : P_CONV + CONV, cols]
        zero = jnp.zeros((8, 256), F32)
        sums = (zero,) * (CONV + 1)
        for s in range(SEQS):

            def chunk(i, sums):
                base = pl.multiple_of(i * 32, 32)
                later = d_act[s, pl.ds(base, 40), cols] * slope[s, pl.ds(base, 40), cols]
                near = conv_in[s, pl.ds(base, 40), cols]
                here = later[0:32]
                back = w[CONV - 1 : CONV] * here
                for k in range(CONV - 1):
                    back = back + w[k : k + 1] * later[3 - k : 35 - k]
                d_proj[pl.ds(pl.multiple_of(s * LEN + base, 32), 32), cols] = back.astype(BF16)

                def fold(v):
                    return (v[0:8] + v[8:16]) + (v[16:24] + v[24:32])

                new = [sums[k] + fold(here * near[5 + k : 37 + k]) for k in range(CONV)]
                return tuple(new) + (sums[CONV] + fold(here),)

            sums = lax.fori_loop(0, LEN // 32, chunk, sums, unroll=8)
        for k in range(CONV):
            g_conv_w[k : k + 1, cols] = jnp.sum(sums[k], axis=0, keepdims=True)
        g_conv_b[:, cols] = jnp.sum(sums[CONV], axis=0, keepdims=True)
        put_tile(j).start()

    flush()

    def put_grads(j):
        cols = pl.ds(pl.multiple_of(j * 256, 256), 256)
        return pltpu.make_async_copy(grads.at[:, cols], grads_o.at[:, cols], out_sems.at[j])

    @pl.loop(0, 4, unroll=4)
    def _(j):
        cols = pl.ds(pl.multiple_of(j * 256, 256), 256)
        src = pl.ds(pl.multiple_of(j * 256 + (1 - core) * HALF1, 256), 256)
        grads[:, cols] = dot_nn(wide_turned[...], d_proj[:, src]).astype(BF16)
        put_grads(j).start()

    for j in range(8):
        put_tile(j).wait()
    for j in range(4):
        put_grads(j).wait()


def kernel_g(
    ready, _, pos, turned, d_proj_i, got, g_conv_w, g_conv_b, g_gated, g_norm,
    g_dt, g_alog, g_skip, out0, out1, out2, out3,
    total, d_proj, small, sem, out_sems,
):
    z0, x0, core = pos[0], pos[1], pos[2]
    src = pl.ds(pl.multiple_of(core * HALF1, HALF1), HALF1)
    get = pltpu.make_async_copy(d_proj_i.at[:, src], d_proj, sem)
    get.start()
    rest = CONV_CH - HALF1
    small[...] = jnp.zeros_like(small)
    ready()
    small[0:4] = g_conv_w[:, :HALF1]
    small[4:8, :rest] = g_conv_w[:, HALF1:]
    small[8:9] = g_conv_b[:, :HALF1]
    small[9:10, :rest] = g_conv_b[:, HALF1:]
    small[10:11] = g_gated[:, :HALF1]
    small[11:12, : DI - HALF1] = g_gated[:, HALF1:]
    small[12:13, :D] = g_norm[...]
    small[12:13, D : D + 128] = g_dt[...]
    small[12:13, D + 128 :] = g_alog[...]
    small[14:15, :128] = g_skip[...]
    for k in (12, 14):
        exact = small[k : k + 1]
        small[k + 1 : k + 2] = exact - exact.astype(BF16).astype(F32)
    sent = small[...].astype(BF16)
    for r3 in range(4):
        total[r3, 192:208] = sent
    get.wait()

    @pl.loop(0, 4, unroll=4)
    def _(j):
        cols = pl.ds(pl.multiple_of(j * 256, 256), 256)
        g = dot_nn(turned[...], d_proj[:, cols]) + got[:, cols].astype(F32)
        g = g.astype(BF16)
        for zx in range(16):
            dz = lax.rem(zx // 4 - z0 + 4, 4)
            dx = lax.rem(zx % 4 - x0 + 4, 4)
            r3 = jnp.where(core == 0, dz, dx)
            r2 = jnp.where(core == 0, dx, dz)
            rows = pl.ds(pl.multiple_of(r2 * 48, 16), 48)
            total[r3, rows, cols] = g[zx * 48 : zx * 48 + 48]

    puts = [
        pltpu.make_async_copy(total.at[r], out, out_sems.at[r])
        for r, out in enumerate((out0, out1, out2, out3))
    ]
    for put in puts:
        put.start()
    for put in puts:
        put.wait()


def sum_of_four(a, b, c, d):
    return (a[...].astype(F32) + c[...].astype(F32)) + (b[...].astype(F32) + d[...].astype(F32))


def kernel_k(ready, flush, own, got1, got2, got3, _, *outs):
    ready()
    total = sum_of_four(own, got1, got2, got3).astype(BF16)
    for r2, out in enumerate(outs):
        out[0:48] = total[r2 * 48 : r2 * 48 + 48]
        out[48:64] = total[192:208]
    flush()


def kernel_l(ready, flush, own, got1, got2, got3, two, out):
    ready()
    total = sum_of_four(own, got1, got2, got3)
    rides = jnp.concatenate([total[48:56], total[56:64]], axis=1).astype(BF16)
    zero = jnp.zeros((2, HALF1), F32)
    for d in range(8):
        eight = slice(d * 8, d * 8 + 8)
        out[eight, :DI] = two[eight]
        piece = jnp.concatenate([total[d * 6 : d * 6 + 6], zero], axis=0)
        out[eight, DI : DI + HALF1] = piece.astype(BF16)
        out[eight, DI + HALF1 :] = rides
    flush()


def kernel_d(
    ready, flush, d_proj_i, w1_i, d_hid_i, tokens_i, params, cot_i, grad_tokens_o, gain_grad,
    d_proj, w1, d_hid, tokens, cot, d_full, grad_tokens, sems, out_sems,
):
    gets = [
        pltpu.make_async_copy(src, dst, sems.at[k])
        for k, (src, dst) in enumerate(
            (
                (d_proj_i, d_proj),
                (w1_i.at[0:256], w1.at[0:256]),
                (w1_i.at[256:512], w1.at[256:512]),
                (w1_i.at[512:768], w1.at[512:768]),
                (d_hid_i, d_hid), (tokens_i, tokens), (cot_i, cot),
            )
        )
    ]
    for copy in gets:
        copy.start()
    gets[0].wait()
    for j in range(3):
        cols = slice(j * 256, (j + 1) * 256)
        gets[1 + j].wait()
        d_full[:, cols] = dot_nt(d_proj[...], w1[cols])

    for copy in gets[4:]:
        copy.wait()
    ready()
    gain = params[P_GAIN : P_GAIN + 1, :D]

    def chunk(i, total):
        rows = pl.ds(pl.multiple_of(i * 32, 32), 32)
        t = tokens[rows].astype(F32)
        inv = lax.rsqrt(jnp.mean(t * t, axis=1, keepdims=True) + EPS)
        normal = t * inv
        dh = d_full[rows] + d_hid[rows]
        prod = dh * normal
        dn = dh * gain
        mean = jnp.mean(dn * normal, axis=1, keepdims=True)
        grad_tokens[rows] = cot[rows].astype(F32) + inv * (dn - normal * mean)
        return total + (prod[0:8] + prod[8:16]) + (prod[16:24] + prod[24:32])

    total = jnp.zeros((8, D), F32)
    puts = []
    for s in range(4):
        total = lax.fori_loop(s * 4, s * 4 + 4, chunk, total, unroll=4)
        span = pl.ds(s * 128, 128)
        puts.append(
            pltpu.make_async_copy(grad_tokens.at[span], grad_tokens_o.at[span], out_sems.at[s])
        )
        puts[-1].start()
    gain_grad[...] = jnp.sum(total, axis=0, keepdims=True)
    flush()
    for put in puts:
        put.wait()


def kernel_h(
    ready, flush, got, g_in, g_out, g_norm, g_conv_w, g_conv_b, g_dt, g_alog, g_skip, g_gated, rows,
):
    def added(core, start, size):
        parts = [
            got[16 * y + 8 * core : 16 * y + 8 * core + 8, start : start + size].astype(F32)
            for y in range(4)
        ]
        return (parts[0] + parts[1]) + (parts[2] + parts[3])

    ready()
    rows[:, :DI] = added(0, 0, DI)
    rows[:, DI : DI + HALF1] = added(0, DI, HALF1)
    rows[:, DI + HALF1 :] = added(1, DI, HALF1)
    outs = added(1, 0, DI)
    for r in range(6):
        g_in[pl.ds(r * NCOL, NCOL)] = rows[r : r + 1, :NCOL].reshape(NCOL)
        g_out[pl.ds(r * DI, DI)] = outs[r : r + 1].reshape(DI)
    base = DI + HALF1
    top = added(0, base, HALF1) + added(1, base, HALF1)
    low = added(0, base + HALF1, HALF1) + added(1, base + HALF1, HALF1)
    rest = CONV_CH - HALF1
    g_conv_w[:, :HALF1] = top[0:4]
    g_conv_w[:, HALF1:] = top[4:8, :rest]
    g_conv_b[...] = jnp.concatenate([low[0:1], low[1:2, :rest]], axis=1).reshape(CONV_CH)
    g_gated[...] = jnp.concatenate([low[2:3], low[3:4, : DI - HALF1]], axis=1).reshape(DI)
    exact = low[4:5] + low[5:6]
    skip = low[6:7, :128] + low[7:8, :128]
    g_norm[...] = exact[:, :D].reshape(D)
    g_dt[...] = exact[0, D : D + NH]
    g_alog[...] = exact[0, D + 128 : D + 128 + NH]
    g_skip[...] = skip[0, :NH]
    flush()


VM = pl.BlockSpec(memory_space=pltpu.VMEM)
SM = pl.BlockSpec(memory_space=pltpu.SMEM)
HB = pl.BlockSpec(memory_space=pl.ANY)


def call(kernel, name, ins, outs, scratch, args, us=0.01):
    taken = [k for k, spec in enumerate(ins) if spec is VM]
    given = [k for k, out in enumerate(outs) if out[2] is VM]
    n_in, n_out, n_scratch = len(ins), len(outs), len(scratch)

    def body(*refs):
        in_refs = list(refs[:n_in])
        out_refs = list(refs[n_in : n_in + n_out])
        own = refs[n_in + n_out : n_in + n_out + n_scratch]
        rest = refs[n_in + n_out + n_scratch :]
        in_bufs, rest = rest[: len(taken)], rest[len(taken) :]
        out_bufs, rest = rest[: len(given)], rest[len(given) :]
        gets, puts = [], []
        for n, k in enumerate(taken):
            gets.append(pltpu.make_async_copy(in_refs[k], in_bufs[n], rest[0].at[n]))
            in_refs[k] = in_bufs[n]
        for n, k in enumerate(given):
            puts.append(pltpu.make_async_copy(out_bufs[n], out_refs[k], rest[1].at[n]))
            out_refs[k] = out_bufs[n]
        for copy in gets:
            copy.start()

        def ready():
            for copy in gets:
                copy.wait()

        def flush():
            for copy in puts:
                copy.start()

        kernel(ready, flush, *in_refs, *out_refs, *own)
        for copy in puts:
            copy.wait()

    dma = pltpu.SemaphoreType.DMA
    extra = [pltpu.VMEM(args[k].shape, args[k].dtype) for k in taken]
    extra += [pltpu.VMEM(outs[k][0], outs[k][1]) for k in given]
    extra += [dma((max(len(taken), 1),)), dma((max(len(given), 1),))]
    return pl.pallas_call(
        body,
        name=name,
        in_specs=[HB if spec is VM else spec for spec in ins],
        out_specs=[HB] * n_out,
        out_shape=[jax.ShapeDtypeStruct(o[0], o[1]) for o in outs],
        scratch_shapes=list(scratch) + extra,
        compiler_params=pltpu.CompilerParams(vmem_limit_bytes=LIMIT),
        cost_estimate=pl.CostEstimate(
            flops=int(us * 1.1e9), bytes_accessed=100_000, transcendentals=0
        ),
    )(*args)


def per_device(
    tokens,
    in_weight,
    out_weight,
    norm_gain,
    conv_weight,
    conv_bias,
    dt_bias,
    a_log,
    d_skip,
    gated_gain,
    cotangent,
):
    me = lax.axis_index("fsdp")
    core = lax.rem(me, 2)
    pos = jnp.stack([me // 32, lax.rem(me // 8, 4), core]).astype(jnp.int32)

    win = in_weight.reshape(6, NCOL)
    conv_cols = jnp.pad(win[:, DI:], ((0, 0), (0, WIDE1 - (NCOL - DI))))
    halves = jnp.stack(
        [
            jnp.concatenate([conv_cols[:, :HALF1], win[:, :DI]], axis=1),
            jnp.concatenate([conv_cols[:, HALF1:], out_weight.reshape(6, DI)], axis=1),
        ]
    )
    sent = jnp.broadcast_to(halves[None], (4, 2, 6, HALF1 + DI)).reshape(8, 6, HALF1 + DI)
    eight = lax.all_to_all(sent, "fsdp", 0, 0, axis_index_groups=EIGHTS)

    def row(v):
        return jnp.pad(v, (0, CONV_CH - v.shape[0]))[None]

    params = jnp.concatenate(
        [
            row(norm_gain), conv_weight, row(conv_bias), row(dt_bias), row(-jnp.exp(a_log)),
            row(jnp.repeat(d_skip, HEAD)), row(gated_gain),
            jnp.zeros((P_ROWS - P_GATED - 1, CONV_CH), F32),
        ],
        axis=0,
    )
    eight, params, pos = lax.optimization_barrier((eight, params, pos))
    near = ring_gather(eight.reshape(48, HALF1 + DI), False)
    own1 = ring_gather(jnp.concatenate([v[:, :HALF1] for v in near], axis=0), True)

    def second_part(v):
        as_gate = jnp.concatenate([v[:, HALF1 : HALF1 + D], v[:, HALF1 + D :]], axis=0)
        return jnp.where(core == 0, as_gate, v[:, HALF1:].reshape(96, D))

    near2 = jnp.concatenate([second_part(v) for v in near], axis=0)
    own1, near2 = lax.optimization_barrier((own1, near2))
    other1 = [swap_core(v) for v in own1]
    own2 = ring_gather(near2, True)
    dma = pltpu.SemaphoreType.DMA

    hidden, turned, w1, conv_in, slope, xs, bc, dt_pre, acum, bcum = call(
        kernel_a,
        "forward_conv",
        [SM] + [VM] * 2 + [HB] * 8,
        [
            ((ROWS, D), BF16, HB),
            ((D, ROWS), BF16, HB),
            ((D, WIDE1), BF16, HB),
            ((SEQS, PADLEN, CONV_CH), F32, HB),
            ((ROWS, CONV_CH), F32, HB),
            ((ROWS, DI), BF16, HB),
            ((ROWS, 2 * DS), BF16, VM),
            ((ROWS, 128), F32, VM),
            ((ROWS, 128), F32, VM),
            ((ROWS, 128), F32, VM),
        ],
        [
            pltpu.VMEM((ROWS, D), BF16),
            pltpu.VMEM((D, ROWS), BF16),
            pltpu.VMEM((D, WIDE1), BF16),
            pltpu.VMEM((SEQS, PADLEN, CONV_CH), F32),
            pltpu.VMEM((ROWS, CONV_CH), F32),
            pltpu.VMEM((ROWS, DI), BF16),
            dma((2, 4, 4)),
            dma((3,)),
            dma((7, 4)),
        ],
        [pos, tokens, params] + own1 + other1,
        14,
    )
    other2 = [swap_core(v) for v in own2]
    (y,) = call(
        kernel_s,
        "forward_ssd",
        [VM, HB, VM, VM, VM],
        [((ROWS, DI), F32, HB)],
        [
            pltpu.VMEM((ROWS, DI), BF16),
            pltpu.VMEM((ROWS, DI), F32),
            pltpu.VMEM((LEN, LEN), F32),
            pltpu.VMEM((128, LEN), F32),
            dma((2,)),
            dma((2,)),
        ],
        [params, xs, bc, acum, bcum],
        9,
    )

    out, d_y, grads2, d_hid, normed, d_gate, g_gated = call(
        kernel_b,
        "gate_output",
        [SM, VM, VM, HB, HB, HB, VM] + [HB] * 8,
        [
            ((ROWS, D), BF16, HB),
            ((ROWS, DI), F32, HB),
            ((16, 96, D), BF16, HB),
            ((ROWS, D), F32, HB),
            ((ROWS, DI), BF16, HB),
            ((ROWS, DI), BF16, HB),
            ((1, DI), F32, VM),
        ],
        [
            pltpu.VMEM((ROWS, DI), F32),
            pltpu.VMEM((ROWS, D), BF16),
            pltpu.VMEM((ROWS, D), BF16),
            pltpu.VMEM((ROWS, D), BF16),
            pltpu.VMEM((ROWS, DI), F32),
            pltpu.VMEM((16, 96, D), BF16),
            pltpu.VMEM((ROWS, D), F32),
            pltpu.VMEM((2 * DI, D), BF16),
            pltpu.VMEM((ROWS, DI), F32),
            pltpu.VMEM((ROWS, DI), F32),
            pltpu.VMEM((ROWS, DI), BF16),
            pltpu.VMEM((ROWS, DI), BF16),
            pltpu.VMEM((ROWS, 128), F32),
            pltpu.VMEM((16, DI), F32),
            dma((2, 4, 4, 2)),
            dma((12,)),
        ],
        [pos, hidden, turned, y, tokens, cotangent, params] + own2 + other2,
        18,
    )

    got2 = swap_core(grads2)

    (sum2,) = call(
        kernel_f,
        "grad_gate_out",
        [SM, HB, HB, HB, HB, HB],
        [((16, 96, D), BF16, HB)],
        [
            pltpu.VMEM((D, ROWS), BF16),
            pltpu.VMEM((ROWS, D), BF16),
            pltpu.VMEM((ROWS, DI), BF16),
            pltpu.VMEM((16, 96, D), BF16),
            pltpu.VMEM((16, 96, D), BF16),
            dma((10,)),
        ],
        [pos, turned, cotangent, d_gate, normed, got2],
    )
    before = sum2
    sum2 = lax.all_to_all(sum2, "fsdp", 0, 0, axis_index_groups=SIXTEENS)

    grads1, d_proj, g_conv_w, g_conv_b, g_skip, g_dt, g_alog = call(
        kernel_c,
        "backward_ssd_conv",
        [SM, HB, VM, VM, VM, VM, HB, HB, VM, HB, HB, VM, HB],
        [
            ((D, HALF1), BF16, HB),
            ((ROWS, WIDE1), BF16, HB),
            ((CONV, CONV_CH), F32, VM),
            ((1, CONV_CH), F32, VM),
            ((1, 128), F32, VM),
            ((1, 128), F32, VM),
            ((1, 128), F32, VM),
        ],
        [
            pltpu.VMEM((ROWS, DI), BF16),
            pltpu.VMEM((ROWS, DI), F32),
            pltpu.VMEM((ROWS, DI), F32),
            pltpu.VMEM((SEQS, PADLEN, CONV_CH), F32),
            pltpu.VMEM((LEN, LEN), F32),
            pltpu.VMEM((128, LEN), F32),
            pltpu.VMEM((LEN, LEN), F32),
            pltpu.VMEM((LEN, 128), F32),
            pltpu.VMEM((LEN, 128), F32),
            dma((2, 3)),
            pltpu.VMEM((ROWS, WIDE1), BF16),
            pltpu.VMEM((SEQS, PADLEN, CONV_CH), F32),
            pltpu.VMEM((SEQS, PADLEN, CONV_CH), F32),
            pltpu.VMEM((D, HALF1), BF16),
            dma((2, 2)),
            dma((4,)),
            dma((8,)),
        ],
        [pos, xs, bc, acum, bcum, dt_pre, d_y, y, params, conv_in, slope, turned, before],
    )

    got1 = swap_core(grads1)
    grad_tokens, g_norm = call(
        kernel_d,
        "grad_tokens",
        [HB, HB, HB, HB, VM, HB],
        [((ROWS, D), F32, HB), ((1, D), F32, VM)],
        [
            pltpu.VMEM((ROWS, WIDE1), BF16),
            pltpu.VMEM((D, WIDE1), BF16),
            pltpu.VMEM((ROWS, D), F32),
            pltpu.VMEM((ROWS, D), BF16),
            pltpu.VMEM((ROWS, D), BF16),
            pltpu.VMEM((ROWS, D), F32),
            pltpu.VMEM((ROWS, D), F32),
            dma((7,)),
            dma((4,)),
        ],
        [d_proj, w1, d_hid, tokens, params, cotangent],
    )
    sum1 = call(
        kernel_g,
        "grad_conv_columns",
        [SM, VM, HB] + [VM] * 8,
        [((208, HALF1), BF16, HB)] * 4,
        [
            pltpu.VMEM((4, 208, HALF1), BF16),
            pltpu.VMEM((ROWS, HALF1), BF16),
            pltpu.VMEM((16, HALF1), F32),
            dma,
            dma((4,)),
        ],
        [pos, turned, d_proj, got1, g_conv_w, g_conv_b, g_gated, g_norm]
        + [g_dt, g_alog, g_skip],
    )

    def ring(blocks, last):
        return [blocks[0]] + [
            lax.ppermute(blocks[r], "fsdp", ring_pairs(r, last)) for r in (1, 2, 3)
        ]

    sum1 = call(
        kernel_k,
        "ring_sums",
        [VM] * 4 + [HB],
        [((64, HALF1), BF16, VM)] * 4,
        [],
        ring(sum1, True) + [sum2],
    )
    sum2 = jnp.sum(sum2.astype(F32), axis=0)
    as_gate = jnp.concatenate([sum2[:48], sum2[48:]], axis=1)
    sum2 = jnp.where(core == 0, as_gate, sum2.reshape(48, DI)).astype(BF16).reshape(8, 6, DI)
    sum2 = jnp.pad(sum2, ((0, 0), (0, 2), (0, 0))).reshape(64, DI)

    (both,) = call(
        kernel_l,
        "pieces_of_eight",
        [VM] * 5,
        [((64, DI + 3 * HALF1), BF16, VM)],
        [],
        ring(sum1, False) + [sum2],
    )
    both = lax.all_to_all(
        both.reshape(8, 8, DI + 3 * HALF1), "fsdp", 0, 0, axis_index_groups=EIGHTS
    ).reshape(64, DI + 3 * HALF1)
    return (out, grad_tokens) + tuple(
        call(
            kernel_h,
            "last_sums",
            [VM],
            [
                ((6 * NCOL,), F32, VM),
                ((6 * DI,), F32, VM),
                ((D,), F32, VM),
                ((CONV, CONV_CH), F32, VM),
                ((CONV_CH,), F32, VM),
                ((NH,), F32, VM),
                ((NH,), F32, VM),
                ((NH,), F32, VM),
                ((DI,), F32, VM),
            ],
            [pltpu.VMEM((8, DI + 2 * HALF1), F32)],
            [both],
        )
    )


def solution(mesh):
    rows = P("fsdp", None)
    flat = P("fsdp")
    same = P()
    return jax.shard_map(
        per_device,
        mesh=mesh,
        in_specs=(rows, flat, flat) + (same,) * 7 + (rows,),
        out_specs=(rows, rows, flat, flat) + (same,) * 7,
        check_vma=False,
    )
```
